32 devices in a mesh: bx: 4 (over y, x), by: 4 (over z), gz: 2 (over core).
Axes of the slice: x: 2, y: 2, z: 4, core: 2. Of those that a mesh axis runs over, the one named last changes fastest.
Arguments:
- electric_start: float32 [3, 64, 64, 256], P(None, 'by', 'bx', 'gz'), may hold values from -6 to 6
- magnetic_start: float32 [3, 64, 64, 256], P(None, 'by', 'bx', 'gz'), may hold values from -6 to 6
- current_start: float32 [3, 64, 64, 256], P(None, 'by', 'bx', 'gz'), may hold values from -6 to 6
- cotangent: float32 [3, 64, 64, 256], P(None, 'by', 'bx', 'gz'), may hold values from -6 to 6
- level_set: float32 [64, 64, 256], P('by', 'bx', 'gz'), may hold values from -8 to 8
- material: int32 [64, 64, 256], P('by', 'bx', 'gz'), may hold values from 0 to 2
- source_cell: int32 [256], P(('bx', 'by', 'gz')), may hold values from 0 to 32767
- basis: bfloat16 [8192, 64, 256], P(('bx', 'by', 'gz')), may hold values from 0 to 1
- block_owner: int32 [8192, 1], P(('bx', 'by', 'gz')), may hold values from 0 to 15; in each aligned block of 256 rows (0 to 255, 256 to 511, ...) at most 32 rows name the same one
- block_group: int32 [8192], P(('bx', 'by', 'gz')), may hold values from 0 to 127
Outputs:
- final_electric: float32 [3, 64, 64, 256], P(None, 'by', 'bx', 'gz')
- adjoint_electric: float32 [3, 64, 64, 256], P(None, 'by', 'bx', 'gz')
- coef_grad: float32 [64, 4096], P(None, ('bx', 'by', 'gz'))
The draws below stay inside these ranges and needn't reach their ends.
Inputs may be any that keep to these rules, and one draw needn't show every extreme that they name: `material`: 0 is vacuum, 1 design dielectric, 2 silver. `source_cell`: a flat cell index within the device's own brick; a cell may be named more than once. `block_owner`: among the 256 blocks of one device no owner is named by more than 32 blocks, and in some device one owner is named by exactly 32.
All inputs are finite; a program needn't handle non-finite values.
Results may differ from the reference program's by a relative error of at most 0.0029.
Values sent between devices are 32-bit elements; how exact they have to be, the bound alone decides.
No kernel may reach another device: no remote copies, remote signals or barrier semaphores. Data moves between devices by JAX's collectives and lax.ppermute only.
A program may use at most 64 MiB of HBM per device.

```python
import math
import jax
import jax.numpy as jnp
import numpy as np
from jax import lax

CY = 16
CX = 16
CZ = 128
NSTEP = 2
KB = 64
TILE = 256
FAN = 2
GRP_DEV = 128
SRC_DEV = 8
NX = 64
NY = 64
NZ = 256
CELLS = 32768
TILES = 128
NB = 256
PLANES = 16
CAP = 32
GROUPS = 4096
N_BX = 4
N_BY = 4
N_GZ = 2


def place_ends(array, own_key, low, high):
    extent = array.shape
    spot = [jax.random.randint(jax.random.fold_in(own_key, axis), (), 0, extent[axis]) for axis in range(len(extent))]
    array = array.at[tuple(spot)].set(low)
    longest = extent.index(max(extent))
    spot[longest] = (spot[longest] + 1) % extent[longest]
    return array.at[tuple(spot)].set(high)


def level_of(rng, shape, shards, low, largest):
    level, own = 1.0, jax.random.fold_in(rng, 6)
    for position, blocks in shards:
        steps = jnp.exp(jax.random.uniform(jax.random.fold_in(own, position), (blocks,), jnp.float32, low / len(shards), largest / len(shards)))
        level = level * jnp.repeat(steps, shape[position] // blocks).reshape([-1 if axis == position else 1 for axis in range(len(shape))])
    return level


def deal_out(key, own, number, rows, count, top, limit, skew):
    sequence = jax.random.permutation(key, count)
    packed, ordinary = shares(count, rows * top, limit, skew, True), shares(count, rows * top, limit, skew, False)
    places = jnp.arange(count)

    def named(lengths, offset_by):
        used = int((lengths > 0).sum())
        fixed = max(1, used // 4)
        passed = fixed + (places - fixed + offset_by * (used - fixed)) % max(1, count - fixed)
        return jnp.zeros((count,), jnp.int32).at[sequence[jnp.where(places < fixed, places, passed)]].set(jnp.asarray(lengths, jnp.int32))

    lengths = jnp.where(number % 4 == 0, named(packed, number // 4), named(ordinary, number - number // 4 - 1))
    mixed = jax.random.permutation(jax.random.fold_in(own, 3), count)
    source_of, receiver = mixed[0:count // 2 * 2:2], mixed[1:count // 2 * 2:2]
    room = jnp.minimum(lengths[source_of] - 1, limit - lengths[receiver]) // 2
    room = jnp.where((source_of == sequence[0]) | (receiver == sequence[0]) | (lengths[receiver] == 0), 0, jnp.maximum(room, 0))
    passed = jax.random.randint(jax.random.fold_in(own, 4), (count // 2,), 0, 1 << 20) % (room + 1)
    lengths = lengths.at[source_of].add(-passed).at[receiver].add(passed)
    members = jnp.searchsorted(jnp.cumsum(lengths), jnp.arange(rows * top), side="right").astype(jnp.int32)
    listing = members.reshape(top, rows).T
    listing = listing[jax.random.permutation(jax.random.fold_in(own, 1), rows)]
    offset_by = jax.random.randint(jax.random.fold_in(own, 2), (rows, 1), 0, top)
    return jnp.take_along_axis(listing, (jnp.arange(top)[None, :] + offset_by) % top, axis=1)


def shares(amount, total, most, slope, full):
    weights = [(1 << 20) // math.isqrt(standing ** slope) + 1 for standing in range(1, amount + 1)]
    largest = most if full else min(most, max(-(-total // amount), total * weights[0] // sum(weights)))
    least = 1 if total - largest >= amount - 1 else 0
    holding, spare = [largest] + [least] * (amount - 1), total - largest - least * (amount - 1)
    while spare > 0:
        movable = [i for i in range(1, amount) if holding[i] < largest] or [i for i in range(1, amount) if holding[i] < most]
        mass, remaining = sum([weights[i] for i in movable]), spare
        for i in movable:
            extra = min(most - holding[i], max(1, remaining * weights[i] // mass), spare)
            holding[i] = holding[i] + extra
            spare = spare - extra
    return np.array(holding)


def bell_draw(own_key, shape, scale, most, cuts=(), held_as=jnp.bfloat16):
    gain = level_of(own_key, shape, cuts, -0.22, 0.18) if cuts else 1.0
    result = jax.random.normal(own_key, shape, jnp.float32) * scale * gain
    return jnp.minimum(jnp.maximum(result, -most), most).astype(held_as)


def setup_inputs(seed: int = 0) -> dict:
    splits = jax.random.split(jax.random.key(seed), 11)
    electric_start = bell_draw(splits[0], (3, NY, NX, NZ), 1.0, 6.0, ((1, 4), (2, 4), (3, 2)), jnp.float32)
    magnetic_start = bell_draw(splits[1], (3, NY, NX, NZ), 1.0, 6.0, ((1, 4), (2, 4), (3, 2)), jnp.float32)
    current_start = bell_draw(splits[2], (3, NY, NX, NZ), 1.0, 6.0, ((1, 4), (2, 4), (3, 2)), jnp.float32)
    cotangent = bell_draw(splits[3], (3, NY, NX, NZ), 1.0, 6.0, ((1, 4), (2, 4), (3, 2)), jnp.float32)
    level_set = bell_draw(splits[4], (NY, NX, NZ), 2.0, 8.0, ((0, 4), (1, 4), (2, 2)), jnp.float32)
    material = place_ends(jax.random.randint(splits[5], (NY, NX, NZ), 0, 3), jax.random.fold_in(splits[5], 1), 0, 2).astype(jnp.int32)
    source_cell = place_ends(jax.random.randint(splits[6], (SRC_DEV * N_BX * N_BY * N_GZ,), 0, CELLS), jax.random.fold_in(splits[6], 1), 0, CELLS - 1).astype(jnp.int32)
    basis = jnp.clip(1.0 * jax.random.uniform(splits[7], (NB * N_BX * N_BY * N_GZ, KB, TILE), jnp.float32) ** level_of(splits[7], (NB * N_BX * N_BY * N_GZ, KB, TILE), ((0, 32),), -0.2, 0.2), 0.0, 1.0).astype(jnp.bfloat16)
    block_owner_keys = jax.random.split(jax.random.fold_in(splits[8], 1), (NB * N_BX * N_BY * N_GZ) // NB)
    block_owner_turns = jax.random.permutation(jax.random.fold_in(splits[8], 3), (NB * N_BX * N_BY * N_GZ) // NB)
    block_owner = jax.vmap(lambda own, number: deal_out(jax.random.fold_in(splits[8], 2), own, number, NB, PLANES, 1, CAP, 2))(block_owner_keys, block_owner_turns).reshape((NB * N_BX * N_BY * N_GZ, 1))
    block_group = place_ends(jax.random.randint(splits[9], (NB * N_BX * N_BY * N_GZ,), 0, GRP_DEV), jax.random.fold_in(splits[9], 1), 0, GRP_DEV - 1).astype(jnp.int32)
    return {"electric_start": electric_start, "magnetic_start": magnetic_start, "current_start": current_start, "cotangent": cotangent, "level_set": level_set, "material": material, "source_cell": source_cell, "basis": basis, "block_owner": block_owner, "block_group": block_group}


time_step = 0.5
drude_keep = 0.9
drude_gain = 1.0
metal_permit = 3.0
design_contrast = 5.0
source_level = 3.0
source_wave = (1.0, -0.6, 0.8, -0.4)

def beside(couple, axis_dim, offset):
    length = couple.shape[axis_dim]
    border = jnp.zeros_like(lax.slice_in_dim(couple, 0, 1, axis=axis_dim))
    if offset < 0:
        return jnp.concatenate([lax.slice_in_dim(couple, 1, length, axis=axis_dim), border], axis=axis_dim)
    return jnp.concatenate([border, lax.slice_in_dim(couple, 0, length - 1, axis=axis_dim)], axis=axis_dim)

def differ(couple, axis_dim, offset):
    neighbour = beside(couple, axis_dim, offset)
    if offset < 0:
        return neighbour - couple
    return couple - neighbour

def curl(fields, offset):
    along_x = differ(jnp.stack([fields[1], fields[2]]), 2, offset)
    along_y = differ(jnp.stack([fields[0], fields[2]]), 1, offset)
    along_z = differ(jnp.stack([fields[0], fields[1]]), 3, offset)
    return jnp.stack([along_y[1] - along_z[1], along_z[0] - along_x[1], along_x[0] - along_y[0]])

def permittivity(material, level_set):
    smooth = jax.nn.sigmoid(level_set)
    return jnp.where(material == 2, metal_permit, jnp.where(material == 1, 1.0 + design_contrast * smooth, 1.0))

def forward(electric, magnetic, current, permit, silver, sources):
    for moment in range(NSTEP):
        magnetic = magnetic - time_step * curl(electric, -1)
        current = silver * (drude_keep * current + drude_gain * electric)
        drive_term = curl(magnetic, 1) - current
        electric = electric + time_step / permit * drive_term
        electric = electric.at[2].add(source_level * source_wave[moment] * sources)
    return electric

def reference(electric_start, magnetic_start, current_start, cotangent, level_set, material, source_cell, basis, block_owner, block_group):
    silver = (material == 2).astype(jnp.float32)
    devices = N_BX * N_BY * N_GZ
    src_rows = jnp.arange(SRC_DEV * devices, dtype=jnp.int32)
    src_dev = src_rows // SRC_DEV
    dev_bx = src_dev // (N_BY * N_GZ)
    dev_by = src_dev // N_GZ % N_BY
    dev_gz = src_dev % N_GZ
    local_y = source_cell // (CX * CZ)
    local_x = source_cell // CZ % CX
    local_z = source_cell % CZ
    sources = jnp.zeros((NY, NX, NZ), jnp.float32).at[dev_by * CY + local_y, dev_bx * CX + local_x, dev_gz * CZ + local_z].add(1.0)

    def propagate(start_field, level_field):
        return forward(start_field, magnetic_start, current_start, permittivity(material, level_field), silver, sources)
    final_field, pullback = jax.vjp(propagate, electric_start, level_set)
    adjoint, level_grad = pullback(cotangent)
    cell_grad = level_grad.astype(jnp.bfloat16)
    bricks = cell_grad.reshape(N_BY, CY, N_BX, CX, N_GZ, CZ).transpose(2, 0, 4, 1, 3, 5).reshape(devices, TILES, TILE)
    blocks = basis.reshape(devices, TILES, FAN, KB, TILE)

    def project(couple):
        return jnp.einsum('tfkc,tc->tfk', couple[0].astype(jnp.float32), couple[1].astype(jnp.float32))
    partials = lax.map(project, (blocks, bricks)).reshape(devices * NB, KB)
    block_rows = jnp.arange(devices * NB, dtype=jnp.int32)
    plane_gz = block_rows // NB % N_GZ
    group_index = (block_owner[:, 0] * N_GZ + plane_gz) * GRP_DEV + block_group
    coef_sum = jax.ops.segment_sum(partials, group_index, num_segments=GROUPS)
    return (final_field, adjoint, coef_sum.T)
```

```python
import functools

import jax
import jax.numpy as jnp
from jax import lax
from jax.experimental import pallas as pl
from jax.experimental.pallas import tpu as pltpu
from jax.sharding import PartitionSpec as P

KB = 64
GRP_DEV = 128

time_step = 0.5
drude_keep = 0.9
drude_gain = 1.0
metal_permit = 3.0
design_contrast = 5.0
source_level = 3.0
source_wave = (1.0, -0.6, 0.8, -0.4)

PAIRS, SINGLES = 9, 4
UNITS = 2 * PAIRS + SINGLES
UNITS_PAD = 24
ARRAYS = PAIRS + SINGLES
F32 = jnp.float32
BF16 = jnp.bfloat16
LIMIT = 56 * 1024 * 1024


def is_even(axis):
    return lax.rem(lax.axis_index(axis), 2) == 0


def lanes(shape):
    return lax.broadcasted_iota(jnp.int32, shape, len(shape) - 1)


def prepare_kernel(cells_ref, e_ref, h_ref, j_ref, c_ref, level_ref, mat_ref,
                   fa_ref, fb_ref, b_ref, s_ref, r_ref, w_ref, j1_ref, q_ref):
    ny, nx, nz = mat_ref.shape
    flat = lax.broadcasted_iota(jnp.int32, (nx, nz), 0) * nz + lanes((nx, nz))

    def row(y, carry):
        mat = mat_ref[y]
        silver, design = mat == 2, mat == 1
        smooth = 1.0 / (1.0 + jnp.exp(-level_ref[y]))
        permit = jnp.where(silver, metal_permit, jnp.where(design, 1.0 + design_contrast * smooth, 1.0))
        ratio = time_step / permit
        r_ref[y] = jnp.where(silver, -ratio, ratio)
        w_ref[y] = jnp.where(design, (-design_contrast / time_step) * ratio * smooth * (1.0 - smooth), 0.0)
        count = jnp.zeros((nx, nz), F32)
        for i in range(cells_ref.shape[0]):
            count = count + jnp.where(flat + y * (nx * nz) == cells_ref[i], 1.0, 0.0)
        q_ref[y] = count
        for c in range(3):
            current = jnp.where(silver, drude_keep * j_ref[c, y] + drude_gain * e_ref[c, y], 0.0)
            j1_ref[c, y] = current
            start = e_ref[c, y] - ratio * current
            if c == 2:
                start = start + (source_level * source_wave[0]) * count
            b_ref[c, y] = start
            s_ref[c, y] = ratio * c_ref[c, y]
        return carry

    lax.fori_loop(0, ny, row, 0, unroll=2)

    def face(out, low, near):
        for k, ref in enumerate((e_ref, h_ref, s_ref)):
            for c in range(3):
                for d in range(2):
                    out[6 * k + 2 * c + d] = ref[c, low + d]
        for c in range(3):
            out[18 + c] = b_ref[c, near]
        out[21] = r_ref[near]

    even = is_even("by")

    @pl.when(even)
    def _():
        face(fa_ref, ny - 2, ny - 1)
        face(fb_ref, 0, 0)

    @pl.when(jnp.logical_not(even))
    def _():
        face(fb_ref, ny - 2, ny - 1)
        face(fa_ref, 0, 0)


def x_face_kernel(e_ref, h_ref, s_ref, b_ref, r_ref, ga_ref, gb_ref, xa_ref, xb_ref):
    ny, nx, nz = r_ref.shape
    y_even, x_even = is_even("by"), is_even("bx")

    def face(out, low, near):
        out[:, UNITS:, :] = jnp.zeros((ny + 4, UNITS_PAD - UNITS, nz), F32)
        for k, ref in enumerate((e_ref, h_ref, s_ref)):
            for c in range(3):
                u = 6 * k + 2 * c
                out[2:ny + 2, u:u + 2, :] = ref[c, :, low:low + 2, :]
                for d in range(2):
                    ga, gb = ga_ref[u + d], gb_ref[u + d]
                    out[d, u:u + 2, :] = jnp.where(y_even, gb, ga)[low:low + 2]
                    out[ny + 2 + d, u:u + 2, :] = jnp.where(y_even, ga, gb)[low:low + 2]
        zero = jnp.zeros((SINGLES, nz), F32)
        out[0, 18:UNITS, :] = zero
        out[ny + 3, 18:UNITS, :] = zero
        for u in range(18, UNITS):
            if u < 21:
                out[2:ny + 2, u:u + 1, :] = b_ref[u - 18, :, near:near + 1, :]
            else:
                out[2:ny + 2, u:u + 1, :] = r_ref[:, near:near + 1, :]
            ga, gb = ga_ref[u], gb_ref[u]
            out[1, u:u + 1, :] = jnp.where(y_even, gb, ga)[near:near + 1]
            out[ny + 2, u:u + 1, :] = jnp.where(y_even, ga, gb)[near:near + 1]

    @pl.when(x_even)
    def _():
        face(xa_ref, nx - 2, nx - 1)
        face(xb_ref, 0, 0)

    @pl.when(jnp.logical_not(x_even))
    def _():
        face(xb_ref, nx - 2, nx - 1)
        face(xa_ref, 0, 0)


def extend_kernel(e_ref, h_ref, s_ref, b_ref, r_ref, ga_ref, gb_ref, xa_ref, xb_ref,
                  ext_ref, zp_ref, acc_ref):
    ny, nx, nz = r_ref.shape
    wy, wx = ny + 4, nx + 8
    y_even, x_even = is_even("by"), is_even("bx")
    gz0 = lax.axis_index("gz") == 0
    own = [ref.at[c] for ref in (e_ref, h_ref, s_ref, b_ref) for c in range(3)] + [r_ref]
    ext_ref[:, :, nx:, :] = jnp.zeros((ARRAYS, wy, wx - nx, nz), F32)
    for i in range(ARRAYS):
        ext_ref[i, 2:ny + 2, 0:nx, :] = own[i][...]
        u, deep = (2 * i, 2) if i < PAIRS else (9 + i, 1)
        for d in range(2):
            if deep == 2:
                ga, gb = ga_ref[u + d], gb_ref[u + d]
                ext_ref[i, d, 0:nx, :] = jnp.where(y_even, gb, ga)
                ext_ref[i, ny + 2 + d, 0:nx, :] = jnp.where(y_even, ga, gb)
            else:
                ga, gb, zero = ga_ref[u], gb_ref[u], jnp.zeros((nx, nz), F32)
                ext_ref[i, d, 0:nx, :] = jnp.where(y_even, gb, ga) if d == 1 else zero
                ext_ref[i, ny + 2 + d, 0:nx, :] = jnp.where(y_even, ga, gb) if d == 0 else zero
        xa, xb = xa_ref[:, u:u + deep, :], xb_ref[:, u:u + deep, :]
        ext_ref[i, :, nx:nx + deep, :] = jnp.where(x_even, xa, xb)
        ext_ref[i, :, wx - deep:, :] = jnp.where(x_even, xb, xa)

    lane = lanes((wx, nz))
    back = jnp.where(gz0, 1, 0)

    def pack(y, carry):
        acc = jnp.zeros((wx, nz), F32)
        for i in range(ARRAYS):
            if i < PAIRS:
                acc = jnp.where(lane // 2 == i, pltpu.roll(ext_ref[i, y], 2 * i + 2 * back, 1), acc)
            else:
                acc = jnp.where(lane == 9 + i, pltpu.roll(ext_ref[i, y], 9 + i + back, 1), acc)
        acc_ref[pl.ds(pl.multiple_of(y * wx, 8), wx), :] = acc
        return carry

    lax.fori_loop(0, wy, pack, 0, unroll=2)
    full = acc_ref.shape[0]
    acc_ref[wy * wx:, :] = jnp.zeros((full - wy * wx, nz), F32)
    zp_ref[...] = acc_ref[...].T[:UNITS_PAD]


def curl_of(dx, dy, dz):
    return dy[2] - dz[1], dz[0] - dx[2], dx[1] - dy[0]


def slab_planes(slab_ref, wx, by0, bx0):
    full = slab_ref.shape[2]
    lane = lanes((8, full))
    line = (lane * 683) >> 14
    column = lane - line * wx
    mask = jnp.where((by0 & (line < 2)) | (bx0 & (column >= wx - 2)), 0.0, 1.0)

    def plus(f):
        ahead = lambda a: jnp.where(column == wx - 1, pltpu.roll(a, wx - 1, 1), pltpu.roll(a, full - 1, 1)) - a
        return curl_of(
            (None, ahead(f[1]), ahead(f[2])),
            (pltpu.roll(f[0], full - wx, 1) - f[0], None, pltpu.roll(f[2], full - wx, 1) - f[2]),
            (pltpu.roll(f[0], 7, 0) - f[0], pltpu.roll(f[1], 7, 0) - f[1]),
        )

    def minus(f):
        behind = lambda a: a - jnp.where(column == 0, pltpu.roll(a, full - wx + 1, 1), pltpu.roll(a, 1, 1))
        return curl_of(
            (None, behind(f[1]), behind(f[2])),
            (f[0] - pltpu.roll(f[0], wx, 1), None, f[2] - pltpu.roll(f[2], wx, 1)),
            (f[0] - pltpu.roll(f[0], 1, 0), f[1] - pltpu.roll(f[1], 1, 0)),
        )

    e, h, s, b = ([slab_ref[3 * k + c] for c in range(3)] for k in range(4))
    code = slab_ref[12]
    ratio = jnp.abs(code)
    h1 = [(a - time_step * d) * mask for a, d in zip(h, plus(e))]
    g1 = [d * mask for d in plus(s)]
    e1 = [a + ratio * d for a, d in zip(b, minus(h1))]
    s1 = [jnp.where(code < 0, a * (1.0 - ratio), a) - time_step * ratio * d for a, d in zip(s, minus(g1))]
    h2 = [(a - time_step * d) * mask for a, d in zip(h1, plus(e1))]
    g2 = [(a + d) * mask for a, d in zip(g1, plus(s1))]
    return (e, e1, s, s1), (h1, h2, g1, g2)


def main_kernel(ext_ref, zo_ref, zg_ref, j1_ref, c_ref, w_ref, q_ref, place_ref, ids_ref, basis_ref,
                e2_ref, a0_ref, send_ref,
                slab_ref, plane_ref, col_ref, h1_ref, g1_ref, e1_ref, s1_ref, h2_ref, g2_ref,
                d1_ref, d2_ref, cell_ref, blocks_ref, sem):
    fetch = pltpu.make_async_copy(basis_ref, blocks_ref, sem)
    fetch.start()
    ny, nx, nz = w_ref.shape
    wy, wx = ny + 4, nx + 8
    by0, bx0 = lax.axis_index("by") == 0, lax.axis_index("bx") == 0
    gz0 = lax.axis_index("gz") == 0

    for i in range(ARRAYS):
        u, deep = (2 * i, 2) if i < PAIRS else (9 + i, 1)
        mine, other = zo_ref[u:u + deep, :], zg_ref[u:u + deep, :]
        slab_ref[i] = jnp.zeros(slab_ref.shape[1:], F32)
        slab_ref[i, 2 - deep:2, :] = jnp.where(gz0, mine, other)
        slab_ref[i, 2:2 + deep, :] = jnp.where(gz0, other, mine)
    upper, lower = slab_planes(slab_ref, wx, by0, bx0)
    plane_ref[...] = jnp.zeros(plane_ref.shape, F32)
    for p in range(4):
        for c in range(2):
            plane_ref[2 * p + c:2 * p + c + 1, :] = jnp.where(gz0, upper[p][c][2:3], lower[p][c][1:2])
    col_ref[...] = plane_ref[...].T

    lane = lanes((wx, nz))
    column = lax.broadcasted_iota(jnp.int32, (wx, nz), 0)
    x_mask = jnp.where(bx0 & (column >= wx - 2), 0.0, 1.0)
    up_part, low_part = jnp.where(gz0, 1.0, 0.0), jnp.where(gz0, 0.0, 1.0)

    def mask_of(y):
        return x_mask * jnp.where(by0 & (y < 2), 0.0, 1.0)

    def cols_of(y):
        return col_ref[pl.ds(pl.multiple_of(y * wx, 8), wx), :]

    def plus(ref, y, cols, p):
        f, g = [ref[c, y] for c in range(3)], [ref[c, y + 1] for c in (0, 2)]
        dz = []
        for c in range(2):
            k = 2 * p + c
            beyond = (pltpu.roll(cols, nz - k, 1) if k else cols) * up_part
            dz.append(pltpu.roll(jnp.where(lane == 0, beyond, f[c]), nz - 1, 1) - f[c])
        dx = [None] + [pltpu.roll(f[c], wx - 1, 0) - f[c] for c in (1, 2)]
        return curl_of(dx, (g[0] - f[0], None, g[1] - f[2]), dz)

    def minus(ref, y, cols, p):
        f, g = [ref[c, y] for c in range(3)], [ref[c, y - 1] for c in (0, 2)]
        dz = []
        for c in range(2):
            k = 2 * p + c
            beyond = pltpu.roll(cols, nz - 1 - k, 1) * low_part
            dz.append(f[c] - pltpu.roll(jnp.where(lane == nz - 1, beyond, f[c]), 1, 1))
        dx = [None] + [f[c] - pltpu.roll(f[c], 1, 0) for c in (1, 2)]
        return curl_of(dx, (f[0] - g[0], None, f[2] - g[1]), dz)

    e_ext, h_ext, s_ext, b_ext = (ext_ref.at[3 * k:3 * k + 3] for k in range(4))

    def first_magnetic(y, carry):
        cols, mask = cols_of(y), mask_of(y)
        for c, d in enumerate(plus(e_ext, y, cols, 0)):
            h1_ref[c, y] = (h_ext[c, y] - time_step * d) * mask
        for c, d in enumerate(plus(s_ext, y, cols, 2)):
            g1_ref[c, y] = d * mask
        return carry

    def first_electric(y, carry):
        cols, code = cols_of(y), ext_ref[12, y]
        ratio = jnp.abs(code)
        for c, d in enumerate(minus(h1_ref, y, cols, 0)):
            d1_ref[c, y] = d[:nx]
            e1_ref[c, y] = b_ext[c, y] + ratio * d
        for c, d in enumerate(minus(g1_ref, y, cols, 2)):
            d2_ref[c, y] = d[:nx]
            s = s_ext[c, y]
            s1_ref[c, y] = jnp.where(code < 0, s * (1.0 - ratio), s) - time_step * ratio * d
        return carry

    def second_magnetic(y, carry):
        cols, mask = cols_of(y), mask_of(y)
        for c, d in enumerate(plus(e1_ref, y, cols, 1)):
            h2_ref[c, y] = (h1_ref[c, y] - time_step * d) * mask
        for c, d in enumerate(plus(s1_ref, y, cols, 3)):
            g2_ref[c, y] = (g1_ref[c, y] + d) * mask
        return carry

    def second_electric(y, carry):
        cols, at = cols_of(y), y - 2
        code = ext_ref[12, y, 0:nx, :]
        ratio, silver = jnp.abs(code), code < 0
        eps = jnp.zeros((nx, nz), F32)
        for c, (d, g) in enumerate(zip(minus(h2_ref, y, cols, 1), minus(g2_ref, y, cols, 3))):
            e1, s1, s = e1_ref[c, y, 0:nx, :], s1_ref[c, y, 0:nx, :], s_ext[c, y, 0:nx, :]
            j1 = j1_ref[c, at]
            drive = d[:nx] - jnp.where(silver, drude_keep * j1 + drude_gain * e1, 0.0)
            final = e1 + ratio * drive
            if c == 2:
                final = final + (source_level * source_wave[1]) * q_ref[at]
            e2_ref[c, at] = final
            eps = eps + s * drive + s1 * (d1_ref[c, y] - j1)
            back = c_ref[c, at] - time_step * (d2_ref[c, y] + g[:nx])
            a0_ref[c, at] = back - jnp.where(silver, drude_gain * ((1.0 + drude_keep) * s + s1), 0.0)
        cell_ref[pl.ds(pl.multiple_of(at * nx, 8), nx), :] = w_ref[at] * eps
        return carry

    lax.fori_loop(0, wy - 1, first_magnetic, 0)
    lax.fori_loop(1, wy - 1, first_electric, 0)
    lax.fori_loop(1, wy - 2, second_magnetic, 0)
    lax.fori_loop(2, wy - 2, second_electric, 0)

    tiles = ny * nx // 2
    cells = jnp.concatenate([cell_ref[pl.ds(0, tiles, stride=2), :], cell_ref[pl.ds(1, tiles, stride=2), :]], axis=1)
    cells = cells.astype(BF16)
    fetch.wait()
    tile_rows = blocks_ref.shape[0] // tiles
    group = 8
    at_lane = lanes((tile_rows, tiles))

    def project(n, acc):
        start = pl.multiple_of(n * (group * tile_rows), group * tile_rows)
        prods = lax.dot_general(blocks_ref[pl.ds(start, group * tile_rows), :], cells,
                                (((1,), (1,)), ((), ())), preferred_element_type=F32)
        for i in range(group):
            acc = jnp.where(at_lane == n * group + i, prods[i * tile_rows:(i + 1) * tile_rows], acc)
        return acc

    acc = lax.fori_loop(0, tiles // group, project, jnp.zeros((tile_rows, tiles), F32))
    partial = jnp.concatenate([acc[:KB], acc[KB:]], axis=1)
    high = partial.astype(BF16)
    low = (partial - high.astype(F32)).astype(BF16)
    zero = jnp.zeros(high.shape, BF16)
    out = jnp.zeros((place_ref.shape[1], 2 * KB), F32)
    for part in (high, low):
        for half in range(2):
            rows = jnp.concatenate([part, zero] if half == 0 else [zero, part], axis=0)
            out = out + lax.dot_general(place_ref[half], rows, (((1,), (1,)), ((), ())), preferred_element_type=F32)
    planes, width, _ = send_ref.shape
    send_ref[...] = out.reshape(planes, width, 2 * KB)
    id_row = rows_of(planes, place_ref.shape[2])
    for d in range(planes):
        send_ref[d, id_row:id_row + 1, :] = ids_ref[d:d + 1, :]


def capacity_of(planes, blocks):
    return max(2, 2 * blocks // planes)


def rows_of(planes, blocks):
    return capacity_of(planes, blocks) // 2


def place_kernel(rows, width, owner_ref, group_ref, place_ref, ids_ref):
    blocks = owner_ref.shape[1]
    planes = ids_ref.shape[0]
    row, column = (lax.broadcasted_iota(jnp.int32, (blocks, blocks), k) for k in range(2))
    half = blocks // 2
    swap = jnp.where(row == jnp.where(column < half, 2 * column, 2 * (column - half) + 1), 1.0, 0.0).astype(BF16)

    def arranged(ref):
        wide = jnp.broadcast_to(ref[...].astype(F32), (8, blocks)).astype(BF16)
        return lax.dot_general(wide, swap, (((1,), (0,)), ((), ())), preferred_element_type=F32)[:1]

    owner, group = arranged(owner_ref), arranged(group_ref)
    plane = lax.broadcasted_iota(jnp.int32, (planes, blocks), 0).astype(F32)
    hits = jnp.where(plane == owner, 1.0, 0.0)
    earlier = jnp.where(row < column, 1.0, 0.0).astype(BF16)
    before = lax.dot_general(hits.astype(BF16), earlier, (((1,), (0,)), ((), ())), preferred_element_type=F32)
    rank = jnp.sum(before * hits, axis=0, keepdims=True)
    slots = place_ref.shape[1]
    slot = lax.broadcasted_iota(jnp.int32, (slots, blocks), 0).astype(F32)
    for k in range(2):
        inner = rank - float(k * rows)
        target = jnp.where((inner >= 0.0) & (inner < float(rows)), owner * float(width) + inner, -1.0)
        place_ref[k] = jnp.where(slot == target, 1.0, 0.0).astype(BF16)
    ranks = lax.broadcasted_iota(jnp.int32, (128, blocks), 0).astype(F32)
    ranked = jnp.where(ranks == rank, 1.0, 0.0).astype(BF16)
    named = (hits * (group + 1.0)).astype(BF16)
    ids_ref[...] = lax.dot_general(named, ranked, (((1,), (1,)), ((), ())), preferred_element_type=F32) - 1.0


def collect_kernel(rows, got_ref, coef_ref):
    planes, width, line = got_ref.shape
    shape = (planes, width, line)
    ids = jnp.broadcast_to(got_ref[:, rows:rows + 1, :], shape)
    place = lax.broadcasted_iota(jnp.int32, shape, 1)
    lane = lanes(shape)
    values = got_ref[...].reshape(planes * width, line).T
    high = values.astype(BF16)
    low = (values - high.astype(F32)).astype(BF16)
    parts = []
    for k in range(2):
        mine = jnp.sum(jnp.where(lane == place + k * rows, ids + 1.0, 0.0), axis=2, keepdims=True)
        mine = jnp.where(place < rows, mine, 0.0)
        hits = jnp.where(mine == lane.astype(F32) + 1.0, 1.0, 0.0).astype(BF16)
        hits = hits.reshape(planes * width, line)
        dots = [lax.dot_general(part, hits, (((1,), (0,)), ((), ())), preferred_element_type=F32) for part in (high, low)]
        parts.append((dots[0] + dots[1])[k * KB:(k + 1) * KB])
    coef_ref[...] = parts[0] + parts[1]


def call(kernel, outs, ins, scratch=(), smem_first=False, any_last=False, flops=100000):
    specs = [pl.BlockSpec(memory_space=pltpu.VMEM) for _ in ins]
    if smem_first:
        specs[0] = pl.BlockSpec(memory_space=pltpu.SMEM)
    if any_last:
        specs[-1] = pl.BlockSpec(memory_space=pl.ANY)
    return pl.pallas_call(
        kernel,
        out_shape=[jax.ShapeDtypeStruct(*o) for o in outs],
        in_specs=specs,
        out_specs=[pl.BlockSpec(memory_space=pltpu.VMEM) for _ in outs],
        scratch_shapes=list(scratch),
        compiler_params=pltpu.CompilerParams(vmem_limit_bytes=LIMIT),
    )(*ins)


def swapped(first, second, axis):
    size = lax.axis_size(axis)
    arrived = []
    for start, value in ((0, first), (1, second)):
        pairs = []
        for low in range(start, size - 1, 2):
            pairs += [(low, low + 1), (low + 1, low)]
        arrived.append(lax.ppermute(value, axis, pairs) if pairs else jnp.zeros_like(value))
    return arrived


def local(electric_start, magnetic_start, current_start, cotangent, level_set, material, source_cell, basis,
          block_owner, block_group):
    ny, nx, nz = material.shape
    wy, wx = ny + 4, nx + 8
    field, scalar = ((3, ny, nx, nz), F32), ((ny, nx, nz), F32)
    blocks = basis.shape[0]
    planes = lax.axis_size("bx") * lax.axis_size("by")
    rows = rows_of(planes, blocks)
    width = -(-(rows + 1) // 8) * 8
    place, ids = call(
        functools.partial(place_kernel, rows, width),
        [((2, planes * width, blocks), BF16), ((planes, 128), F32)],
        [block_owner.reshape(1, blocks), block_group.reshape(1, blocks)],
    )
    face = ((UNITS, nx, nz), F32)
    fa, fb, b, s, r, w, j1, q = call(
        prepare_kernel,
        [face, face, field, field, scalar, scalar, field, scalar],
        [source_cell, electric_start, magnetic_start, current_start, cotangent, level_set, material],
        smem_first=True,
    )
    ga, gb = swapped(fa, fb, "by")
    x_face = ((wy, UNITS_PAD, nz), F32)
    xa, xb = call(x_face_kernel, [x_face, x_face], [electric_start, magnetic_start, s, b, r, ga, gb])
    xa, xb = swapped(xa, xb, "bx")
    full = -(-wy * wx // 128) * 128
    ext, zp = call(
        extend_kernel,
        [((ARRAYS, wy, wx, nz), F32), ((UNITS_PAD, full), F32)],
        [electric_start, magnetic_start, s, b, r, ga, gb, xa, xb],
        scratch=[pltpu.VMEM((full, nz), F32)],
    )
    zg = lax.ppermute(zp, "gz", [(0, 1), (1, 0)])
    wide = pltpu.VMEM((3, wy, wx, nz), F32)
    inner = pltpu.VMEM((3, wy, nx, nz), F32)
    electric, adjoint, send = call(
        main_kernel,
        [field, field, ((planes, width, 2 * KB), F32)],
        [ext, zp, zg, j1, cotangent, w, q, place, ids, basis.reshape(blocks * KB, basis.shape[2])],
        scratch=[
            pltpu.VMEM((ARRAYS, 8, full), F32),
            pltpu.VMEM((128, full), F32),
            pltpu.VMEM((full, 128), F32),
            wide, wide, wide, wide, wide, wide,
            inner, inner,
            pltpu.VMEM((ny * nx, nz), F32),
            pltpu.VMEM((blocks * KB, basis.shape[2]), BF16),
            pltpu.SemaphoreType.DMA,
        ],
        any_last=True,
    )
    got = lax.all_to_all(send, ("bx", "by"), split_axis=0, concat_axis=0, tiled=True)
    (coef,) = call(functools.partial(collect_kernel, rows), [((KB, GRP_DEV), F32)], [got])
    return electric, adjoint, coef


def solution(mesh):
    field = P(None, "by", "bx", "gz")
    scalar = P("by", "bx", "gz")
    flat = ("bx", "by", "gz")
    return jax.shard_map(
        local,
        mesh=mesh,
        in_specs=(field, field, field, field, scalar, scalar, P(flat), P(flat, None, None), P(flat, None), P(flat)),
        out_specs=(field, field, P(None, flat)),
        check_vma=False,
    )
```

```python
import functools

import jax
import jax.numpy as jnp
from jax import lax
from jax.experimental import pallas as pl
from jax.experimental.pallas import tpu as pltpu
from jax.sharding import PartitionSpec as P

KB = 64
GRP_DEV = 128

time_step = 0.5
drude_keep = 0.9
drude_gain = 1.0
metal_permit = 3.0
design_contrast = 5.0
source_level = 3.0
source_wave = (1.0, -0.6, 0.8, -0.4)

PAIRS, SINGLES = 9, 4
UNITS = 2 * PAIRS + SINGLES
UNITS_PAD = 24
ARRAYS = PAIRS + SINGLES
F32 = jnp.float32
BF16 = jnp.bfloat16


def is_even(axis):
    return lax.rem(lax.axis_index(axis), 2) == 0


def lanes(shape):
    return lax.broadcasted_iota(jnp.int32, shape, len(shape) - 1)


def prepare_kernel(cells_ref, e_ref, h_ref, j_ref, c_ref, level_ref, mat_ref,
                   fa_ref, fb_ref, xa_ref, xb_ref, own_ref, w_ref, j1_ref, q_ref, c_out_ref):
    ny, nx, nz = mat_ref.shape
    flat = lax.broadcasted_iota(jnp.int32, (nx, nz), 0) * nz + lanes((nx, nz))

    def row(y, carry):
        mat = mat_ref[y]
        silver, design = mat == 2, mat == 1
        smooth = 1.0 / (1.0 + jnp.exp(-level_ref[y]))
        permit = jnp.where(silver, metal_permit, jnp.where(design, 1.0 + design_contrast * smooth, 1.0))
        ratio = time_step / permit
        own_ref[12, y] = jnp.where(silver, -ratio, ratio)
        w_ref[y] = jnp.where(design, (-design_contrast / time_step) * ratio * smooth * (1.0 - smooth), 0.0)
        count = jnp.zeros((nx, nz), F32)
        for i in range(cells_ref.shape[0]):
            count = count + jnp.where(flat + y * (nx * nz) == cells_ref[i], 1.0, 0.0)
        q_ref[y] = count
        for c in range(3):
            electric, weight = e_ref[c, y], c_ref[c, y]
            current = jnp.where(silver, drude_keep * j_ref[c, y] + drude_gain * electric, 0.0)
            j1_ref[c, y] = current
            start = electric - ratio * current
            if c == 2:
                start = start + (source_level * source_wave[0]) * count
            own_ref[c, y] = electric
            own_ref[3 + c, y] = h_ref[c, y]
            own_ref[6 + c, y] = ratio * weight
            own_ref[9 + c, y] = start
            c_out_ref[c, y] = weight
        return carry

    lax.fori_loop(0, ny, row, 0, unroll=4)

    def y_face(out, low, near):
        for i in range(PAIRS):
            for d in range(2):
                out[2 * i + d] = own_ref[i, low + d]
        for i in range(PAIRS, ARRAYS):
            out[9 + i] = own_ref[i, near]

    def x_face(out, low, near):
        out[:, UNITS:, :] = jnp.zeros((ny, UNITS_PAD - UNITS, nz), F32)
        for i in range(PAIRS):
            out[:, 2 * i:2 * i + 2, :] = own_ref[i, :, low:low + 2, :]
        for i in range(PAIRS, ARRAYS):
            out[:, 9 + i:10 + i, :] = own_ref[i, :, near:near + 1, :]

    for face, even, a_ref, b_ref, n in ((y_face, is_even("by"), fa_ref, fb_ref, ny), (x_face, is_even("bx"), xa_ref, xb_ref, nx)):
        @pl.when(even)
        def _():
            face(a_ref, n - 2, n - 1)
            face(b_ref, 0, 0)

        @pl.when(jnp.logical_not(even))
        def _():
            face(b_ref, n - 2, n - 1)
            face(a_ref, 0, 0)


def corner_kernel(ga_ref, gb_ref, ca_ref, cb_ref):
    nx, nz = ga_ref.shape[1:]
    y_even, x_even = is_even("by"), is_even("bx")

    def face(out, low, near):
        out[...] = jnp.zeros(out.shape, F32)
        for i in range(ARRAYS):
            u, deep = (2 * i, 2) if i < PAIRS else (9 + i, 1)
            first = low if deep == 2 else near
            for d in range(deep):
                ga, gb = ga_ref[u + d], gb_ref[u + d]
                out[d if deep == 2 else 1, u:u + deep, :] = jnp.where(y_even, gb, ga)[first:first + deep]
                out[2 + d, u:u + deep, :] = jnp.where(y_even, ga, gb)[first:first + deep]

    @pl.when(x_even)
    def _():
        face(ca_ref, nx - 2, nx - 1)
        face(cb_ref, 0, 0)

    @pl.when(jnp.logical_not(x_even))
    def _():
        face(cb_ref, nx - 2, nx - 1)
        face(ca_ref, 0, 0)


def extend_kernel(own_ref, ga_ref, gb_ref, xa_ref, xb_ref, ca_ref, cb_ref, ext_ref, zp_ref, acc_ref):
    ny, nx, nz = own_ref.shape[1:]
    wy, wx = ny + 4, nx + 8
    y_even, x_even = is_even("by"), is_even("bx")
    gz0 = lax.axis_index("gz") == 0
    ext_ref[:, :, nx:, :] = jnp.zeros((ARRAYS, wy, wx - nx, nz), F32)
    for i in range(ARRAYS):
        ext_ref[i, 2:ny + 2, 0:nx, :] = own_ref[i]
        u, deep = (2 * i, 2) if i < PAIRS else (9 + i, 1)
        for d in range(2):
            if deep == 2:
                ga, gb = ga_ref[u + d], gb_ref[u + d]
                ext_ref[i, d, 0:nx, :] = jnp.where(y_even, gb, ga)
                ext_ref[i, ny + 2 + d, 0:nx, :] = jnp.where(y_even, ga, gb)
            else:
                ga, gb, zero = ga_ref[u], gb_ref[u], jnp.zeros((nx, nz), F32)
                ext_ref[i, d, 0:nx, :] = jnp.where(y_even, gb, ga) if d == 1 else zero
                ext_ref[i, ny + 2 + d, 0:nx, :] = jnp.where(y_even, ga, gb) if d == 0 else zero
        for a_ref, b_ref, first, last, to in ((xa_ref, xb_ref, 0, ny, 2), (ca_ref, cb_ref, 0, 2, 0), (ca_ref, cb_ref, 2, 4, ny + 2)):
            a, b = a_ref[first:last, u:u + deep, :], b_ref[first:last, u:u + deep, :]
            rows = slice(to, to + last - first)
            ext_ref[i, rows, nx:nx + deep, :] = jnp.where(x_even, a, b)
            ext_ref[i, rows, wx - deep:, :] = jnp.where(x_even, b, a)

    lane = lanes((wx, nz))
    back = jnp.where(gz0, 1, 0)

    def pack(y, carry):
        acc = jnp.zeros((wx, nz), F32)
        for i in range(ARRAYS):
            if i < PAIRS:
                acc = jnp.where(lane // 2 == i, pltpu.roll(ext_ref[i, y], 2 * i + 2 * back, 1), acc)
            else:
                acc = jnp.where(lane == 9 + i, pltpu.roll(ext_ref[i, y], 9 + i + back, 1), acc)
        acc_ref[pl.ds(pl.multiple_of(y * wx, 8), wx), :] = acc
        return carry

    lax.fori_loop(0, wy, pack, 0, unroll=4)
    full = acc_ref.shape[0]
    acc_ref[wy * wx:, :] = jnp.zeros((full - wy * wx, nz), F32)
    zp_ref[...] = acc_ref[...].T[:UNITS_PAD]


def curl_of(dx, dy, dz):
    return dy[2] - dz[1], dz[0] - dx[2], dx[1] - dy[0]


def slab_planes(slab_ref, wx, by0, bx0):
    full = slab_ref.shape[2]
    lane = lanes((8, full))
    line = (lane * 683) >> 14
    column = lane - line * wx
    mask = jnp.where((by0 & (line < 2)) | (bx0 & (column >= wx - 2)), 0.0, 1.0)

    def plus(f):
        ahead = lambda a: jnp.where(column == wx - 1, pltpu.roll(a, wx - 1, 1), pltpu.roll(a, full - 1, 1)) - a
        return curl_of(
            (None, ahead(f[1]), ahead(f[2])),
            (pltpu.roll(f[0], full - wx, 1) - f[0], None, pltpu.roll(f[2], full - wx, 1) - f[2]),
            (pltpu.roll(f[0], 7, 0) - f[0], pltpu.roll(f[1], 7, 0) - f[1]),
        )

    def minus(f):
        behind = lambda a: a - jnp.where(column == 0, pltpu.roll(a, full - wx + 1, 1), pltpu.roll(a, 1, 1))
        return curl_of(
            (None, behind(f[1]), behind(f[2])),
            (f[0] - pltpu.roll(f[0], wx, 1), None, f[2] - pltpu.roll(f[2], wx, 1)),
            (f[0] - pltpu.roll(f[0], 1, 0), f[1] - pltpu.roll(f[1], 1, 0)),
        )

    e, h, s, b = ([slab_ref[3 * k + c] for c in range(3)] for k in range(4))
    code = slab_ref[12]
    ratio = jnp.abs(code)
    h1 = [(a - time_step * d) * mask for a, d in zip(h, plus(e))]
    g1 = [d * mask for d in plus(s)]
    e1 = [a + ratio * d for a, d in zip(b, minus(h1))]
    s1 = [jnp.where(code < 0, a * (1.0 - ratio), a) - time_step * ratio * d for a, d in zip(s, minus(g1))]
    h2 = [(a - time_step * d) * mask for a, d in zip(h1, plus(e1))]
    g2 = [(a + d) * mask for a, d in zip(g1, plus(s1))]
    return (e, e1, s, s1), (h1, h2, g1, g2)


def main_kernel(ext_ref, zo_ref, zg_ref, j1_ref, c_ref, w_ref, q_ref, place_ref, ids_ref, blocks_ref,
                e2_ref, a0_ref, send_ref,
                slab_ref, plane_ref, col_ref, h1_ref, g1_ref, e1_ref, s1_ref, h2_ref, g2_ref,
                d1_ref, d2_ref, cell_ref):
    ny, nx, nz = w_ref.shape
    wy, wx = ny + 4, nx + 8
    by0, bx0 = lax.axis_index("by") == 0, lax.axis_index("bx") == 0
    gz0 = lax.axis_index("gz") == 0

    for i in range(ARRAYS):
        u, deep = (2 * i, 2) if i < PAIRS else (9 + i, 1)
        mine, other = zo_ref[u:u + deep, :], zg_ref[u:u + deep, :]
        slab_ref[i] = jnp.zeros(slab_ref.shape[1:], F32)
        slab_ref[i, 2 - deep:2, :] = jnp.where(gz0, mine, other)
        slab_ref[i, 2:2 + deep, :] = jnp.where(gz0, other, mine)
    upper, lower = slab_planes(slab_ref, wx, by0, bx0)
    plane_ref[...] = jnp.zeros(plane_ref.shape, F32)
    for p in range(4):
        for c in range(2):
            plane_ref[2 * p + c:2 * p + c + 1, :] = jnp.where(gz0, upper[p][c][2:3], lower[p][c][1:2])
    col_ref[...] = plane_ref[...].T

    lane = lanes((wx, nz))
    column = lax.broadcasted_iota(jnp.int32, (wx, nz), 0)
    x_mask = jnp.where(bx0 & (column >= wx - 2), 0.0, 1.0)
    up_part, low_part = jnp.where(gz0, 1.0, 0.0), jnp.where(gz0, 0.0, 1.0)

    def mask_of(y):
        return x_mask * jnp.where(by0 & (y < 2), 0.0, 1.0)

    def cols_of(y):
        return col_ref[pl.ds(pl.multiple_of(y * wx, 8), wx), :]

    def plus(ref, y, cols, p):
        f, g = [ref[c, y] for c in range(3)], [ref[c, y + 1] for c in (0, 2)]
        dz = []
        for c in range(2):
            k = 2 * p + c
            beyond = (pltpu.roll(cols, nz - k, 1) if k else cols) * up_part
            dz.append(pltpu.roll(jnp.where(lane == 0, beyond, f[c]), nz - 1, 1) - f[c])
        dx = [None] + [pltpu.roll(f[c], wx - 1, 0) - f[c] for c in (1, 2)]
        return curl_of(dx, (g[0] - f[0], None, g[1] - f[2]), dz)

    def minus(ref, y, cols, p):
        f, g = [ref[c, y] for c in range(3)], [ref[c, y - 1] for c in (0, 2)]
        dz = []
        for c in range(2):
            k = 2 * p + c
            beyond = pltpu.roll(cols, nz - 1 - k, 1) * low_part
            dz.append(f[c] - pltpu.roll(jnp.where(lane == nz - 1, beyond, f[c]), 1, 1))
        dx = [None] + [f[c] - pltpu.roll(f[c], 1, 0) for c in (1, 2)]
        return curl_of(dx, (f[0] - g[0], None, f[2] - g[1]), dz)

    e_ext, h_ext, s_ext, b_ext = (ext_ref.at[3 * k:3 * k + 3] for k in range(4))

    def first_magnetic(y, carry):
        cols, mask = cols_of(y), mask_of(y)
        for c, d in enumerate(plus(e_ext, y, cols, 0)):
            h1_ref[c, y] = (h_ext[c, y] - time_step * d) * mask
        for c, d in enumerate(plus(s_ext, y, cols, 2)):
            g1_ref[c, y] = d * mask
        return carry

    def first_electric(y, carry):
        cols, code = cols_of(y), ext_ref[12, y]
        ratio = jnp.abs(code)
        for c, d in enumerate(minus(h1_ref, y, cols, 0)):
            d1_ref[c, y] = d[:nx]
            e1_ref[c, y] = b_ext[c, y] + ratio * d
        for c, d in enumerate(minus(g1_ref, y, cols, 2)):
            d2_ref[c, y] = d[:nx]
            s = s_ext[c, y]
            s1_ref[c, y] = jnp.where(code < 0, s * (1.0 - ratio), s) - time_step * ratio * d
        return carry

    def second_magnetic(y, carry):
        cols, mask = cols_of(y), mask_of(y)
        for c, d in enumerate(plus(e1_ref, y, cols, 1)):
            h2_ref[c, y] = (h1_ref[c, y] - time_step * d) * mask
        for c, d in enumerate(plus(s1_ref, y, cols, 3)):
            g2_ref[c, y] = (g1_ref[c, y] + d) * mask
        return carry

    def second_electric(y, carry):
        cols, at = cols_of(y), y - 2
        code = ext_ref[12, y, 0:nx, :]
        ratio, silver = jnp.abs(code), code < 0
        eps = jnp.zeros((nx, nz), F32)
        for c, (d, g) in enumerate(zip(minus(h2_ref, y, cols, 1), minus(g2_ref, y, cols, 3))):
            e1, s1, s = e1_ref[c, y, 0:nx, :], s1_ref[c, y, 0:nx, :], s_ext[c, y, 0:nx, :]
            j1 = j1_ref[c, at]
            drive = d[:nx] - jnp.where(silver, drude_keep * j1 + drude_gain * e1, 0.0)
            final = e1 + ratio * drive
            if c == 2:
                final = final + (source_level * source_wave[1]) * q_ref[at]
            e2_ref[c, at] = final
            eps = eps + s * drive + s1 * (d1_ref[c, y] - j1)
            back = c_ref[c, at] - time_step * (d2_ref[c, y] + g[:nx])
            a0_ref[c, at] = back - jnp.where(silver, drude_gain * ((1.0 + drude_keep) * s + s1), 0.0)
        cell_ref[pl.ds(pl.multiple_of(at * nx, 8), nx), :] = w_ref[at] * eps
        return carry

    lax.fori_loop(0, wy - 1, first_magnetic, 0, unroll=4)
    lax.fori_loop(1, wy - 1, first_electric, 0, unroll=4)
    lax.fori_loop(1, wy - 2, second_magnetic, 0, unroll=4)
    lax.fori_loop(2, wy - 2, second_electric, 0, unroll=4)

    tiles = ny * nx // 2
    cells = jnp.concatenate([cell_ref[pl.ds(0, tiles, stride=2), :], cell_ref[pl.ds(1, tiles, stride=2), :]], axis=1)
    cells = cells.astype(BF16)
    tile_rows = blocks_ref.shape[0] // tiles
    group = 32
    at_lane = lanes((tile_rows, tiles))

    def project(n, acc):
        start = pl.multiple_of(n * (group * tile_rows), group * tile_rows)
        prods = lax.dot_general(blocks_ref[pl.ds(start, group * tile_rows), :], cells,
                                (((1,), (1,)), ((), ())), preferred_element_type=F32)
        for i in range(group):
            acc = jnp.where(at_lane == n * group + i, prods[i * tile_rows:(i + 1) * tile_rows], acc)
        return acc

    acc = lax.fori_loop(0, tiles // group, project, jnp.zeros((tile_rows, tiles), F32), unroll=2)
    partial = jnp.concatenate([acc[:KB], acc[KB:]], axis=1)
    high = partial.astype(BF16)
    low = (partial - high.astype(F32)).astype(BF16)
    zero = jnp.zeros(high.shape, BF16)
    out = jnp.zeros((place_ref.shape[1], 2 * KB), F32)
    for part in (high, low):
        for half in range(2):
            rows = jnp.concatenate([part, zero] if half == 0 else [zero, part], axis=0)
            out = out + lax.dot_general(place_ref[half], rows, (((1,), (1,)), ((), ())), preferred_element_type=F32)
    planes, width, _ = send_ref.shape
    send_ref[...] = out.reshape(planes, width, 2 * KB)
    id_row = rows_of(planes, place_ref.shape[2])
    for d in range(planes):
        send_ref[d, id_row:id_row + 1, :] = ids_ref[d:d + 1, :]


def capacity_of(planes, blocks):
    return max(2, 2 * blocks // planes)


def rows_of(planes, blocks):
    return capacity_of(planes, blocks) // 2


def place_kernel(rows, width, owner_ref, group_ref, basis_ref, place_ref, ids_ref, blocks_ref, sem):
    fetch = pltpu.make_async_copy(basis_ref, blocks_ref, sem)
    fetch.start()
    blocks = owner_ref.shape[1]
    planes = ids_ref.shape[0]
    row, column = (lax.broadcasted_iota(jnp.int32, (blocks, blocks), k) for k in range(2))
    half = blocks // 2
    swap = jnp.where(row == jnp.where(column < half, 2 * column, 2 * (column - half) + 1), 1.0, 0.0).astype(BF16)

    def arranged(ref):
        wide = jnp.broadcast_to(ref[...].astype(F32), (8, blocks)).astype(BF16)
        return lax.dot_general(wide, swap, (((1,), (0,)), ((), ())), preferred_element_type=F32)[:1]

    owner, group = arranged(owner_ref), arranged(group_ref)
    plane = lax.broadcasted_iota(jnp.int32, (planes, blocks), 0).astype(F32)
    hits = jnp.where(plane == owner, 1.0, 0.0)
    earlier = jnp.where(row < column, 1.0, 0.0).astype(BF16)
    before = lax.dot_general(hits.astype(BF16), earlier, (((1,), (0,)), ((), ())), preferred_element_type=F32)
    rank = jnp.sum(before * hits, axis=0, keepdims=True)
    slots = place_ref.shape[1]
    slot = lax.broadcasted_iota(jnp.int32, (slots, blocks), 0).astype(F32)
    for k in range(2):
        inner = rank - float(k * rows)
        target = jnp.where((inner >= 0.0) & (inner < float(rows)), owner * float(width) + inner, -1.0)
        place_ref[k] = jnp.where(slot == target, 1.0, 0.0).astype(BF16)
    ranks = lax.broadcasted_iota(jnp.int32, (128, blocks), 0).astype(F32)
    ranked = jnp.where(ranks == rank, 1.0, 0.0).astype(BF16)
    named = (hits * (group + 1.0)).astype(BF16)
    ids_ref[...] = lax.dot_general(named, ranked, (((1,), (1,)), ((), ())), preferred_element_type=F32) - 1.0
    fetch.wait()


def collect_kernel(rows, got_ref, coef_ref):
    planes, width, line = got_ref.shape
    shape = (planes, width, line)
    ids = jnp.broadcast_to(got_ref[:, rows:rows + 1, :], shape)
    place = lax.broadcasted_iota(jnp.int32, shape, 1)
    lane = lanes(shape)
    values = got_ref[...].reshape(planes * width, line).T
    high = values.astype(BF16)
    low = (values - high.astype(F32)).astype(BF16)
    parts = []
    for k in range(2):
        mine = jnp.sum(jnp.where(lane == place + k * rows, ids + 1.0, 0.0), axis=2, keepdims=True)
        mine = jnp.where(place < rows, mine, 0.0)
        hits = jnp.where(mine == lane.astype(F32) + 1.0, 1.0, 0.0).astype(BF16)
        hits = hits.reshape(planes * width, line)
        dots = [lax.dot_general(part, hits, (((1,), (0,)), ((), ())), preferred_element_type=F32) for part in (high, low)]
        parts.append((dots[0] + dots[1])[k * KB:(k + 1) * KB])
    coef_ref[...] = parts[0] + parts[1]


def call(kernel, outs, ins, scratch=(), places=None, leave=0, limit=16, cost=None):
    spaces = places or [pltpu.VMEM] * len(ins)
    keep = lambda a, space: pltpu.with_memory_space_constraint(a, space) if space is pltpu.VMEM else a
    return pl.pallas_call(
        kernel,
        out_shape=[jax.ShapeDtypeStruct(*o) if i < leave else pltpu.VMEM(*o) for i, o in enumerate(outs)],
        in_specs=[pl.BlockSpec(memory_space=pltpu.VMEM if space is None else space) for space in spaces],
        out_specs=[pl.BlockSpec(memory_space=pltpu.VMEM) for _ in outs],
        scratch_shapes=list(scratch),
        compiler_params=pltpu.CompilerParams(vmem_limit_bytes=limit * 1024 * 1024),
        cost_estimate=cost,
    )(*[keep(a, space) for a, space in zip(ins, spaces)])


def swapped(first, second, axis):
    size = lax.axis_size(axis)
    arrived = []
    for start, value in ((0, first), (1, second)):
        pairs = []
        for low in range(start, size - 1, 2):
            pairs += [(low, low + 1), (low + 1, low)]
        arrived.append(lax.ppermute(value, axis, pairs) if pairs else jnp.zeros_like(value))
    return arrived


def local(electric_start, magnetic_start, current_start, cotangent, level_set, material, source_cell, basis,
          block_owner, block_group):
    ny, nx, nz = material.shape
    wy, wx = ny + 4, nx + 8
    field, scalar = ((3, ny, nx, nz), F32), ((ny, nx, nz), F32)
    blocks = basis.shape[0]
    planes = lax.axis_size("bx") * lax.axis_size("by")
    rows = rows_of(planes, blocks)
    width = -(-(rows + 1) // 8) * 8
    y_face, x_face, corner = ((UNITS, nx, nz), F32), ((ny, UNITS_PAD, nz), F32), ((4, UNITS_PAD, nz), F32)
    fa, fb, xa, xb, own, w, j1, q, weight = call(
        prepare_kernel,
        [y_face, y_face, x_face, x_face, ((ARRAYS, ny, nx, nz), F32), scalar, field, scalar, field],
        [source_cell, electric_start, magnetic_start, current_start, cotangent, level_set, material],
        places=[pltpu.SMEM] + [None] * 6, limit=58,
    )
    ga, gb = swapped(fa, fb, "by")
    xa, xb = swapped(xa, xb, "bx")
    ca, cb = call(corner_kernel, [corner, corner], [ga, gb])
    ca, cb, owner, group = lax.optimization_barrier((ca, cb, block_owner.reshape(1, blocks), block_group.reshape(1, blocks)))
    ca, cb = swapped(ca, cb, "bx")
    place, ids, basis_here = call(
        functools.partial(place_kernel, rows, width),
        [((2, planes * width, blocks), BF16), ((planes, 128), F32), ((blocks * KB, basis.shape[2]), BF16)],
        [owner, group, basis.reshape(blocks * KB, basis.shape[2])],
        scratch=[pltpu.SemaphoreType.DMA],
        places=[None, None, pltpu.HBM], limit=46,
    )
    ca, cb, ids = lax.optimization_barrier((ca, cb, ids))
    full = -(-wy * wx // 128) * 128
    ext, zp = call(
        extend_kernel,
        [((ARRAYS, wy, wx, nz), F32), ((UNITS_PAD, full), F32)],
        [own, ga, gb, xa, xb, ca, cb],
        scratch=[pltpu.VMEM((full, nz), F32)],
    )
    zg = lax.ppermute(zp, "gz", [(0, 1), (1, 0)])
    wide = pltpu.VMEM((3, wy, wx, nz), F32)
    inner = pltpu.VMEM((3, wy, nx, nz), F32)
    electric, adjoint, send = call(
        main_kernel,
        [field, field, ((planes, width, 2 * KB), F32)],
        [ext, zp, zg, j1, weight, w, q, place, ids, basis_here],
        scratch=[
            pltpu.VMEM((ARRAYS, 8, full), F32),
            pltpu.VMEM((128, full), F32),
            pltpu.VMEM((full, 128), F32),
            wide, wide, wide, wide, wide, wide,
            inner, inner,
            pltpu.VMEM((ny * nx, nz), F32),
        ],
        leave=2,
        limit=24,
    )
    got = lax.all_to_all(send, ("bx", "by"), split_axis=0, concat_axis=0, tiled=True)
    (coef,) = call(functools.partial(collect_kernel, rows), [((KB, GRP_DEV), F32)], [got], leave=1)
    return electric, adjoint, coef


def solution(mesh):
    field = P(None, "by", "bx", "gz")
    scalar = P("by", "bx", "gz")
    flat = ("bx", "by", "gz")
    return jax.shard_map(
        local,
        mesh=mesh,
        in_specs=(field, field, field, field, scalar, scalar, P(flat), P(flat, None, None), P(flat, None), P(flat)),
        out_specs=(field, field, P(None, flat)),
        check_vma=False,
    )
```

```python
import functools

import jax
import jax.numpy as jnp
from jax import lax
from jax.experimental import pallas as pl
from jax.experimental.pallas import tpu as pltpu
from jax.sharding import PartitionSpec as P

KB = 64
GRP_DEV = 128

time_step = 0.5
drude_keep = 0.9
drude_gain = 1.0
metal_permit = 3.0
design_contrast = 5.0
source_level = 3.0
source_wave = (1.0, -0.6, 0.8, -0.4)

PAIRS, ARRAYS = 9, 13
UNITS = ARRAYS + 4
Z_UNITS = 24
F32 = jnp.float32
BF16 = jnp.bfloat16


def is_even(axis):
    return lax.rem(lax.axis_index(axis), 2) == 0


def lanes(shape):
    return lax.broadcasted_iota(jnp.int32, shape, len(shape) - 1)


def prepare_kernel(cells_ref, e_ref, h_ref, j_ref, c_ref, level_ref, mat_ref,
                   fa_ref, fb_ref, xa_ref, xb_ref, own_ref, w_ref, j1_ref, q_ref, c_out_ref):
    ny, nx, nz = mat_ref.shape
    flat = lax.broadcasted_iota(jnp.int32, (nx, nz), 0) * nz + lanes((nx, nz))

    def row(y, carry):
        mat = mat_ref[y]
        silver, design = mat == 2, mat == 1
        smooth = 1.0 / (1.0 + jnp.exp(-level_ref[y]))
        permit = jnp.where(silver, metal_permit, jnp.where(design, 1.0 + design_contrast * smooth, 1.0))
        ratio = time_step / permit
        own_ref[12, y] = jnp.where(silver, -ratio, ratio)
        w_ref[y] = jnp.where(design, (-design_contrast / time_step) * ratio * smooth * (1.0 - smooth), 0.0)
        count = jnp.zeros((nx, nz), F32)
        for i in range(cells_ref.shape[0]):
            count = count + jnp.where(flat + y * (nx * nz) == cells_ref[i], 1.0, 0.0)
        q_ref[y] = count
        for c in range(3):
            electric, weight = e_ref[c, y], c_ref[c, y]
            current = jnp.where(silver, drude_keep * j_ref[c, y] + drude_gain * electric, 0.0)
            j1_ref[c, y] = current
            start = electric - ratio * current
            if c == 2:
                start = start + (source_level * source_wave[0]) * count
            own_ref[c, y] = electric
            own_ref[3 + c, y] = h_ref[c, y]
            own_ref[6 + c, y] = ratio * weight
            own_ref[9 + c, y] = start
            c_out_ref[c, y] = weight
        return carry

    lax.fori_loop(0, ny, row, 0, unroll=4)

    def y_face(out, near, deep, up):
        layers = [[own_ref[i, y] for i in range(ARRAYS)] for y in (near, deep)]
        for u, unit in enumerate(face_units(*layers, 1, up)):
            out[u] = unit

    lines = own_ref.reshape(ARRAYS * ny * nx, nz)

    def x_face(out, near, deep, up):
        layers = [[lines[pl.ds(i * ny * nx + x, ny, stride=nx), :] for i in range(ARRAYS)] for x in (near, deep)]
        for u, unit in enumerate(face_units(*layers, 0, up)):
            out[u] = unit

    for face, even, a_ref, b_ref, n in ((y_face, is_even("by"), fa_ref, fb_ref, ny), (x_face, is_even("bx"), xa_ref, xb_ref, nx)):
        @pl.when(even)
        def _():
            face(a_ref, n - 1, n - 2, True)
            face(b_ref, 0, 1, False)

        @pl.when(jnp.logical_not(even))
        def _():
            face(b_ref, n - 1, n - 2, True)
            face(a_ref, 0, 1, False)


def face_units(near, deep, axis, up):
    first, second = (axis + 1) % 3, (axis + 2) % 3
    units = list(near)
    if up:
        ratio = jnp.abs(near[12])
        units[9 + first] = near[9 + first] + ratio * (deep[3 + second] + time_step * deep[first])
        units[9 + second] = near[9 + second] - ratio * (deep[3 + first] - time_step * deep[second])
    else:
        units[3 + first] = near[3 + first] + time_step * deep[second]
        units[3 + second] = near[3 + second] - time_step * deep[first]
    return units + [deep[axis], deep[6], deep[7], deep[8]]


def sides(axis, even, a, b):
    at, zero = lax.axis_index(axis), jnp.zeros(a.shape, F32)
    lower = jnp.where(at == 0, zero, jnp.where(even, b, a))
    upper = jnp.where(at == lax.axis_size(axis) - 1, zero, jnp.where(even, a, b))
    return lower, upper


def rows_along_y(ga_ref, gb_ref):
    even, zero = is_even("by"), jnp.zeros(ga_ref.shape[1:], F32)
    units = [sides("by", even, ga_ref[u], gb_ref[u]) for u in range(UNITS)]
    lower, upper = ([unit[k] for unit in units] for k in range(2))
    below = [zero, lower[13], zero] + [zero] * 3 + lower[14:] + [zero] * 4
    above = [zero] * 6 + upper[14:] + [zero] * 4
    return below, lower[:ARRAYS], upper[:ARRAYS], above


def corner_kernel(ga_ref, gb_ref, ca_ref, cb_ref):
    nx = ga_ref.shape[1]
    rows = rows_along_y(ga_ref, gb_ref)
    even = is_even("bx")
    ca_ref[4 * UNITS:, :] = jnp.zeros((ca_ref.shape[0] - 4 * UNITS, ca_ref.shape[1]), F32)
    cb_ref[4 * UNITS:, :] = jnp.zeros((cb_ref.shape[0] - 4 * UNITS, cb_ref.shape[1]), F32)

    def face(out, near, deep, up):
        for k, row in enumerate(rows):
            for u, unit in enumerate(face_units([a[near:near + 1] for a in row], [a[deep:deep + 1] for a in row], 0, up)):
                out[4 * u + k:4 * u + k + 1, :] = unit

    @pl.when(even)
    def _():
        face(ca_ref, nx - 1, nx - 2, True)
        face(cb_ref, 0, 1, False)

    @pl.when(jnp.logical_not(even))
    def _():
        face(cb_ref, nx - 1, nx - 2, True)
        face(ca_ref, 0, 1, False)


def extend_kernel(own_ref, ga_ref, gb_ref, xa_ref, xb_ref, ca_ref, cb_ref, ext_ref, zp_ref, acc_ref):
    ny, nx, nz = own_ref.shape[1:]
    wy, wx = ny + 4, nx + 8
    x_even = is_even("bx")
    gz0 = lax.axis_index("gz") == 0
    ext_ref[:, :, nx:, :] = jnp.zeros((ARRAYS, wy, wx - nx, nz), F32)
    ext_ref[:, 2:ny + 2, 0:nx, :] = own_ref[...]
    for y, row in zip((0, 1, ny + 2, ny + 3), rows_along_y(ga_ref, gb_ref)):
        for i in range(ARRAYS):
            ext_ref[i, y, 0:nx, :] = row[i]
    lines = ext_ref.reshape(ARRAYS * wy * wx, nz)
    for u in range(UNITS):
        i, near = (u, True) if u < ARRAYS else ((0, 6, 7, 8)[u - ARRAYS], False)
        lower, upper = sides("bx", x_even, xa_ref[u], xb_ref[u])
        low_corner, up_corner = sides("bx", x_even, ca_ref[4 * u:4 * u + 4, :], cb_ref[4 * u:4 * u + 4, :])
        for x, side, corner in ((wx - 1 if near else wx - 2, lower, low_corner), (nx if near else nx + 1, upper, up_corner)):
            if u == ARRAYS and side is upper:
                continue
            start = i * wy * wx + x
            lines[pl.ds(start + 2 * wx, ny, stride=wx), :] = side
            for k, y in enumerate((0, 1, ny + 2, ny + 3)):
                lines[start + y * wx:start + y * wx + 1, :] = corner[k:k + 1]

    lane = lanes((wx, nz))
    back = jnp.where(gz0, 1, 0)

    def pack(y, carry):
        acc = jnp.zeros((wx, nz), F32)
        for i in range(ARRAYS):
            if i < PAIRS:
                acc = jnp.where(lane // 2 == i, pltpu.roll(ext_ref[i, y], 2 * i + 2 * back, 1), acc)
            else:
                acc = jnp.where(lane == 9 + i, pltpu.roll(ext_ref[i, y], 9 + i + back, 1), acc)
        acc_ref[pl.ds(pl.multiple_of(y * wx, 8), wx), :] = acc
        return carry

    lax.fori_loop(0, wy, pack, 0, unroll=4)
    full = acc_ref.shape[0]
    acc_ref[wy * wx:, :] = jnp.zeros((full - wy * wx, nz), F32)
    zp_ref[...] = acc_ref[...].T[:Z_UNITS]


def curl_of(dx, dy, dz):
    return dy[2] - dz[1], dz[0] - dx[2], dx[1] - dy[0]


def slab_planes(slab_ref, wx, by0, bx0):
    full = slab_ref.shape[2]
    lane = lanes((8, full))
    line = (lane * 683) >> 14
    column = lane - line * wx
    mask = jnp.where((by0 & (line < 2)) | (bx0 & (column >= wx - 2)), 0.0, 1.0)

    def plus(f):
        ahead = lambda a: jnp.where(column == wx - 1, pltpu.roll(a, wx - 1, 1), pltpu.roll(a, full - 1, 1)) - a
        return curl_of(
            (None, ahead(f[1]), ahead(f[2])),
            (pltpu.roll(f[0], full - wx, 1) - f[0], None, pltpu.roll(f[2], full - wx, 1) - f[2]),
            (pltpu.roll(f[0], 7, 0) - f[0], pltpu.roll(f[1], 7, 0) - f[1]),
        )

    def minus(f):
        behind = lambda a: a - jnp.where(column == 0, pltpu.roll(a, full - wx + 1, 1), pltpu.roll(a, 1, 1))
        return curl_of(
            (None, behind(f[1]), behind(f[2])),
            (f[0] - pltpu.roll(f[0], wx, 1), None, f[2] - pltpu.roll(f[2], wx, 1)),
            (f[0] - pltpu.roll(f[0], 1, 0), f[1] - pltpu.roll(f[1], 1, 0)),
        )

    e, h, s, b = ([slab_ref[3 * k + c] for c in range(3)] for k in range(4))
    code = slab_ref[12]
    ratio = jnp.abs(code)
    h1 = [(a - time_step * d) * mask for a, d in zip(h, plus(e))]
    g1 = [d * mask for d in plus(s)]
    e1 = [a + ratio * d for a, d in zip(b, minus(h1))]
    s1 = [jnp.where(code < 0, a * (1.0 - ratio), a) - time_step * ratio * d for a, d in zip(s, minus(g1))]
    h2 = [(a - time_step * d) * mask for a, d in zip(h1, plus(e1))]
    g2 = [(a + d) * mask for a, d in zip(g1, plus(s1))]
    return (e, e1, s, s1), (h1, h2, g1, g2)


def main_kernel(ext_ref, zo_ref, zg_ref, j1_ref, c_ref, w_ref, q_ref, owner_ref, group_ref, basis_ref,
                e2_ref, a0_ref, send_ref, place_ref, ids_ref, blocks_ref, sem,
                slab_ref, plane_ref, col_ref, h1_ref, g1_ref, e1_ref, s1_ref, h2_ref, g2_ref,
                d1_ref, d2_ref, cell_ref):
    fetch = pltpu.make_async_copy(basis_ref, blocks_ref, sem)
    fetch.start()
    planes, width, _ = send_ref.shape
    rows = rows_of(planes, owner_ref.shape[1])
    make_places(rows, width, owner_ref, group_ref, place_ref, ids_ref)
    ny, nx, nz = w_ref.shape
    wy, wx = ny + 4, nx + 8
    by0, bx0 = lax.axis_index("by") == 0, lax.axis_index("bx") == 0
    gz0 = lax.axis_index("gz") == 0

    for i in range(ARRAYS):
        u, deep = (2 * i, 2) if i < PAIRS else (9 + i, 1)
        mine, other = zo_ref[u:u + deep, :], zg_ref[u:u + deep, :]
        slab_ref[i] = jnp.zeros(slab_ref.shape[1:], F32)
        slab_ref[i, 2 - deep:2, :] = jnp.where(gz0, mine, other)
        slab_ref[i, 2:2 + deep, :] = jnp.where(gz0, other, mine)
    upper, lower = slab_planes(slab_ref, wx, by0, bx0)
    plane_ref[...] = jnp.zeros(plane_ref.shape, F32)
    for p in range(4):
        for c in range(2):
            plane_ref[2 * p + c:2 * p + c + 1, :] = jnp.where(gz0, upper[p][c][2:3], lower[p][c][1:2])
    rest = plane_ref[0:8, :]
    for k in range(3):
        part = rest.astype(BF16).astype(F32)
        plane_ref[8 * k:8 * k + 8, :] = part
        rest = rest - part
    wide = 8 * nz
    row, place = lax.broadcasted_iota(jnp.int32, (128, wide), 0), lanes((128, wide))
    border = place % nz == jnp.where(gz0, 0, nz - 1)
    chosen = jnp.where(border & (row % 8 == place // nz) & (row < 24), 1.0, 0.0).astype(BF16)
    col_ref[...] = lax.dot_general(plane_ref[...].T.astype(BF16), chosen, (((1,), (0,)), ((), ())), preferred_element_type=F32)

    lane = lanes((wx, nz))
    column = lax.broadcasted_iota(jnp.int32, (wx, nz), 0)
    x_mask = jnp.where(bx0 & (column >= wx - 2), 0.0, 1.0)

    def mask_of(y):
        return x_mask * jnp.where(by0 & (y < 2), 0.0, 1.0)

    def beyond(y, k):
        return col_ref[pl.ds(pl.multiple_of(y * wx, 8), wx), k * nz:(k + 1) * nz]

    def plus(ref, y, p):
        f, g = [ref[c, y] for c in range(3)], [ref[c, y + 1] for c in (0, 2)]
        dz = []
        for c in range(2):
            dz.append(pltpu.roll(jnp.where(lane == 0, beyond(y, 2 * p + c), f[c]), nz - 1, 1) - f[c])
        dx = [None] + [pltpu.roll(f[c], wx - 1, 0) - f[c] for c in (1, 2)]
        return curl_of(dx, (g[0] - f[0], None, g[1] - f[2]), dz)

    def minus(ref, y, p):
        f, g = [ref[c, y] for c in range(3)], [ref[c, y - 1] for c in (0, 2)]
        dz = []
        for c in range(2):
            dz.append(f[c] - pltpu.roll(jnp.where(lane == nz - 1, beyond(y, 2 * p + c), f[c]), 1, 1))
        dx = [None] + [f[c] - pltpu.roll(f[c], 1, 0) for c in (1, 2)]
        return curl_of(dx, (f[0] - g[0], None, f[2] - g[1]), dz)

    e_ext, h_ext, s_ext, b_ext = (ext_ref.at[3 * k:3 * k + 3] for k in range(4))

    def first_magnetic(y, carry):
        mask = mask_of(y)
        for c, d in enumerate(plus(e_ext, y, 0)):
            h1_ref[c, y] = (h_ext[c, y] - time_step * d) * mask
        for c, d in enumerate(plus(s_ext, y, 2)):
            g1_ref[c, y] = d * mask
        return carry

    def first_electric(y, carry):
        code = ext_ref[12, y]
        ratio = jnp.abs(code)
        for c, d in enumerate(minus(h1_ref, y, 0)):
            d1_ref[c, y] = d[:nx]
            e1_ref[c, y] = b_ext[c, y] + ratio * d
        for c, d in enumerate(minus(g1_ref, y, 2)):
            d2_ref[c, y] = d[:nx]
            s = s_ext[c, y]
            s1_ref[c, y] = jnp.where(code < 0, s * (1.0 - ratio), s) - time_step * ratio * d
        return carry

    def second_magnetic(y, carry):
        mask = mask_of(y)
        for c, d in enumerate(plus(e1_ref, y, 1)):
            h2_ref[c, y] = (h1_ref[c, y] - time_step * d) * mask
        for c, d in enumerate(plus(s1_ref, y, 3)):
            g2_ref[c, y] = (g1_ref[c, y] + d) * mask
        return carry

    def second_electric(y, carry):
        at = y - 2
        code = ext_ref[12, y, 0:nx, :]
        ratio, silver = jnp.abs(code), code < 0
        eps = jnp.zeros((nx, nz), F32)
        for c, (d, g) in enumerate(zip(minus(h2_ref, y, 1), minus(g2_ref, y, 3))):
            e1, s1, s = e1_ref[c, y, 0:nx, :], s1_ref[c, y, 0:nx, :], s_ext[c, y, 0:nx, :]
            j1 = j1_ref[c, at]
            drive = d[:nx] - jnp.where(silver, drude_keep * j1 + drude_gain * e1, 0.0)
            final = e1 + ratio * drive
            if c == 2:
                final = final + (source_level * source_wave[1]) * q_ref[at]
            e2_ref[c, at] = final
            eps = eps + s * drive + s1 * (d1_ref[c, y] - j1)
            back = c_ref[c, at] - time_step * (d2_ref[c, y] + g[:nx])
            a0_ref[c, at] = back - jnp.where(silver, drude_gain * ((1.0 + drude_keep) * s + s1), 0.0)
        cell_ref[pl.ds(pl.multiple_of(at * nx, 8), nx), :] = w_ref[at] * eps
        return carry

    lax.fori_loop(0, wy - 1, first_magnetic, 0, unroll=4)
    lax.fori_loop(1, wy - 1, first_electric, 0, unroll=4)
    lax.fori_loop(1, wy - 2, second_magnetic, 0, unroll=4)
    lax.fori_loop(2, wy - 2, second_electric, 0, unroll=4)

    tiles = ny * nx // 2
    cells = jnp.concatenate([cell_ref[pl.ds(0, tiles, stride=2), :], cell_ref[pl.ds(1, tiles, stride=2), :]], axis=1)
    cells = cells.astype(BF16)
    fetch.wait()
    tile_rows = blocks_ref.shape[0] // tiles
    group = 32
    at_lane = lanes((tile_rows, tiles))

    def project(n, acc):
        start = pl.multiple_of(n * (group * tile_rows), group * tile_rows)
        prods = lax.dot_general(blocks_ref[pl.ds(start, group * tile_rows), :], cells,
                                (((1,), (1,)), ((), ())), preferred_element_type=F32)
        for i in range(group):
            acc = jnp.where(at_lane == n * group + i, prods[i * tile_rows:(i + 1) * tile_rows], acc)
        return acc

    acc = lax.fori_loop(0, tiles // group, project, jnp.zeros((tile_rows, tiles), F32), unroll=2)
    partial = jnp.concatenate([acc[:KB], acc[KB:]], axis=1)
    high = partial.astype(BF16)
    low = (partial - high.astype(F32)).astype(BF16)
    zero = jnp.zeros(high.shape, BF16)
    out = jnp.zeros((place_ref.shape[1], 2 * KB), F32)
    for part in (high, low):
        for half in range(2):
            both = jnp.concatenate([part, zero] if half == 0 else [zero, part], axis=0)
            out = out + lax.dot_general(place_ref[half], both, (((1,), (1,)), ((), ())), preferred_element_type=F32)
    send_ref[...] = out.reshape(planes, width, 2 * KB)
    for d in range(planes):
        send_ref[d, rows:rows + 1, :] = ids_ref[d:d + 1, :]


def capacity_of(planes, blocks):
    return max(2, 2 * blocks // planes)


def rows_of(planes, blocks):
    return capacity_of(planes, blocks) // 2


def make_places(rows, width, owner_ref, group_ref, place_ref, ids_ref):
    blocks = owner_ref.shape[1]
    planes = ids_ref.shape[0]
    row, column = (lax.broadcasted_iota(jnp.int32, (blocks, blocks), k) for k in range(2))
    half = blocks // 2
    swap = jnp.where(row == jnp.where(column < half, 2 * column, 2 * (column - half) + 1), 1.0, 0.0).astype(BF16)

    def arranged(ref):
        wide = jnp.broadcast_to(ref[...].astype(F32), (8, blocks)).astype(BF16)
        return lax.dot_general(wide, swap, (((1,), (0,)), ((), ())), preferred_element_type=F32)[:1]

    owner, group = arranged(owner_ref), arranged(group_ref)
    plane = lax.broadcasted_iota(jnp.int32, (planes, blocks), 0).astype(F32)
    hits = jnp.where(plane == owner, 1.0, 0.0)
    earlier = jnp.where(row < column, 1.0, 0.0).astype(BF16)
    before = lax.dot_general(hits.astype(BF16), earlier, (((1,), (0,)), ((), ())), preferred_element_type=F32)
    rank = jnp.sum(before * hits, axis=0, keepdims=True)
    slots = place_ref.shape[1]
    slot = lax.broadcasted_iota(jnp.int32, (slots, blocks), 0).astype(F32)
    for k in range(2):
        inner = rank - float(k * rows)
        target = jnp.where((inner >= 0.0) & (inner < float(rows)), owner * float(width) + inner, -1.0)
        place_ref[k] = jnp.where(slot == target, 1.0, 0.0).astype(BF16)
    ranks = lax.broadcasted_iota(jnp.int32, (128, blocks), 0).astype(F32)
    ranked = jnp.where(ranks == rank, 1.0, 0.0).astype(BF16)
    named = (hits * (group + 1.0)).astype(BF16)
    ids_ref[...] = lax.dot_general(named, ranked, (((1,), (1,)), ((), ())), preferred_element_type=F32) - 1.0


def collect_kernel(rows, got_ref, coef_ref):
    planes, width, line = got_ref.shape
    shape = (planes, width, line)
    ids = jnp.broadcast_to(got_ref[:, rows:rows + 1, :], shape)
    place = lax.broadcasted_iota(jnp.int32, shape, 1)
    lane = lanes(shape)
    values = got_ref[...].reshape(planes * width, line).T
    high = values.astype(BF16)
    low = (values - high.astype(F32)).astype(BF16)
    parts = []
    for k in range(2):
        mine = jnp.sum(jnp.where(lane == place + k * rows, ids + 1.0, 0.0), axis=2, keepdims=True)
        mine = jnp.where(place < rows, mine, 0.0)
        hits = jnp.where(mine == lane.astype(F32) + 1.0, 1.0, 0.0).astype(BF16)
        hits = hits.reshape(planes * width, line)
        dots = [lax.dot_general(part, hits, (((1,), (0,)), ((), ())), preferred_element_type=F32) for part in (high, low)]
        parts.append((dots[0] + dots[1])[k * KB:(k + 1) * KB])
    coef_ref[...] = parts[0] + parts[1]


def call(kernel, outs, ins, scratch=(), places=None, leave=0, limit=16, cost=None):
    spaces = places or [pltpu.VMEM] * len(ins)
    keep = lambda a, space: pltpu.with_memory_space_constraint(a, space) if space is pltpu.VMEM else a
    return pl.pallas_call(
        kernel,
        out_shape=[jax.ShapeDtypeStruct(*o) if i < leave else pltpu.VMEM(*o) for i, o in enumerate(outs)],
        in_specs=[pl.BlockSpec(memory_space=pltpu.VMEM if space is None else space) for space in spaces],
        out_specs=[pl.BlockSpec(memory_space=pltpu.VMEM) for _ in outs],
        scratch_shapes=list(scratch),
        compiler_params=pltpu.CompilerParams(vmem_limit_bytes=limit * 1024 * 1024),
        cost_estimate=cost,
    )(*[keep(a, space) for a, space in zip(ins, spaces)])


def swapped(first, second, axis):
    axes = ("bx", "by", "gz")
    sizes = [lax.axis_size(name) for name in axes]
    along = axes.index(axis)
    arrived = []
    for start, value in ((0, first), (1, second)):
        pairs = []
        for flat in range(sizes[0] * sizes[1] * sizes[2]):
            at = [flat // (sizes[1] * sizes[2]), flat // sizes[2] % sizes[1], flat % sizes[2]]
            other = at[along] + 1 if at[along] % 2 == start else at[along] - 1
            if 0 <= other < sizes[along]:
                at[along] = other
            else:
                at[2] = (at[2] + 1) % sizes[2]
            pairs.append((flat, (at[0] * sizes[1] + at[1]) * sizes[2] + at[2]))
        arrived.append(lax.ppermute(value, axes, pairs))
    return arrived


def local(electric_start, magnetic_start, current_start, cotangent, level_set, material, source_cell, basis,
          block_owner, block_group):
    ny, nx, nz = material.shape
    wy, wx = ny + 4, nx + 8
    field, scalar = ((3, ny, nx, nz), F32), ((ny, nx, nz), F32)
    blocks = basis.shape[0]
    planes = lax.axis_size("bx") * lax.axis_size("by")
    rows = rows_of(planes, blocks)
    width = -(-(rows + 1) // 8) * 8
    y_face, x_face, corner = ((UNITS, nx, nz), F32), ((UNITS, ny, nz), F32), ((-(-4 * UNITS // 8) * 8, nz), F32)
    fa, fb, xa, xb, own, w, j1, q, weight = call(
        prepare_kernel,
        [y_face, y_face, x_face, x_face, ((ARRAYS, ny, nx, nz), F32), scalar, field, scalar, field],
        [source_cell, electric_start, magnetic_start, current_start, cotangent, level_set, material],
        places=[pltpu.SMEM] + [None] * 6, limit=58,
    )
    xa, xb = swapped(xa, xb, "bx")
    ga, gb = swapped(fa, fb, "by")
    ca, cb = call(corner_kernel, [corner, corner], [ga, gb])
    ca, cb = swapped(ca, cb, "bx")
    full = -(-wy * wx // 128) * 128
    ext, zp = call(
        extend_kernel,
        [((ARRAYS, wy, wx, nz), F32), ((Z_UNITS, full), F32)],
        [own, ga, gb, xa, xb, ca, cb],
        scratch=[pltpu.VMEM((full, nz), F32)],
    )
    zg = lax.ppermute(zp, "gz", [(0, 1), (1, 0)])
    wide = pltpu.VMEM((3, wy, wx, nz), F32)
    inner = pltpu.VMEM((3, wy, nx, nz), F32)
    electric, adjoint, send = call(
        main_kernel,
        [field, field, ((planes, width, 2 * KB), F32)],
        [ext, zp, zg, j1, weight, w, q, block_owner.reshape(1, blocks), block_group.reshape(1, blocks),
         basis.reshape(blocks * KB, basis.shape[2])],
        scratch=[
            pltpu.VMEM((2, planes * width, blocks), BF16),
            pltpu.VMEM((planes, 128), F32),
            pltpu.VMEM((blocks * KB, basis.shape[2]), BF16),
            pltpu.SemaphoreType.DMA,
            pltpu.VMEM((ARRAYS, 8, full), F32),
            pltpu.VMEM((128, full), F32),
            pltpu.VMEM((full, 8 * nz), F32),
            wide, wide, wide, wide, wide, wide,
            inner, inner,
            pltpu.VMEM((ny * nx, nz), F32),
        ],
        places=[pltpu.VMEM] * 7 + [None, None, pl.ANY],
        limit=50,
    )
    got = lax.all_to_all(send, ("bx", "by"), split_axis=0, concat_axis=0, tiled=True)
    (coef,) = call(functools.partial(collect_kernel, rows), [((KB, GRP_DEV), F32)], [got], leave=1)
    return electric, adjoint, coef


def solution(mesh):
    field = P(None, "by", "bx", "gz")
    scalar = P("by", "bx", "gz")
    flat = ("bx", "by", "gz")
    return jax.shard_map(
        local,
        mesh=mesh,
        in_specs=(field, field, field, field, scalar, scalar, P(flat), P(flat, None, None), P(flat, None), P(flat)),
        out_specs=(field, field, P(None, flat)),
        check_vma=False,
    )
```

```python
import functools

import jax
import jax.numpy as jnp
from jax import lax
from jax.experimental import pallas as pl
from jax.experimental.pallas import tpu as pltpu
from jax.sharding import PartitionSpec as P

KB = 64
GRP_DEV = 128

time_step = 0.5
drude_keep = 0.9
drude_gain = 1.0
metal_permit = 3.0
design_contrast = 5.0
source_level = 3.0
source_wave = (1.0, -0.6, 0.8, -0.4)

PAIRS, ARRAYS = 9, 13
UNITS = ARRAYS + 4
Z_UNITS = 24
F32 = jnp.float32
BF16 = jnp.bfloat16


def is_even(axis):
    return lax.rem(lax.axis_index(axis), 2) == 0


def lanes(shape):
    return lax.broadcasted_iota(jnp.int32, shape, len(shape) - 1)


def prepare_kernel(cells_ref, e_ref, h_ref, j_ref, c_ref, level_ref, mat_ref, owner_ref, group_ref,
                   fa_ref, fb_ref, xa_ref, xb_ref, own_ref, w_ref, j1_ref, q_ref, c_out_ref, owner_out_ref, group_out_ref):
    owner_out_ref[...] = owner_ref[...]
    group_out_ref[...] = group_ref[...]
    ny, nx, nz = mat_ref.shape
    flat = lax.broadcasted_iota(jnp.int32, (nx, nz), 0) * nz + lanes((nx, nz))

    def row(y, carry):
        mat = mat_ref[y]
        silver, design = mat == 2, mat == 1
        smooth = 1.0 / (1.0 + jnp.exp(-level_ref[y]))
        permit = jnp.where(silver, metal_permit, jnp.where(design, 1.0 + design_contrast * smooth, 1.0))
        ratio = time_step / permit
        own_ref[12, y] = jnp.where(silver, -ratio, ratio)
        w_ref[y] = jnp.where(design, (-design_contrast / time_step) * ratio * smooth * (1.0 - smooth), 0.0)
        count = jnp.zeros((nx, nz), F32)
        for i in range(cells_ref.shape[0]):
            count = count + jnp.where(flat + y * (nx * nz) == cells_ref[i], 1.0, 0.0)
        q_ref[y] = count
        for c in range(3):
            electric, weight = e_ref[c, y], c_ref[c, y]
            current = jnp.where(silver, drude_keep * j_ref[c, y] + drude_gain * electric, 0.0)
            j1_ref[c, y] = current
            start = electric - ratio * current
            if c == 2:
                start = start + (source_level * source_wave[0]) * count
            own_ref[c, y] = electric
            own_ref[3 + c, y] = h_ref[c, y]
            own_ref[6 + c, y] = ratio * weight
            own_ref[9 + c, y] = start
            c_out_ref[c, y] = weight
        return carry

    lax.fori_loop(0, ny, row, 0, unroll=4)

    def y_face(out, near, deep, up):
        layers = [[own_ref[i, y] for i in range(ARRAYS)] for y in (near, deep)]
        for u, unit in enumerate(face_units(*layers, 1, up)):
            out[u] = unit

    lines = own_ref.reshape(ARRAYS * ny * nx, nz)

    def x_face(out, near, deep, up):
        layers = [[lines[pl.ds(i * ny * nx + x, ny, stride=nx), :] for i in range(ARRAYS)] for x in (near, deep)]
        for u, unit in enumerate(face_units(*layers, 0, up)):
            out[u] = unit

    for face, even, a_ref, b_ref, n in ((y_face, is_even("by"), fa_ref, fb_ref, ny), (x_face, is_even("bx"), xa_ref, xb_ref, nx)):
        @pl.when(even)
        def _():
            face(a_ref, n - 1, n - 2, True)
            face(b_ref, 0, 1, False)

        @pl.when(jnp.logical_not(even))
        def _():
            face(b_ref, n - 1, n - 2, True)
            face(a_ref, 0, 1, False)


def face_units(near, deep, axis, up):
    first, second = (axis + 1) % 3, (axis + 2) % 3
    units = list(near)
    if up:
        ratio = jnp.abs(near[12])
        units[9 + first] = near[9 + first] + ratio * (deep[3 + second] + time_step * deep[first])
        units[9 + second] = near[9 + second] - ratio * (deep[3 + first] - time_step * deep[second])
    else:
        units[3 + first] = near[3 + first] + time_step * deep[second]
        units[3 + second] = near[3 + second] - time_step * deep[first]
    return units + [deep[axis], deep[6], deep[7], deep[8]]


def sides(axis, even, a, b):
    at, zero = lax.axis_index(axis), jnp.zeros(a.shape, F32)
    lower = jnp.where(at == 0, zero, jnp.where(even, b, a))
    upper = jnp.where(at == lax.axis_size(axis) - 1, zero, jnp.where(even, a, b))
    return lower, upper


def rows_along_y(ga_ref, gb_ref):
    even, zero = is_even("by"), jnp.zeros(ga_ref.shape[1:], F32)
    units = [sides("by", even, ga_ref[u], gb_ref[u]) for u in range(UNITS)]
    lower, upper = ([unit[k] for unit in units] for k in range(2))
    below = [zero, lower[13], zero] + [zero] * 3 + lower[14:] + [zero] * 4
    above = [zero] * 6 + upper[14:] + [zero] * 4
    return below, lower[:ARRAYS], upper[:ARRAYS], above


def corner_kernel(ga_ref, gb_ref, ca_ref, cb_ref):
    nx = ga_ref.shape[1]
    rows = rows_along_y(ga_ref, gb_ref)
    even = is_even("bx")
    ca_ref[4 * UNITS:, :] = jnp.zeros((ca_ref.shape[0] - 4 * UNITS, ca_ref.shape[1]), F32)
    cb_ref[4 * UNITS:, :] = jnp.zeros((cb_ref.shape[0] - 4 * UNITS, cb_ref.shape[1]), F32)

    def face(out, near, deep, up):
        for k, row in enumerate(rows):
            for u, unit in enumerate(face_units([a[near:near + 1] for a in row], [a[deep:deep + 1] for a in row], 0, up)):
                out[4 * u + k:4 * u + k + 1, :] = unit

    @pl.when(even)
    def _():
        face(ca_ref, nx - 1, nx - 2, True)
        face(cb_ref, 0, 1, False)

    @pl.when(jnp.logical_not(even))
    def _():
        face(cb_ref, nx - 1, nx - 2, True)
        face(ca_ref, 0, 1, False)


def gather_planes(ref, y, back):
    shape = ref.shape[2:]
    lane, acc = lanes(shape), jnp.zeros(shape, F32)
    for i in range(ARRAYS):
        if i < PAIRS:
            acc = jnp.where(lane // 2 == i, pltpu.roll(ref[i, y], 2 * i + 2 * back, 1), acc)
        else:
            acc = jnp.where(lane == 9 + i, pltpu.roll(ref[i, y], 9 + i + back, 1), acc)
    return acc


def widen_kernel(rows, width, own_ref, ga_ref, gb_ref, owner_ref, group_ref, body_ref, acc_ref, place_ref, ids_ref):
    make_places(rows, width, owner_ref, group_ref, place_ref, ids_ref)
    ny = own_ref.shape[1]
    body_ref[:, 2:ny + 2] = own_ref[...]
    for y, row in zip((0, 1, ny + 2, ny + 3), rows_along_y(ga_ref, gb_ref)):
        for i in range(ARRAYS):
            body_ref[i, y] = row[i]
    back = jnp.where(lax.axis_index("gz") == 0, 1, 0)

    for y in range(ny + 4):
        acc_ref[y] = gather_planes(body_ref, y, back)


def extend_kernel(acc_ref, xa_ref, xb_ref, ca_ref, cb_ref, side_ref, zp_ref, all_ref):
    wy, nx, nz = acc_ref.shape
    ny, ws = wy - 4, side_ref.shape[2]
    wx = nx + ws
    x_even = is_even("bx")
    side_ref[...] = jnp.zeros(side_ref.shape, F32)
    lines = side_ref.reshape(ARRAYS * wy * ws, nz)
    for u in range(UNITS):
        i, near = (u, True) if u < ARRAYS else ((0, 6, 7, 8)[u - ARRAYS], False)
        lower, upper = sides("bx", x_even, xa_ref[u], xb_ref[u])
        low_corner, up_corner = sides("bx", x_even, ca_ref[4 * u:4 * u + 4, :], cb_ref[4 * u:4 * u + 4, :])
        for x, rows, corner in ((ws - 1 if near else ws - 2, lower, low_corner), (0 if near else 1, upper, up_corner)):
            if u == ARRAYS and rows is upper:
                continue
            start = i * wy * ws + x
            lines[pl.ds(start + 2 * ws, ny, stride=ws), :] = rows
            for k, y in enumerate((0, 1, ny + 2, ny + 3)):
                lines[start + y * ws:start + y * ws + 1, :] = corner[k:k + 1]
    back = jnp.where(lax.axis_index("gz") == 0, 1, 0)

    for y in range(wy):
        all_ref[y * wx:y * wx + nx, :] = acc_ref[y]
        all_ref[y * wx + nx:(y + 1) * wx, :] = gather_planes(side_ref, y, back)
    full = all_ref.shape[0]
    all_ref[wy * wx:, :] = jnp.zeros((full - wy * wx, nz), F32)
    zp_ref[...] = all_ref[...].T[:Z_UNITS]


def curl_of(dx, dy, dz):
    return dy[2] - dz[1], dz[0] - dx[2], dx[1] - dy[0]


def slab_planes(slab_ref, wx, by0, bx0):
    full = slab_ref.shape[2]
    lane = lanes((8, full))
    line = (lane * 683) >> 14
    column = lane - line * wx
    half = jnp.where((by0 & (line < 2)) | (bx0 & (column >= wx - 2)), 0.0, time_step)

    def plus(f):
        ahead = lambda a: jnp.where(column == wx - 1, pltpu.roll(a, wx - 1, 1), pltpu.roll(a, full - 1, 1)) - a
        return curl_of(
            (None, ahead(f[1]), ahead(f[2])),
            (pltpu.roll(f[0], full - wx, 1) - f[0], None, pltpu.roll(f[2], full - wx, 1) - f[2]),
            (pltpu.roll(f[0], 7, 0) - f[0], pltpu.roll(f[1], 7, 0) - f[1]),
        )

    def minus(f):
        behind = lambda a: a - jnp.where(column == 0, pltpu.roll(a, full - wx + 1, 1), pltpu.roll(a, 1, 1))
        return curl_of(
            (None, behind(f[1]), behind(f[2])),
            (f[0] - pltpu.roll(f[0], wx, 1), None, f[2] - pltpu.roll(f[2], wx, 1)),
            (f[0] - pltpu.roll(f[0], 1, 0), f[1] - pltpu.roll(f[1], 1, 0)),
        )

    e, h, s, b = ([slab_ref[3 * k + c] for c in range(3)] for k in range(4))
    code = slab_ref[12]
    ratio = jnp.abs(code)
    h1 = [a - half * d for a, d in zip(h, plus(e))]
    g1 = [half * d for d in plus(s)]
    e1 = [a + ratio * d for a, d in zip(b, minus(h1))]
    s1 = [jnp.where(code < 0, a * (1.0 - ratio), a) - ratio * d for a, d in zip(s, minus(g1))]
    h2 = [a - half * d for a, d in zip(h1, plus(e1))]
    g2 = [a + half * d for a, d in zip(g1, plus(s1))]
    return (e, e1, s, s1), (h1, h2, g1, g2)


class Borders:
    def __init__(self, col_ref, wx, nz):
        self.col_ref, self.wx, self.nz, self.lane = col_ref, wx, nz, lanes((wx, nz))

    def beyond(self, y, k):
        return self.col_ref[pl.ds(pl.multiple_of(y * self.wx, 8), self.wx), k * self.nz:(k + 1) * self.nz]

    def plus(self, get, y, p):
        f, g = [get(c, y) for c in range(3)], [get(c, y + 1) for c in (0, 2)]
        dz = [pltpu.roll(jnp.where(self.lane == 0, self.beyond(y, 2 * p + c), f[c]), self.nz - 1, 1) - f[c] for c in range(2)]
        dx = [None] + [pltpu.roll(f[c], self.wx - 1, 0) - f[c] for c in (1, 2)]
        return curl_of(dx, (g[0] - f[0], None, g[1] - f[2]), dz)

    def minus(self, get, y, p):
        f, g = [get(c, y) for c in range(3)], [get(c, y - 1) for c in (0, 2)]
        dz = [f[c] - pltpu.roll(jnp.where(self.lane == self.nz - 1, self.beyond(y, 2 * p + c), f[c]), 1, 1) for c in range(2)]
        dx = [None] + [f[c] - pltpu.roll(f[c], 1, 0) for c in (1, 2)]
        return curl_of(dx, (f[0] - g[0], None, f[2] - g[1]), dz)


def halves(wx, nz):
    by0, bx0 = lax.axis_index("by") == 0, lax.axis_index("bx") == 0
    column = lax.broadcasted_iota(jnp.int32, (wx, nz), 0)
    along = jnp.where(bx0 & (column >= wx - 2), 0.0, time_step)
    return lambda y: along * jnp.where(by0 & (y < 2), 0.0, 1.0)


def main_kernel(body_ref, side_ref, zo_ref, zg_ref, j1_ref, c_ref, w_ref, q_ref, place_ref, ids_ref, blocks_ref,
                e2_ref, a0_ref, send_ref,
                slab_ref, plane_ref, col_ref, h1_ref, e1_ref, h2_ref, g1_ref, s1_ref, g2_ref,
                d1_ref, back_ref, cell_ref, partial_ref):
    size = 2 * w_ref.shape[1] * w_ref.shape[2] // blocks_ref.shape[1] * (2 * KB)
    ny, nx, nz = w_ref.shape
    tile_rows = size // nx
    wy, wx = ny + 4, nx + side_ref.shape[2]
    by0, bx0 = lax.axis_index("by") == 0, lax.axis_index("bx") == 0
    gz0 = lax.axis_index("gz") == 0

    for i in range(ARRAYS):
        u, deep = (2 * i, 2) if i < PAIRS else (9 + i, 1)
        mine, other = zo_ref[u:u + deep, :], zg_ref[u:u + deep, :]
        slab_ref[i] = jnp.zeros(slab_ref.shape[1:], F32)
        slab_ref[i, 2 - deep:2, :] = jnp.where(gz0, mine, other)
        slab_ref[i, 2:2 + deep, :] = jnp.where(gz0, other, mine)
    upper, lower = slab_planes(slab_ref, wx, by0, bx0)
    plane_ref[...] = jnp.zeros(plane_ref.shape, F32)
    for p in range(4):
        for c in range(2):
            plane_ref[2 * p + c:2 * p + c + 1, :] = jnp.where(gz0, upper[p][c][2:3], lower[p][c][1:2])
    rest = plane_ref[0:8, :]
    for k in range(3):
        part = rest.astype(BF16).astype(F32)
        plane_ref[8 * k:8 * k + 8, :] = part
        rest = rest - part
    wide = 8 * nz
    row, place = lax.broadcasted_iota(jnp.int32, (128, wide), 0), lanes((128, wide))
    border = place % nz == jnp.where(gz0, 0, nz - 1)
    chosen = jnp.where(border & (row % 8 == place // nz) & (row < 24), 1.0, 0.0).astype(BF16)
    col_ref[...] = lax.dot_general(plane_ref[...].T.astype(BF16), chosen, (((1,), (0,)), ((), ())), preferred_element_type=F32)

    borders, half = Borders(col_ref, wx, nz), halves(wx, nz)

    def array(k):
        return lambda c, y: jnp.concatenate([body_ref[3 * k + c, y], side_ref[3 * k + c, y]], axis=0)

    def row_of(ref):
        return lambda c, y: ref[c, y]

    electric, magnetic, scaled, start = (array(k) for k in range(4))

    def first_magnetic(y):
        factor = half(y)
        for c, d in enumerate(borders.plus(electric, y, 0)):
            h1_ref[c, y] = magnetic(c, y) - factor * d
        for c, d in enumerate(borders.plus(scaled, y, 2)):
            g1_ref[c, y] = factor * d

    def first_electric(y):
        code = array(4)(0, y)
        ratio = jnp.abs(code)
        kept = jnp.where(code < 0, 1.0 - ratio, 1.0)
        for c, d in enumerate(borders.minus(row_of(h1_ref), y, 0)):
            d1_ref[c, y] = d[:nx]
            e1_ref[c, y] = start(c, y) + ratio * d
        for c, d in enumerate(borders.minus(row_of(g1_ref), y, 2)):
            back_ref[c, y] = d[:nx]
            s1_ref[c, y] = scaled(c, y) * kept - ratio * d

    def second_magnetic(y):
        factor = half(y)
        for c, d in enumerate(borders.plus(row_of(e1_ref), y, 1)):
            h2_ref[c, y] = h1_ref[c, y] - factor * d

    def second_electric(y):
        at = y - 2
        code = body_ref[12, y]
        ratio, silver = jnp.abs(code), code < 0
        eps = jnp.zeros((nx, nz), F32)
        for c, d in enumerate(borders.minus(row_of(h2_ref), y, 1)):
            e1, j1 = e1_ref[c, y, 0:nx, :], j1_ref[c, at]
            drive = d[:nx] - jnp.where(silver, drude_keep * j1 + drude_gain * e1, 0.0)
            final = e1 + ratio * drive
            if c == 2:
                final = final + (source_level * source_wave[1]) * q_ref[at]
            e2_ref[c, at] = final
            eps = eps + body_ref[6 + c, y] * drive + s1_ref[c, y, 0:nx, :] * (d1_ref[c, y] - j1)
        cell_ref[pl.ds(pl.multiple_of(at * nx, 8), nx), :] = w_ref[at] * eps

    def last_magnetic(y):
        factor = half(y)
        for c, d in enumerate(borders.plus(row_of(s1_ref), y, 3)):
            g2_ref[c, y] = g1_ref[c, y] + factor * d

    def last_electric(y):
        silver = body_ref[12, y] < 0
        for c, d in enumerate(borders.minus(row_of(g2_ref), y, 3)):
            lost = jnp.where(silver, drude_gain * ((1.0 + drude_keep) * body_ref[6 + c, y] + s1_ref[c, y, 0:nx, :]), 0.0)
            a0_ref[c, y - 2] = c_ref[c, y - 2] - back_ref[c, y] - d[:nx] - lost

    for y in range(wy - 1):
        first_magnetic(y)
    for y in range(1, wy - 1):
        first_electric(y)
    for y in range(1, wy - 2):
        second_magnetic(y)

    group = nx
    sub = lax.broadcasted_iota(jnp.int32, (group, tile_rows), 0)

    def project(n):
        parts = [cell_ref[pl.ds(n * 2 * group + k, group, stride=2), :] for k in range(2)]
        cells = jnp.concatenate(parts, axis=1).astype(BF16)
        prods = lax.dot_general(cells, blocks_ref[n * size:(n + 1) * size, :], (((1,), (1,)), ((), ())), preferred_element_type=F32)
        acc = jnp.zeros((group, tile_rows), F32)
        for i in range(group):
            acc = jnp.where(sub == i, prods[:, i * tile_rows:(i + 1) * tile_rows], acc)
        partial_ref[n * group:(n + 1) * group, :] = acc

    second_electric(2)
    second_electric(3)
    last_magnetic(1)
    for n in range(1, ny // 2):
        for y in (2 * n + 2, 2 * n + 3):
            second_electric(y)
        for y in (2 * n, 2 * n + 1):
            last_magnetic(y)
        for y in (2 * n, 2 * n + 1):
            last_electric(y)
        project(n - 1)
    for y in (ny, ny + 1):
        last_magnetic(y)
    for y in (ny, ny + 1):
        last_electric(y)
    project(ny // 2 - 1)

    partial = partial_ref[...]
    turned = pltpu.roll(partial, KB, 1)
    low_lanes = lanes(partial.shape) < KB
    low = [jnp.where(low_lanes, a, 0.0) for a in (partial, turned)]
    high = [jnp.where(low_lanes, 0.0, a) for a in (turned, partial)]
    rhs = jnp.concatenate(low + high, axis=0)
    most = rhs.astype(BF16)
    rhs = jnp.concatenate([most, (rhs - most.astype(F32)).astype(BF16)], axis=0)
    lhs = jnp.concatenate([place_ref[0], place_ref[1], place_ref[0], place_ref[1]], axis=1)
    send_ref[...] = lax.dot_general(lhs, rhs, (((1,), (0,)), ((), ())), preferred_element_type=F32)
    planes = ids_ref.shape[0]
    width = send_ref.shape[0] // planes
    for d in range(planes):
        send_ref[d * width + width - 1:(d + 1) * width, :] = ids_ref[d:d + 1, :]


def capacity_of(planes, blocks):
    return max(2, 2 * blocks // planes)


def rows_of(planes, blocks):
    return capacity_of(planes, blocks) // 2


def make_places(rows, width, owner_ref, group_ref, place_ref, ids_ref):
    blocks = owner_ref.shape[1]
    planes = ids_ref.shape[0]
    row, column = (lax.broadcasted_iota(jnp.int32, (blocks, blocks), k) for k in range(2))
    half = blocks // 2
    swap = jnp.where(row == jnp.where(column < half, 2 * column, 2 * (column - half) + 1), 1.0, 0.0).astype(BF16)

    def arranged(ref):
        wide = jnp.broadcast_to(ref[...].astype(F32), (8, blocks)).astype(BF16)
        return lax.dot_general(wide, swap, (((1,), (0,)), ((), ())), preferred_element_type=F32)[:1]

    owner, group = arranged(owner_ref), arranged(group_ref)
    plane = lax.broadcasted_iota(jnp.int32, (planes, blocks), 0).astype(F32)
    hits = jnp.where(plane == owner, 1.0, 0.0)
    earlier = jnp.where(row < column, 1.0, 0.0).astype(BF16)
    before = lax.dot_general(hits.astype(BF16), earlier, (((1,), (0,)), ((), ())), preferred_element_type=F32)
    rank = jnp.sum(before * hits, axis=0, keepdims=True)
    slots = place_ref.shape[1]
    slot = lax.broadcasted_iota(jnp.int32, (slots, blocks), 0).astype(F32)
    for k in range(2):
        inner = rank - float(k * rows)
        target = jnp.where((inner >= 0.0) & (inner < float(rows)), owner * float(width) + inner, -1.0)
        place_ref[k] = jnp.where(slot == target, 1.0, 0.0).astype(BF16)
    ranks = lax.broadcasted_iota(jnp.int32, (128, blocks), 0).astype(F32)
    ranked = jnp.where(ranks == rank, 1.0, 0.0).astype(BF16)
    named = (hits * (group + 1.0)).astype(BF16)
    ids_ref[...] = lax.dot_general(named, ranked, (((1,), (1,)), ((), ())), preferred_element_type=F32) - 1.0


def collect_kernel(planes, got_ref, coef_ref, ids_ref):
    total, line = got_ref.shape
    width = total // planes
    rows = width - 1
    ids_ref[...] = jnp.zeros(ids_ref.shape, F32)
    for d in range(planes):
        ids_ref[d:d + 1, :] = got_ref[d * width + rows:(d + 1) * width, :] + 1.0
    shape = (total, line)
    index = lax.broadcasted_iota(jnp.int32, shape, 0)
    source = jnp.zeros(shape, jnp.int32)
    for d in range(1, planes):
        source = source + jnp.where(index >= d * width, 1, 0)
    place, lane = index - source * width, lanes(shape)
    spread = jnp.where(source == lane, 1.0, 0.0).astype(BF16)
    ids = lax.dot_general(spread, ids_ref[...].astype(BF16), (((1,), (0,)), ((), ())), preferred_element_type=F32)
    values = got_ref[...].T
    high = values.astype(BF16)
    low = (values - high.astype(F32)).astype(BF16)
    parts = []
    for k in range(2):
        mine = jnp.sum(jnp.where(lane == place + k * rows, ids, 0.0), axis=1, keepdims=True)
        hits = jnp.where((mine == lane.astype(F32) + 1.0) & (place < rows), 1.0, 0.0).astype(BF16)
        dots = [lax.dot_general(part, hits, (((1,), (0,)), ((), ())), preferred_element_type=F32) for part in (high, low)]
        parts.append((dots[0] + dots[1])[k * KB:(k + 1) * KB])
    coef_ref[...] = parts[0] + parts[1]


def call(kernel, outs, ins, scratch=(), places=None, leave=0, limit=16, cost=None):
    spaces = places or [pltpu.VMEM] * len(ins)
    keep = lambda a, space: pltpu.with_memory_space_constraint(a, space) if space is pltpu.VMEM else a
    return pl.pallas_call(
        kernel,
        out_shape=[jax.ShapeDtypeStruct(*o) if i < leave else pltpu.VMEM(*o) for i, o in enumerate(outs)],
        in_specs=[pl.BlockSpec(memory_space=pltpu.VMEM if space is None else space) for space in spaces],
        out_specs=[pl.BlockSpec(memory_space=pltpu.VMEM) for _ in outs],
        scratch_shapes=list(scratch),
        compiler_params=pltpu.CompilerParams(vmem_limit_bytes=limit * 1024 * 1024),
        cost_estimate=cost,
    )(*[keep(a, space) for a, space in zip(ins, spaces)])


def swapped(first, second, axis):
    axes = ("bx", "by", "gz")
    sizes = [lax.axis_size(name) for name in axes]
    along = axes.index(axis)
    arrived = []
    for start, value in ((0, first), (1, second)):
        pairs = []
        for flat in range(sizes[0] * sizes[1] * sizes[2]):
            at = [flat // (sizes[1] * sizes[2]), flat // sizes[2] % sizes[1], flat % sizes[2]]
            other = at[along] + 1 if at[along] % 2 == start else at[along] - 1
            if 0 <= other < sizes[along]:
                at[along] = other
            else:
                at[2] = (at[2] + 1) % sizes[2]
            pairs.append((flat, (at[0] * sizes[1] + at[1]) * sizes[2] + at[2]))
        arrived.append(lax.ppermute(value, axes, pairs))
    return arrived


def local(electric_start, magnetic_start, current_start, cotangent, level_set, material, source_cell, basis,
          block_owner, block_group):
    ny, nx, nz = material.shape
    wy, wx = ny + 4, nx + 8
    field, scalar = ((3, ny, nx, nz), F32), ((ny, nx, nz), F32)
    blocks = basis.shape[0]
    planes = lax.axis_size("bx") * lax.axis_size("by")
    rows = rows_of(planes, blocks)
    width = rows + 1
    y_face, x_face, corner = ((UNITS, nx, nz), F32), ((UNITS, ny, nz), F32), ((-(-4 * UNITS // 8) * 8, nz), F32)
    names = ((1, blocks), jnp.int32)
    fa, fb, xa, xb, own, w, j1, q, weight, owner, group = call(
        prepare_kernel,
        [y_face, y_face, x_face, x_face, ((ARRAYS, ny, nx, nz), F32), scalar, field, scalar, field, names, names],
        [source_cell, electric_start, magnetic_start, current_start, cotangent, level_set, material,
         block_owner.reshape(1, blocks), block_group.reshape(1, blocks)],
        places=[pltpu.SMEM] + [None] * 8,
        limit=58,
    )
    ga, gb = swapped(fa, fb, "by")
    xa, xb = swapped(xa, xb, "bx")
    ca, cb = call(corner_kernel, [corner, corner], [ga, gb])
    ca, cb, owner, group = lax.optimization_barrier((ca, cb, owner, group))
    ca, cb = swapped(ca, cb, "bx")
    flat_basis = basis.reshape(blocks * KB, basis.shape[2])
    chunk = 2 * nx * nz // basis.shape[2] * (2 * KB)
    body, acc, place, ids = call(
        functools.partial(widen_kernel, rows, width),
        [((ARRAYS, wy, nx, nz), F32), ((wy, nx, nz), F32), ((2, planes * width, blocks), BF16), ((planes, 128), F32)],
        [own, ga, gb, owner, group],
        cost=pl.CostEstimate(flops=5_000_000_000, transcendentals=0, bytes_accessed=1000),
    )
    ca, cb, ids, acc = lax.optimization_barrier((ca, cb, ids, acc))
    full = -(-wy * wx // 128) * 128
    side, zp = call(
        extend_kernel,
        [((ARRAYS, wy, wx - nx, nz), F32), ((Z_UNITS, full), F32)],
        [acc, xa, xb, ca, cb],
        scratch=[pltpu.VMEM((full, nz), F32)],
    )
    zg = lax.ppermute(zp, "gz", [(0, 1), (1, 0)])
    wide, inner = ((3, wy, wx, nz), F32), ((3, wy, nx, nz), F32)
    electric, adjoint, send = call(
        main_kernel,
        [field, field, ((planes * width, 2 * KB), F32)],
        [body, side, zp, zg, j1, weight, w, q, place, ids, flat_basis],
        scratch=[
            pltpu.VMEM((ARRAYS, 8, full), F32),
            pltpu.VMEM((128, full), F32),
            pltpu.VMEM((full, 8 * nz), F32),
            *[pltpu.VMEM(*wide)] * 6,
            pltpu.VMEM(*inner), pltpu.VMEM(*inner),
            pltpu.VMEM((ny * nx, nz), F32),
            pltpu.VMEM((ny * nx // 2, 2 * KB), F32),
        ],
        limit=20,
    )
    send = send.reshape(planes * width, 1, 2 * KB)
    got = lax.all_to_all(send, ("bx", "by"), split_axis=0, concat_axis=0, tiled=True)
    (coef,) = call(
        functools.partial(collect_kernel, planes),
        [((KB, GRP_DEV), F32)],
        [got.reshape(planes * width, 2 * KB)],
        scratch=[pltpu.VMEM((128, 2 * KB), F32)],
        leave=1,
    )
    return electric, adjoint, coef


def solution(mesh):
    field = P(None, "by", "bx", "gz")
    scalar = P("by", "bx", "gz")
    flat = ("bx", "by", "gz")
    return jax.shard_map(
        local,
        mesh=mesh,
        in_specs=(field, field, field, field, scalar, scalar, P(flat), P(flat, None, None), P(flat, None), P(flat)),
        out_specs=(field, field, P(None, flat)),
        check_vma=False,
    )
```

```python
import functools

import jax
import jax.numpy as jnp
from jax import lax
from jax.experimental import pallas as pl
from jax.experimental.pallas import tpu as pltpu
from jax.sharding import PartitionSpec as P

KB = 64
GRP_DEV = 128

time_step = 0.5
drude_keep = 0.9
drude_gain = 1.0
metal_permit = 3.0
design_contrast = 5.0
source_level = 3.0
source_wave = (1.0, -0.6, 0.8, -0.4)

PAIRS, ARRAYS = 9, 13
UNITS = ARRAYS + 4
CORNER = [(0, u) for u in (1, 5, 6, 7, 8, 15)] + [(k, u) for k in (1, 2) for u in range(UNITS)] + [(3, u) for u in (6, 8, 14)]
CORNER_LINES = -(-len(CORNER) // 8) * 8
Z_UNITS = 24
F32 = jnp.float32
BF16 = jnp.bfloat16


def is_even(axis):
    return lax.rem(lax.axis_index(axis), 2) == 0


def lanes(shape):
    return lax.broadcasted_iota(jnp.int32, shape, len(shape) - 1)


def prepare_kernel(cells_ref, e_ref, h_ref, j_ref, c_ref, level_ref, mat_ref, owner_ref, group_ref,
                   fa_ref, fb_ref, xa_ref, xb_ref, own_ref, w_ref, j1_ref, q_ref, c_out_ref, owner_out_ref, group_out_ref):
    owner_out_ref[...] = owner_ref[...]
    group_out_ref[...] = group_ref[...]
    ny, nx, nz = mat_ref.shape
    flat = lax.broadcasted_iota(jnp.int32, (nx, nz), 0) * nz + lanes((nx, nz))

    def row(y, carry):
        mat = mat_ref[y]
        silver, design = mat == 2, mat == 1
        smooth = 1.0 / (1.0 + jnp.exp(-level_ref[y]))
        permit = jnp.where(silver, metal_permit, jnp.where(design, 1.0 + design_contrast * smooth, 1.0))
        ratio = time_step / permit
        own_ref[12, y] = jnp.where(silver, -ratio, ratio)
        w_ref[y] = jnp.where(design, (-design_contrast / time_step) * ratio * smooth * (1.0 - smooth), 0.0)
        count = jnp.zeros((nx, nz), F32)
        for i in range(cells_ref.shape[0]):
            count = count + jnp.where(flat + y * (nx * nz) == cells_ref[i], 1.0, 0.0)
        q_ref[y] = count
        for c in range(3):
            electric, weight = e_ref[c, y], c_ref[c, y]
            current = jnp.where(silver, drude_keep * j_ref[c, y] + drude_gain * electric, 0.0)
            j1_ref[c, y] = current
            start = electric - ratio * current
            if c == 2:
                start = start + (source_level * source_wave[0]) * count
            own_ref[c, y] = electric
            own_ref[3 + c, y] = h_ref[c, y]
            own_ref[6 + c, y] = ratio * weight
            own_ref[9 + c, y] = start
            c_out_ref[c, y] = weight
        return carry

    lax.fori_loop(0, ny, row, 0, unroll=8)

    def y_face(out, near, deep, up):
        layers = [[own_ref[i, y] for i in range(ARRAYS)] for y in (near, deep)]
        for u, unit in enumerate(face_units(*layers, 1, up)):
            out[u] = unit

    lines = own_ref.reshape(ARRAYS * ny * nx, nz)

    def x_face(out, near, deep, up):
        layers = [[lines[pl.ds(i * ny * nx + x, ny, stride=nx), :] for i in range(ARRAYS)] for x in (near, deep)]
        for u, unit in enumerate(face_units(*layers, 0, up)):
            out[u] = unit

    for face, even, a_ref, b_ref, n in ((y_face, is_even("by"), fa_ref, fb_ref, ny), (x_face, is_even("bx"), xa_ref, xb_ref, nx)):
        @pl.when(even)
        def _():
            face(a_ref, n - 1, n - 2, True)
            face(b_ref, 0, 1, False)

        @pl.when(jnp.logical_not(even))
        def _():
            face(b_ref, n - 1, n - 2, True)
            face(a_ref, 0, 1, False)


def face_units(near, deep, axis, up):
    first, second = (axis + 1) % 3, (axis + 2) % 3
    units = list(near)
    if up:
        ratio = jnp.abs(near[12])
        units[9 + first] = near[9 + first] + ratio * (deep[3 + second] + time_step * deep[first])
        units[9 + second] = near[9 + second] - ratio * (deep[3 + first] - time_step * deep[second])
    else:
        units[3 + first] = near[3 + first] + time_step * deep[second]
        units[3 + second] = near[3 + second] - time_step * deep[first]
    return units + [deep[axis], deep[6], deep[7], deep[8]]


def sides(axis, even, a, b):
    at, zero = lax.axis_index(axis), jnp.zeros(a.shape, F32)
    lower = jnp.where(at == 0, zero, jnp.where(even, b, a))
    upper = jnp.where(at == lax.axis_size(axis) - 1, zero, jnp.where(even, a, b))
    return lower, upper


def rows_along_y(ga_ref, gb_ref):
    even, zero = is_even("by"), jnp.zeros(ga_ref.shape[1:], F32)
    units = [sides("by", even, ga_ref[u], gb_ref[u]) for u in range(UNITS)]
    lower, upper = ([unit[k] for unit in units] for k in range(2))
    below = [zero, lower[13], zero] + [zero] * 3 + lower[14:] + [zero] * 4
    above = [zero] * 6 + upper[14:] + [zero] * 4
    return below, lower[:ARRAYS], upper[:ARRAYS], above


def corner_kernel(ga_ref, gb_ref, ca_ref, cb_ref):
    nx = ga_ref.shape[1]
    rows = rows_along_y(ga_ref, gb_ref)
    even = is_even("bx")
    for ref in (ca_ref, cb_ref):
        ref[len(CORNER):, :] = jnp.zeros((CORNER_LINES - len(CORNER), ref.shape[1]), F32)

    def face(out, near, deep, up):
        units = [face_units([a[near:near + 1] for a in row], [a[deep:deep + 1] for a in row], 0, up) for row in rows]
        for line, (k, u) in enumerate(CORNER):
            out[line:line + 1, :] = units[k][u]

    @pl.when(even)
    def _():
        face(ca_ref, nx - 1, nx - 2, True)
        face(cb_ref, 0, 1, False)

    @pl.when(jnp.logical_not(even))
    def _():
        face(cb_ref, nx - 1, nx - 2, True)
        face(ca_ref, 0, 1, False)


def gather_planes(ref, y, back):
    shape = ref.shape[2:]
    lane, acc = lanes(shape), jnp.zeros(shape, F32)
    for i in range(ARRAYS):
        if i < PAIRS:
            acc = jnp.where(lane // 2 == i, pltpu.roll(ref[i, y], 2 * i + 2 * back, 1), acc)
        else:
            acc = jnp.where(lane == 9 + i, pltpu.roll(ref[i, y], 9 + i + back, 1), acc)
    return acc


def widen_kernel(rows, width, own_ref, ga_ref, gb_ref, owner_ref, group_ref, body_ref, acc_ref, place_ref, ids_ref):
    make_places(rows, width, owner_ref, group_ref, place_ref, ids_ref)
    ny = own_ref.shape[1]
    body_ref[:, 2:ny + 2] = own_ref[...]
    for y, row in zip((0, 1, ny + 2, ny + 3), rows_along_y(ga_ref, gb_ref)):
        for i in range(ARRAYS):
            body_ref[i, y] = row[i]
    back = jnp.where(lax.axis_index("gz") == 0, 1, 0)

    for y in range(ny + 4):
        acc_ref[y] = gather_planes(body_ref, y, back)


def extend_kernel(acc_ref, xa_ref, xb_ref, ca_ref, cb_ref, side_ref, zp_ref, all_ref):
    wy, nx, nz = acc_ref.shape
    ny, ws = wy - 4, side_ref.shape[2]
    wx = nx + ws
    x_even = is_even("bx")
    side_ref[...] = jnp.zeros(side_ref.shape, F32)
    lines = side_ref.reshape(ARRAYS * wy * ws, nz)
    low_corner, up_corner = sides("bx", x_even, ca_ref[...], cb_ref[...])
    for u in range(UNITS):
        i, near = (u, True) if u < ARRAYS else ((0, 6, 7, 8)[u - ARRAYS], False)
        lower, upper = sides("bx", x_even, xa_ref[u], xb_ref[u])
        for x, rows, corner in ((ws - 1 if near else ws - 2, lower, low_corner), (0 if near else 1, upper, up_corner)):
            if u == ARRAYS and rows is upper:
                continue
            start = i * wy * ws + x
            lines[pl.ds(start + 2 * ws, ny, stride=ws), :] = rows
            for line, (k, unit) in enumerate(CORNER):
                if unit == u:
                    at = start + (0, 1, ny + 2, ny + 3)[k] * ws
                    lines[at:at + 1, :] = corner[line:line + 1]
    back = jnp.where(lax.axis_index("gz") == 0, 1, 0)

    for y in range(wy):
        all_ref[y * wx:y * wx + nx, :] = acc_ref[y]
        all_ref[y * wx + nx:(y + 1) * wx, :] = gather_planes(side_ref, y, back)
    full = all_ref.shape[0]
    all_ref[wy * wx:, :] = jnp.zeros((full - wy * wx, nz), F32)
    zp_ref[...] = all_ref[...].T[:Z_UNITS]


def curl_of(dx, dy, dz):
    return dy[2] - dz[1], dz[0] - dx[2], dx[1] - dy[0]


def slab_planes(slab_ref, wx, by0, bx0):
    full = slab_ref.shape[2]
    lane = lanes((8, full))
    line = (lane * 683) >> 14
    column = lane - line * wx
    half = jnp.where((by0 & (line < 2)) | (bx0 & (column >= wx - 2)), 0.0, time_step)

    def plus(f):
        ahead = lambda a: jnp.where(column == wx - 1, pltpu.roll(a, wx - 1, 1), pltpu.roll(a, full - 1, 1)) - a
        return curl_of(
            (None, ahead(f[1]), ahead(f[2])),
            (pltpu.roll(f[0], full - wx, 1) - f[0], None, pltpu.roll(f[2], full - wx, 1) - f[2]),
            (pltpu.roll(f[0], 7, 0) - f[0], pltpu.roll(f[1], 7, 0) - f[1]),
        )

    def minus(f):
        behind = lambda a: a - jnp.where(column == 0, pltpu.roll(a, full - wx + 1, 1), pltpu.roll(a, 1, 1))
        return curl_of(
            (None, behind(f[1]), behind(f[2])),
            (f[0] - pltpu.roll(f[0], wx, 1), None, f[2] - pltpu.roll(f[2], wx, 1)),
            (f[0] - pltpu.roll(f[0], 1, 0), f[1] - pltpu.roll(f[1], 1, 0)),
        )

    e, h, s, b = ([slab_ref[3 * k + c] for c in range(3)] for k in range(4))
    code = slab_ref[12]
    ratio = jnp.abs(code)
    h1 = [a - half * d for a, d in zip(h, plus(e))]
    g1 = [half * d for d in plus(s)]
    e1 = [a + ratio * d for a, d in zip(b, minus(h1))]
    s1 = [jnp.where(code < 0, a * (1.0 - ratio), a) - ratio * d for a, d in zip(s, minus(g1))]
    h2 = [a - half * d for a, d in zip(h1, plus(e1))]
    g2 = [a + half * d for a, d in zip(g1, plus(s1))]
    return (e, e1, s, s1), (h1, h2, g1, g2)


class Borders:
    def __init__(self, col_ref, wx, nz):
        self.col_ref, self.wx, self.nz, self.lane = col_ref, wx, nz, lanes((wx, nz))

    def beyond(self, y, k):
        return self.col_ref[pl.ds(pl.multiple_of(y * self.wx, 8), self.wx), k * self.nz:(k + 1) * self.nz]

    def plus(self, get, y, p):
        f, g = [get(c, y) for c in range(3)], [get(c, y + 1) for c in (0, 2)]
        dz = [pltpu.roll(jnp.where(self.lane == 0, self.beyond(y, 2 * p + c), f[c]), self.nz - 1, 1) - f[c] for c in range(2)]
        dx = [None] + [pltpu.roll(f[c], self.wx - 1, 0) - f[c] for c in (1, 2)]
        return curl_of(dx, (g[0] - f[0], None, g[1] - f[2]), dz)

    def minus(self, get, y, p):
        f, g = [get(c, y) for c in range(3)], [get(c, y - 1) for c in (0, 2)]
        dz = [f[c] - pltpu.roll(jnp.where(self.lane == self.nz - 1, self.beyond(y, 2 * p + c), f[c]), 1, 1) for c in range(2)]
        dx = [None] + [f[c] - pltpu.roll(f[c], 1, 0) for c in (1, 2)]
        return curl_of(dx, (f[0] - g[0], None, f[2] - g[1]), dz)


def halves(wx, nz):
    by0, bx0 = lax.axis_index("by") == 0, lax.axis_index("bx") == 0
    column = lax.broadcasted_iota(jnp.int32, (wx, nz), 0)
    along = jnp.where(bx0 & (column >= wx - 2), 0.0, time_step)
    return lambda y: along * jnp.where(by0 & (y < 2), 0.0, 1.0)


def main_kernel(body_ref, side_ref, zo_ref, zg_ref, j1_ref, c_ref, w_ref, q_ref, place_ref, ids_ref, blocks_ref,
                e2_ref, a0_ref, send_ref,
                slab_ref, plane_ref, col_ref, h1_ref, e1_ref, h2_ref, g1_ref, s1_ref, g2_ref,
                d1_ref, back_ref, cell_ref, partial_ref):
    size = 2 * w_ref.shape[1] * w_ref.shape[2] // blocks_ref.shape[1] * (2 * KB)
    ny, nx, nz = w_ref.shape
    tile_rows = size // nx
    wy, wx = ny + 4, nx + side_ref.shape[2]
    by0, bx0 = lax.axis_index("by") == 0, lax.axis_index("bx") == 0
    gz0 = lax.axis_index("gz") == 0

    for i in range(ARRAYS):
        u, deep = (2 * i, 2) if i < PAIRS else (9 + i, 1)
        mine, other = zo_ref[u:u + deep, :], zg_ref[u:u + deep, :]
        slab_ref[i] = jnp.zeros(slab_ref.shape[1:], F32)
        slab_ref[i, 2 - deep:2, :] = jnp.where(gz0, mine, other)
        slab_ref[i, 2:2 + deep, :] = jnp.where(gz0, other, mine)
    upper, lower = slab_planes(slab_ref, wx, by0, bx0)
    plane_ref[...] = jnp.zeros(plane_ref.shape, F32)
    for p in range(4):
        for c in range(2):
            plane_ref[2 * p + c:2 * p + c + 1, :] = jnp.where(gz0, upper[p][c][2:3], lower[p][c][1:2])
    rest = plane_ref[0:8, :]
    for k in range(3):
        part = rest.astype(BF16).astype(F32)
        plane_ref[8 * k:8 * k + 8, :] = part
        rest = rest - part
    wide = 8 * nz
    row, place = lax.broadcasted_iota(jnp.int32, (128, wide), 0), lanes((128, wide))
    border = place % nz == jnp.where(gz0, 0, nz - 1)
    chosen = jnp.where(border & (row % 8 == place // nz) & (row < 24), 1.0, 0.0).astype(BF16)
    col_ref[...] = lax.dot_general(plane_ref[...].T.astype(BF16), chosen, (((1,), (0,)), ((), ())), preferred_element_type=F32)

    borders, half = Borders(col_ref, wx, nz), halves(wx, nz)

    def array(k):
        return lambda c, y: jnp.concatenate([body_ref[3 * k + c, y], side_ref[3 * k + c, y]], axis=0)

    def row_of(ref):
        return lambda c, y: ref[c, y]

    electric, magnetic, scaled, start = (array(k) for k in range(4))

    def first_magnetic(y):
        factor = half(y)
        for c, d in enumerate(borders.plus(electric, y, 0)):
            h1_ref[c, y] = magnetic(c, y) - factor * d
        for c, d in enumerate(borders.plus(scaled, y, 2)):
            g1_ref[c, y] = factor * d

    def first_electric(y):
        code = array(4)(0, y)
        ratio = jnp.abs(code)
        kept = jnp.where(code < 0, 1.0 - ratio, 1.0)
        for c, d in enumerate(borders.minus(row_of(h1_ref), y, 0)):
            d1_ref[c, y] = d[:nx]
            e1_ref[c, y] = start(c, y) + ratio * d
        for c, d in enumerate(borders.minus(row_of(g1_ref), y, 2)):
            back_ref[c, y] = d[:nx]
            s1_ref[c, y] = scaled(c, y) * kept - ratio * d

    def second_magnetic(y):
        factor = half(y)
        for c, d in enumerate(borders.plus(row_of(e1_ref), y, 1)):
            h2_ref[c, y] = h1_ref[c, y] - factor * d

    def second_electric(y):
        at = y - 2
        code = body_ref[12, y]
        ratio, silver = jnp.abs(code), code < 0
        eps = jnp.zeros((nx, nz), F32)
        for c, d in enumerate(borders.minus(row_of(h2_ref), y, 1)):
            e1, j1 = e1_ref[c, y, 0:nx, :], j1_ref[c, at]
            drive = d[:nx] - jnp.where(silver, drude_keep * j1 + drude_gain * e1, 0.0)
            final = e1 + ratio * drive
            if c == 2:
                final = final + (source_level * source_wave[1]) * q_ref[at]
            e2_ref[c, at] = final
            eps = eps + body_ref[6 + c, y] * drive + s1_ref[c, y, 0:nx, :] * (d1_ref[c, y] - j1)
        cell_ref[pl.ds(pl.multiple_of(at * nx, 8), nx), :] = w_ref[at] * eps

    def last_magnetic(y):
        factor = half(y)
        for c, d in enumerate(borders.plus(row_of(s1_ref), y, 3)):
            g2_ref[c, y] = g1_ref[c, y] + factor * d

    def last_electric(y):
        silver = body_ref[12, y] < 0
        for c, d in enumerate(borders.minus(row_of(g2_ref), y, 3)):
            lost = jnp.where(silver, drude_gain * ((1.0 + drude_keep) * body_ref[6 + c, y] + s1_ref[c, y, 0:nx, :]), 0.0)
            a0_ref[c, y - 2] = c_ref[c, y - 2] - back_ref[c, y] - d[:nx] - lost

    for y in range(wy - 1):
        first_magnetic(y)
    for y in range(1, wy - 1):
        first_electric(y)
    for y in range(1, wy - 2):
        second_magnetic(y)

    group = nx
    sub = lax.broadcasted_iota(jnp.int32, (group, tile_rows), 0)

    def project(n):
        parts = [cell_ref[pl.ds(n * 2 * group + k, group, stride=2), :] for k in range(2)]
        cells = jnp.concatenate(parts, axis=1).astype(BF16)
        prods = lax.dot_general(cells, blocks_ref[n * size:(n + 1) * size, :], (((1,), (1,)), ((), ())), preferred_element_type=F32)
        acc = jnp.zeros((group, tile_rows), F32)
        for i in range(group):
            acc = jnp.where(sub == i, prods[:, i * tile_rows:(i + 1) * tile_rows], acc)
        partial_ref[n * group:(n + 1) * group, :] = acc

    second_electric(2)
    second_electric(3)
    last_magnetic(1)
    for n in range(1, ny // 2):
        for y in (2 * n + 2, 2 * n + 3):
            second_electric(y)
        for y in (2 * n, 2 * n + 1):
            last_magnetic(y)
        for y in (2 * n, 2 * n + 1):
            last_electric(y)
        project(n - 1)
    for y in (ny, ny + 1):
        last_magnetic(y)
    for y in (ny, ny + 1):
        last_electric(y)
    project(ny // 2 - 1)

    partial = partial_ref[...]
    turned = pltpu.roll(partial, KB, 1)
    low_lanes = lanes(partial.shape) < KB
    low = [jnp.where(low_lanes, a, 0.0) for a in (partial, turned)]
    high = [jnp.where(low_lanes, 0.0, a) for a in (turned, partial)]
    rhs = jnp.concatenate(low + high, axis=0)
    most = rhs.astype(BF16)
    rhs = jnp.concatenate([most, (rhs - most.astype(F32)).astype(BF16)], axis=0)
    lhs = jnp.concatenate([place_ref[0], place_ref[1], place_ref[0], place_ref[1]], axis=1)
    send_ref[...] = lax.dot_general(lhs, rhs, (((1,), (0,)), ((), ())), preferred_element_type=F32)
    planes = ids_ref.shape[0]
    width = send_ref.shape[0] // planes
    for d in range(planes):
        send_ref[d * width + width - 1:(d + 1) * width, :] = ids_ref[d:d + 1, :]


def capacity_of(planes, blocks):
    return max(2, 2 * blocks // planes)


def rows_of(planes, blocks):
    return capacity_of(planes, blocks) // 2


def make_places(rows, width, owner_ref, group_ref, place_ref, ids_ref):
    blocks = owner_ref.shape[1]
    planes = ids_ref.shape[0]
    row, column = (lax.broadcasted_iota(jnp.int32, (blocks, blocks), k) for k in range(2))
    half = blocks // 2
    swap = jnp.where(row == jnp.where(column < half, 2 * column, 2 * (column - half) + 1), 1.0, 0.0).astype(BF16)

    def arranged(ref):
        wide = jnp.broadcast_to(ref[...].astype(F32), (8, blocks)).astype(BF16)
        return lax.dot_general(wide, swap, (((1,), (0,)), ((), ())), preferred_element_type=F32)[:1]

    owner, group = arranged(owner_ref), arranged(group_ref)
    plane = lax.broadcasted_iota(jnp.int32, (planes, blocks), 0).astype(F32)
    hits = jnp.where(plane == owner, 1.0, 0.0)
    earlier = jnp.where(row < column, 1.0, 0.0).astype(BF16)
    before = lax.dot_general(hits.astype(BF16), earlier, (((1,), (0,)), ((), ())), preferred_element_type=F32)
    rank = jnp.sum(before * hits, axis=0, keepdims=True)
    slots = place_ref.shape[1]
    slot = lax.broadcasted_iota(jnp.int32, (slots, blocks), 0).astype(F32)
    for k in range(2):
        inner = rank - float(k * rows)
        target = jnp.where((inner >= 0.0) & (inner < float(rows)), owner * float(width) + inner, -1.0)
        place_ref[k] = jnp.where(slot == target, 1.0, 0.0).astype(BF16)
    ranks = lax.broadcasted_iota(jnp.int32, (128, blocks), 0).astype(F32)
    ranked = jnp.where(ranks == rank, 1.0, 0.0).astype(BF16)
    named = (hits * (group + 1.0)).astype(BF16)
    ids_ref[...] = lax.dot_general(named, ranked, (((1,), (1,)), ((), ())), preferred_element_type=F32) - 1.0


def collect_kernel(planes, got_ref, coef_ref, ids_ref):
    total, line = got_ref.shape
    width = total // planes
    rows = width - 1
    ids_ref[...] = jnp.zeros(ids_ref.shape, F32)
    for d in range(planes):
        ids_ref[d:d + 1, :] = got_ref[d * width + rows:(d + 1) * width, :] + 1.0
    shape = (total, line)
    index = lax.broadcasted_iota(jnp.int32, shape, 0)
    source = jnp.zeros(shape, jnp.int32)
    for d in range(1, planes):
        source = source + jnp.where(index >= d * width, 1, 0)
    place, lane = index - source * width, lanes(shape)
    spread = jnp.where(source == lane, 1.0, 0.0).astype(BF16)
    ids = lax.dot_general(spread, ids_ref[...].astype(BF16), (((1,), (0,)), ((), ())), preferred_element_type=F32)
    values = got_ref[...].T
    high = values.astype(BF16)
    low = (values - high.astype(F32)).astype(BF16)
    parts = []
    for k in range(2):
        mine = jnp.sum(jnp.where(lane == place + k * rows, ids, 0.0), axis=1, keepdims=True)
        hits = jnp.where((mine == lane.astype(F32) + 1.0) & (place < rows), 1.0, 0.0).astype(BF16)
        dots = [lax.dot_general(part, hits, (((1,), (0,)), ((), ())), preferred_element_type=F32) for part in (high, low)]
        parts.append((dots[0] + dots[1])[k * KB:(k + 1) * KB])
    coef_ref[...] = parts[0] + parts[1]


def call(kernel, outs, ins, scratch=(), places=None, leave=0, limit=16, cost=None):
    spaces = places or [pltpu.VMEM] * len(ins)
    keep = lambda a, space: pltpu.with_memory_space_constraint(a, space) if space is pltpu.VMEM else a
    return pl.pallas_call(
        kernel,
        out_shape=[jax.ShapeDtypeStruct(*o) if i < leave else pltpu.VMEM(*o) for i, o in enumerate(outs)],
        in_specs=[pl.BlockSpec(memory_space=pltpu.VMEM if space is None else space) for space in spaces],
        out_specs=[pl.BlockSpec(memory_space=pltpu.VMEM) for _ in outs],
        scratch_shapes=list(scratch),
        compiler_params=pltpu.CompilerParams(vmem_limit_bytes=limit * 1024 * 1024),
        cost_estimate=cost,
    )(*[keep(a, space) for a, space in zip(ins, spaces)])


def swapped(first, second, axis):
    axes = ("bx", "by", "gz")
    sizes = [lax.axis_size(name) for name in axes]
    along = axes.index(axis)
    arrived = []
    for start, value in ((0, first), (1, second)):
        pairs = []
        for flat in range(sizes[0] * sizes[1] * sizes[2]):
            at = [flat // (sizes[1] * sizes[2]), flat // sizes[2] % sizes[1], flat % sizes[2]]
            other = at[along] + 1 if at[along] % 2 == start else at[along] - 1
            if 0 <= other < sizes[along]:
                at[along] = other
            else:
                at[2] = (at[2] + 1) % sizes[2]
            pairs.append((flat, (at[0] * sizes[1] + at[1]) * sizes[2] + at[2]))
        arrived.append(lax.ppermute(value, axes, pairs))
    return arrived


def local(electric_start, magnetic_start, current_start, cotangent, level_set, material, source_cell, basis,
          block_owner, block_group):
    ny, nx, nz = material.shape
    wy, wx = ny + 4, nx + 8
    field, scalar = ((3, ny, nx, nz), F32), ((ny, nx, nz), F32)
    blocks = basis.shape[0]
    planes = lax.axis_size("bx") * lax.axis_size("by")
    rows = rows_of(planes, blocks)
    width = rows + 1
    y_face, x_face, corner = ((UNITS, nx, nz), F32), ((UNITS, ny, nz), F32), ((CORNER_LINES, nz), F32)
    names = ((1, blocks), jnp.int32)
    fa, fb, xa, xb, own, w, j1, q, weight, owner, group = call(
        prepare_kernel,
        [y_face, y_face, x_face, x_face, ((ARRAYS, ny, nx, nz), F32), scalar, field, scalar, field, names, names],
        [source_cell, electric_start, magnetic_start, current_start, cotangent, level_set, material,
         block_owner.reshape(1, blocks), block_group.reshape(1, blocks)],
        places=[pltpu.SMEM] + [None] * 8,
        limit=58,
    )
    ga, gb = swapped(fa, fb, "by")
    xa, xb = swapped(xa, xb, "bx")
    ca, cb = call(corner_kernel, [corner, corner], [ga, gb])
    ca, cb, owner, group = lax.optimization_barrier((ca, cb, owner, group))
    ca, cb = swapped(ca, cb, "bx")
    flat_basis = basis.reshape(blocks * KB, basis.shape[2])
    chunk = 2 * nx * nz // basis.shape[2] * (2 * KB)
    body, acc, place, ids = call(
        functools.partial(widen_kernel, rows, width),
        [((ARRAYS, wy, nx, nz), F32), ((wy, nx, nz), F32), ((2, planes * width, blocks), BF16), ((planes, 128), F32)],
        [own, ga, gb, owner, group],
        cost=pl.CostEstimate(flops=5_000_000_000, transcendentals=0, bytes_accessed=1000),
    )
    ca, cb, ids, acc = lax.optimization_barrier((ca, cb, ids, acc))
    full = -(-wy * wx // 128) * 128
    side, zp = call(
        extend_kernel,
        [((ARRAYS, wy, wx - nx, nz), F32), ((Z_UNITS, full), F32)],
        [acc, xa, xb, ca, cb],
        scratch=[pltpu.VMEM((full, nz), F32)],
    )
    zg = lax.ppermute(zp, "gz", [(0, 1), (1, 0)])
    wide, inner = ((3, wy, wx, nz), F32), ((3, wy, nx, nz), F32)
    electric, adjoint, send = call(
        main_kernel,
        [field, field, ((planes * width, 2 * KB), F32)],
        [body, side, zp, zg, j1, weight, w, q, place, ids, flat_basis],
        scratch=[
            pltpu.VMEM((ARRAYS, 8, full), F32),
            pltpu.VMEM((128, full), F32),
            pltpu.VMEM((full, 8 * nz), F32),
            *[pltpu.VMEM(*wide)] * 6,
            pltpu.VMEM(*inner), pltpu.VMEM(*inner),
            pltpu.VMEM((ny * nx, nz), F32),
            pltpu.VMEM((ny * nx // 2, 2 * KB), F32),
        ],
        limit=20,
    )
    send = send.reshape(planes * width, 1, 2 * KB)
    got = lax.all_to_all(send, ("bx", "by"), split_axis=0, concat_axis=0, tiled=True)
    (coef,) = call(
        functools.partial(collect_kernel, planes),
        [((KB, GRP_DEV), F32)],
        [got.reshape(planes * width, 2 * KB)],
        scratch=[pltpu.VMEM((128, 2 * KB), F32)],
        leave=1,
    )
    return electric, adjoint, coef


def solution(mesh):
    field = P(None, "by", "bx", "gz")
    scalar = P("by", "bx", "gz")
    flat = ("bx", "by", "gz")
    return jax.shard_map(
        local,
        mesh=mesh,
        in_specs=(field, field, field, field, scalar, scalar, P(flat), P(flat, None, None), P(flat, None), P(flat)),
        out_specs=(field, field, P(None, flat)),
        check_vma=False,
    )
```

```python
import functools

import jax
import jax.numpy as jnp
from jax import lax
from jax.experimental import pallas as pl
from jax.experimental.pallas import tpu as pltpu
from jax.sharding import PartitionSpec as P

KB = 64
GRP_DEV = 128

time_step = 0.5
drude_keep = 0.9
drude_gain = 1.0
metal_permit = 3.0
design_contrast = 5.0
source_level = 3.0
source_wave = (1.0, -0.6, 0.8, -0.4)

PAIRS, ARRAYS = 9, 13
UNITS = ARRAYS + 4
CORNER = [(0, u) for u in (1, 5, 6, 7, 8, 15)] + [(k, u) for k in (1, 2) for u in range(UNITS)] + [(3, u) for u in (6, 8, 14)]
CORNER_LINES = -(-len(CORNER) // 8) * 8
Z_UNITS = 24
F32 = jnp.float32
BF16 = jnp.bfloat16


def is_even(axis):
    return lax.rem(lax.axis_index(axis), 2) == 0


def lanes(shape):
    return lax.broadcasted_iota(jnp.int32, shape, len(shape) - 1)


def prepare_kernel(cells_ref, e_ref, h_ref, j_ref, c_ref, level_ref, mat_ref, owner_ref, group_ref,
                   fa_ref, fb_ref, xa_ref, xb_ref, own_ref, w_ref, j1_ref, q_ref, c_out_ref, owner_out_ref, group_out_ref):
    owner_out_ref[...] = owner_ref[...]
    group_out_ref[...] = group_ref[...]
    ny, nx, nz = mat_ref.shape
    flat = lax.broadcasted_iota(jnp.int32, (nx, nz), 0) * nz + lanes((nx, nz))

    def row(y, carry):
        mat = mat_ref[y]
        silver, design = mat == 2, mat == 1
        smooth = 1.0 / (1.0 + jnp.exp(-level_ref[y]))
        permit = jnp.where(silver, metal_permit, jnp.where(design, 1.0 + design_contrast * smooth, 1.0))
        ratio = time_step / permit
        own_ref[12, y] = jnp.where(silver, -ratio, ratio)
        w_ref[y] = jnp.where(design, (-design_contrast / time_step) * ratio * smooth * (1.0 - smooth), 0.0)
        count = jnp.zeros((nx, nz), F32)
        for i in range(cells_ref.shape[0]):
            count = count + jnp.where(flat + y * (nx * nz) == cells_ref[i], 1.0, 0.0)
        q_ref[y] = count
        for c in range(3):
            electric, weight = e_ref[c, y], c_ref[c, y]
            current = jnp.where(silver, drude_keep * j_ref[c, y] + drude_gain * electric, 0.0)
            j1_ref[c, y] = current
            start = electric - ratio * current
            if c == 2:
                start = start + (source_level * source_wave[0]) * count
            own_ref[c, y] = electric
            own_ref[3 + c, y] = h_ref[c, y]
            own_ref[6 + c, y] = ratio * weight
            own_ref[9 + c, y] = start
            c_out_ref[c, y] = weight
        return carry

    lax.fori_loop(0, ny, row, 0, unroll=8)

    def y_face(out, near, deep, up):
        layers = [[own_ref[i, y] for i in range(ARRAYS)] for y in (near, deep)]
        for u, unit in enumerate(face_units(*layers, 1, up)):
            out[u] = unit

    lines = own_ref.reshape(ARRAYS * ny * nx, nz)

    def x_face(out, near, deep, up):
        layers = [[lines[pl.ds(i * ny * nx + x, ny, stride=nx), :] for i in range(ARRAYS)] for x in (near, deep)]
        for u, unit in enumerate(face_units(*layers, 0, up)):
            out[u] = unit

    for face, even, a_ref, b_ref, n in ((y_face, is_even("by"), fa_ref, fb_ref, ny), (x_face, is_even("bx"), xa_ref, xb_ref, nx)):
        @pl.when(even)
        def _():
            face(a_ref, n - 1, n - 2, True)
            face(b_ref, 0, 1, False)

        @pl.when(jnp.logical_not(even))
        def _():
            face(b_ref, n - 1, n - 2, True)
            face(a_ref, 0, 1, False)


def face_units(near, deep, axis, up):
    first, second = (axis + 1) % 3, (axis + 2) % 3
    units = list(near)
    if up:
        ratio = jnp.abs(near[12])
        units[9 + first] = near[9 + first] + ratio * (deep[3 + second] + time_step * deep[first])
        units[9 + second] = near[9 + second] - ratio * (deep[3 + first] - time_step * deep[second])
    else:
        units[3 + first] = near[3 + first] + time_step * deep[second]
        units[3 + second] = near[3 + second] - time_step * deep[first]
    return units + [deep[axis], deep[6], deep[7], deep[8]]


def sides(axis, even, a, b):
    at, zero = lax.axis_index(axis), jnp.zeros(a.shape, F32)
    lower = jnp.where(at == 0, zero, jnp.where(even, b, a))
    upper = jnp.where(at == lax.axis_size(axis) - 1, zero, jnp.where(even, a, b))
    return lower, upper


def rows_along_y(ga_ref, gb_ref):
    even, zero = is_even("by"), jnp.zeros(ga_ref.shape[1:], F32)
    units = [sides("by", even, ga_ref[u], gb_ref[u]) for u in range(UNITS)]
    lower, upper = ([unit[k] for unit in units] for k in range(2))
    below = [zero, lower[13], zero] + [zero] * 3 + lower[14:] + [zero] * 4
    above = [zero] * 6 + upper[14:] + [zero] * 4
    return below, lower[:ARRAYS], upper[:ARRAYS], above


def corner_kernel(gb_ref, ga_ref, cb_ref, ca_ref):
    nx = ga_ref.shape[1]
    rows = rows_along_y(ga_ref, gb_ref)
    even = is_even("bx")
    for ref in (ca_ref, cb_ref):
        ref[len(CORNER):, :] = jnp.zeros((CORNER_LINES - len(CORNER), ref.shape[1]), F32)

    def face(out, near, deep, up):
        units = [face_units([a[near:near + 1] for a in row], [a[deep:deep + 1] for a in row], 0, up) for row in rows]
        for line, (k, u) in enumerate(CORNER):
            out[line:line + 1, :] = units[k][u]

    @pl.when(even)
    def _():
        face(ca_ref, nx - 1, nx - 2, True)
        face(cb_ref, 0, 1, False)

    @pl.when(jnp.logical_not(even))
    def _():
        face(cb_ref, nx - 1, nx - 2, True)
        face(ca_ref, 0, 1, False)


def gather_planes(ref, y, back):
    shape = ref.shape[2:]
    lane, acc = lanes(shape), jnp.zeros(shape, F32)
    for i in range(ARRAYS):
        if i < PAIRS:
            acc = jnp.where(lane // 2 == i, pltpu.roll(ref[i, y], 2 * i + 2 * back, 1), acc)
        else:
            acc = jnp.where(lane == 9 + i, pltpu.roll(ref[i, y], 9 + i + back, 1), acc)
    return acc


def widen_kernel(rows, width, own_ref, gb_ref, ga_ref, owner_ref, group_ref, body_ref, acc_ref, place_ref, ids_ref):
    make_places(rows, width, owner_ref, group_ref, place_ref, ids_ref)
    ny = own_ref.shape[1]
    body_ref[:, 2:ny + 2] = own_ref[...]
    for y, row in zip((0, 1, ny + 2, ny + 3), rows_along_y(ga_ref, gb_ref)):
        for i in range(ARRAYS):
            body_ref[i, y] = row[i]
    back = jnp.where(lax.axis_index("gz") == 0, 1, 0)

    for y in range(ny + 4):
        acc_ref[y] = gather_planes(body_ref, y, back)


def extend_kernel(acc_ref, xb_ref, xa_ref, cb_ref, ca_ref, side_ref, zp_ref, all_ref):
    wy, nx, nz = acc_ref.shape
    ny, ws = wy - 4, side_ref.shape[2]
    wx = nx + ws
    x_even = is_even("bx")
    side_ref[...] = jnp.zeros(side_ref.shape, F32)
    lines = side_ref.reshape(ARRAYS * wy * ws, nz)
    low_corner, up_corner = sides("bx", x_even, ca_ref[...], cb_ref[...])
    for u in range(UNITS):
        i, near = (u, True) if u < ARRAYS else ((0, 6, 7, 8)[u - ARRAYS], False)
        lower, upper = sides("bx", x_even, xa_ref[u], xb_ref[u])
        for x, rows, corner in ((ws - 1 if near else ws - 2, lower, low_corner), (0 if near else 1, upper, up_corner)):
            if u == ARRAYS and rows is upper:
                continue
            start = i * wy * ws + x
            lines[pl.ds(start + 2 * ws, ny, stride=ws), :] = rows
            for line, (k, unit) in enumerate(CORNER):
                if unit == u:
                    at = start + (0, 1, ny + 2, ny + 3)[k] * ws
                    lines[at:at + 1, :] = corner[line:line + 1]
    back = jnp.where(lax.axis_index("gz") == 0, 1, 0)

    for y in range(wy):
        all_ref[y * wx:y * wx + nx, :] = acc_ref[y]
        all_ref[y * wx + nx:(y + 1) * wx, :] = gather_planes(side_ref, y, back)
    full = all_ref.shape[0]
    all_ref[wy * wx:, :] = jnp.zeros((full - wy * wx, nz), F32)
    zp_ref[...] = all_ref[...].T[:Z_UNITS]


def curl_of(dx, dy, dz):
    return dy[2] - dz[1], dz[0] - dx[2], dx[1] - dy[0]


def slab_planes(slab_ref, wx, by0, bx0):
    full = slab_ref.shape[2]
    lane = lanes((8, full))
    line = (lane * 683) >> 14
    column = lane - line * wx
    half = jnp.where((by0 & (line < 2)) | (bx0 & (column >= wx - 2)), 0.0, time_step)

    def plus(f):
        ahead = lambda a: jnp.where(column == wx - 1, pltpu.roll(a, wx - 1, 1), pltpu.roll(a, full - 1, 1)) - a
        return curl_of(
            (None, ahead(f[1]), ahead(f[2])),
            (pltpu.roll(f[0], full - wx, 1) - f[0], None, pltpu.roll(f[2], full - wx, 1) - f[2]),
            (pltpu.roll(f[0], 7, 0) - f[0], pltpu.roll(f[1], 7, 0) - f[1]),
        )

    def minus(f):
        behind = lambda a: a - jnp.where(column == 0, pltpu.roll(a, full - wx + 1, 1), pltpu.roll(a, 1, 1))
        return curl_of(
            (None, behind(f[1]), behind(f[2])),
            (f[0] - pltpu.roll(f[0], wx, 1), None, f[2] - pltpu.roll(f[2], wx, 1)),
            (f[0] - pltpu.roll(f[0], 1, 0), f[1] - pltpu.roll(f[1], 1, 0)),
        )

    e, h, s, b = ([slab_ref[3 * k + c] for c in range(3)] for k in range(4))
    code = slab_ref[12]
    ratio = jnp.abs(code)
    h1 = [a - half * d for a, d in zip(h, plus(e))]
    g1 = [half * d for d in plus(s)]
    e1 = [a + ratio * d for a, d in zip(b, minus(h1))]
    s1 = [jnp.where(code < 0, a * (1.0 - ratio), a) - ratio * d for a, d in zip(s, minus(g1))]
    h2 = [a - half * d for a, d in zip(h1, plus(e1))]
    g2 = [a + half * d for a, d in zip(g1, plus(s1))]
    return (e, e1, s, s1), (h1, h2, g1, g2)


class Borders:
    def __init__(self, col_ref, wx, nz):
        self.col_ref, self.wx, self.nz, self.lane = col_ref, wx, nz, lanes((wx, nz))

    def beyond(self, y, k):
        return self.col_ref[pl.ds(pl.multiple_of(y * self.wx, 8), self.wx), k * self.nz:(k + 1) * self.nz]

    def plus(self, get, y, p):
        f, g = [get(c, y) for c in range(3)], [get(c, y + 1) for c in (0, 2)]
        dz = [pltpu.roll(jnp.where(self.lane == 0, self.beyond(y, 2 * p + c), f[c]), self.nz - 1, 1) - f[c] for c in range(2)]
        dx = [None] + [pltpu.roll(f[c], self.wx - 1, 0) - f[c] for c in (1, 2)]
        return curl_of(dx, (g[0] - f[0], None, g[1] - f[2]), dz)

    def minus(self, get, y, p):
        f, g = [get(c, y) for c in range(3)], [get(c, y - 1) for c in (0, 2)]
        dz = [f[c] - pltpu.roll(jnp.where(self.lane == self.nz - 1, self.beyond(y, 2 * p + c), f[c]), 1, 1) for c in range(2)]
        dx = [None] + [f[c] - pltpu.roll(f[c], 1, 0) for c in (1, 2)]
        return curl_of(dx, (f[0] - g[0], None, f[2] - g[1]), dz)


def halves(wx, nz):
    by0, bx0 = lax.axis_index("by") == 0, lax.axis_index("bx") == 0
    column = lax.broadcasted_iota(jnp.int32, (wx, nz), 0)
    along = jnp.where(bx0 & (column >= wx - 2), 0.0, time_step)
    return lambda y: along * jnp.where(by0 & (y < 2), 0.0, 1.0)


def main_kernel(body_ref, side_ref, zo_ref, zg_ref, j1_ref, c_ref, w_ref, q_ref, place_ref, ids_ref, blocks_ref,
                e2_ref, a0_ref, send_ref,
                slab_ref, plane_ref, col_ref, h1_ref, e1_ref, h2_ref, g1_ref, s1_ref, g2_ref,
                d1_ref, back_ref, cell_ref, partial_ref):
    size = 2 * w_ref.shape[1] * w_ref.shape[2] // blocks_ref.shape[1] * (2 * KB)
    ny, nx, nz = w_ref.shape
    tile_rows = size // nx
    wy, wx = ny + 4, nx + side_ref.shape[2]
    by0, bx0 = lax.axis_index("by") == 0, lax.axis_index("bx") == 0
    gz0 = lax.axis_index("gz") == 0

    for i in range(ARRAYS):
        u, deep = (2 * i, 2) if i < PAIRS else (9 + i, 1)
        mine, other = zo_ref[u:u + deep, :], zg_ref[u:u + deep, :]
        slab_ref[i] = jnp.zeros(slab_ref.shape[1:], F32)
        slab_ref[i, 2 - deep:2, :] = jnp.where(gz0, mine, other)
        slab_ref[i, 2:2 + deep, :] = jnp.where(gz0, other, mine)
    upper, lower = slab_planes(slab_ref, wx, by0, bx0)
    plane_ref[...] = jnp.zeros(plane_ref.shape, F32)
    for p in range(4):
        for c in range(2):
            plane_ref[2 * p + c:2 * p + c + 1, :] = jnp.where(gz0, upper[p][c][2:3], lower[p][c][1:2])
    rest = plane_ref[0:8, :]
    for k in range(3):
        part = rest.astype(BF16).astype(F32)
        plane_ref[8 * k:8 * k + 8, :] = part
        rest = rest - part
    wide = 8 * nz
    row, place = lax.broadcasted_iota(jnp.int32, (128, wide), 0), lanes((128, wide))
    border = place % nz == jnp.where(gz0, 0, nz - 1)
    chosen = jnp.where(border & (row % 8 == place // nz) & (row < 24), 1.0, 0.0).astype(BF16)
    col_ref[...] = lax.dot_general(plane_ref[...].T.astype(BF16), chosen, (((1,), (0,)), ((), ())), preferred_element_type=F32)

    borders, half = Borders(col_ref, wx, nz), halves(wx, nz)

    def array(k):
        return lambda c, y: jnp.concatenate([body_ref[3 * k + c, y], side_ref[3 * k + c, y]], axis=0)

    def row_of(ref):
        return lambda c, y: ref[c, y]

    electric, magnetic, scaled, start = (array(k) for k in range(4))

    def first_magnetic(y):
        factor = half(y)
        for c, d in enumerate(borders.plus(electric, y, 0)):
            h1_ref[c, y] = magnetic(c, y) - factor * d
        for c, d in enumerate(borders.plus(scaled, y, 2)):
            g1_ref[c, y] = factor * d

    def first_electric(y):
        code = array(4)(0, y)
        ratio = jnp.abs(code)
        kept = jnp.where(code < 0, 1.0 - ratio, 1.0)
        for c, d in enumerate(borders.minus(row_of(h1_ref), y, 0)):
            d1_ref[c, y] = d[:nx]
            e1_ref[c, y] = start(c, y) + ratio * d
        for c, d in enumerate(borders.minus(row_of(g1_ref), y, 2)):
            back_ref[c, y] = d[:nx]
            s1_ref[c, y] = scaled(c, y) * kept - ratio * d

    def second_magnetic(y):
        factor = half(y)
        for c, d in enumerate(borders.plus(row_of(e1_ref), y, 1)):
            h2_ref[c, y] = h1_ref[c, y] - factor * d

    def second_electric(y):
        at = y - 2
        code = body_ref[12, y]
        ratio, silver = jnp.abs(code), code < 0
        eps = jnp.zeros((nx, nz), F32)
        for c, d in enumerate(borders.minus(row_of(h2_ref), y, 1)):
            e1, j1 = e1_ref[c, y, 0:nx, :], j1_ref[c, at]
            drive = d[:nx] - jnp.where(silver, drude_keep * j1 + drude_gain * e1, 0.0)
            final = e1 + ratio * drive
            if c == 2:
                final = final + (source_level * source_wave[1]) * q_ref[at]
            e2_ref[c, at] = final
            eps = eps + body_ref[6 + c, y] * drive + s1_ref[c, y, 0:nx, :] * (d1_ref[c, y] - j1)
        cell_ref[pl.ds(pl.multiple_of(at * nx, 8), nx), :] = w_ref[at] * eps

    def last_magnetic(y):
        factor = half(y)
        for c, d in enumerate(borders.plus(row_of(s1_ref), y, 3)):
            g2_ref[c, y] = g1_ref[c, y] + factor * d

    def last_electric(y):
        silver = body_ref[12, y] < 0
        for c, d in enumerate(borders.minus(row_of(g2_ref), y, 3)):
            lost = jnp.where(silver, drude_gain * ((1.0 + drude_keep) * body_ref[6 + c, y] + s1_ref[c, y, 0:nx, :]), 0.0)
            a0_ref[c, y - 2] = c_ref[c, y - 2] - back_ref[c, y] - d[:nx] - lost

    for y in range(wy - 1):
        first_magnetic(y)
    for y in range(1, wy - 1):
        first_electric(y)
    for y in range(1, wy - 2):
        second_magnetic(y)

    group = nx
    sub = lax.broadcasted_iota(jnp.int32, (group, tile_rows), 0)

    def project(n):
        parts = [cell_ref[pl.ds(n * 2 * group + k, group, stride=2), :] for k in range(2)]
        cells = jnp.concatenate(parts, axis=1).astype(BF16)
        prods = lax.dot_general(cells, blocks_ref[n * size:(n + 1) * size, :], (((1,), (1,)), ((), ())), preferred_element_type=F32)
        acc = jnp.zeros((group, tile_rows), F32)
        for i in range(group):
            acc = jnp.where(sub == i, prods[:, i * tile_rows:(i + 1) * tile_rows], acc)
        partial_ref[n * group:(n + 1) * group, :] = acc

    second_electric(2)
    second_electric(3)
    last_magnetic(1)
    for n in range(1, ny // 2):
        for y in (2 * n + 2, 2 * n + 3):
            second_electric(y)
        for y in (2 * n, 2 * n + 1):
            last_magnetic(y)
        for y in (2 * n, 2 * n + 1):
            last_electric(y)
        project(n - 1)
    for y in (ny, ny + 1):
        last_magnetic(y)
    for y in (ny, ny + 1):
        last_electric(y)
    project(ny // 2 - 1)

    partial = partial_ref[...]
    turned = pltpu.roll(partial, KB, 1)
    low_lanes = lanes(partial.shape) < KB
    low = [jnp.where(low_lanes, a, 0.0) for a in (partial, turned)]
    high = [jnp.where(low_lanes, 0.0, a) for a in (turned, partial)]
    rhs = jnp.concatenate(low + high, axis=0)
    most = rhs.astype(BF16)
    rhs = jnp.concatenate([most, (rhs - most.astype(F32)).astype(BF16)], axis=0)
    lhs = jnp.concatenate([place_ref[0], place_ref[1], place_ref[0], place_ref[1]], axis=1)
    send_ref[...] = lax.dot_general(lhs, rhs, (((1,), (0,)), ((), ())), preferred_element_type=F32)
    planes = ids_ref.shape[0]
    width = send_ref.shape[0] // planes
    for d in range(planes):
        send_ref[d * width + width - 1:(d + 1) * width, :] = ids_ref[d:d + 1, :]


def capacity_of(planes, blocks):
    return max(2, 2 * blocks // planes)


def rows_of(planes, blocks):
    return capacity_of(planes, blocks) // 2


def make_places(rows, width, owner_ref, group_ref, place_ref, ids_ref):
    blocks = owner_ref.shape[1]
    planes = ids_ref.shape[0]
    row, column = (lax.broadcasted_iota(jnp.int32, (blocks, blocks), k) for k in range(2))
    half = blocks // 2
    swap = jnp.where(row == jnp.where(column < half, 2 * column, 2 * (column - half) + 1), 1.0, 0.0).astype(BF16)

    def arranged(ref):
        wide = jnp.broadcast_to(ref[...].astype(F32), (8, blocks)).astype(BF16)
        return lax.dot_general(wide, swap, (((1,), (0,)), ((), ())), preferred_element_type=F32)[:1]

    owner, group = arranged(owner_ref), arranged(group_ref)
    plane = lax.broadcasted_iota(jnp.int32, (planes, blocks), 0).astype(F32)
    hits = jnp.where(plane == owner, 1.0, 0.0)
    earlier = jnp.where(row < column, 1.0, 0.0).astype(BF16)
    before = lax.dot_general(hits.astype(BF16), earlier, (((1,), (0,)), ((), ())), preferred_element_type=F32)
    rank = jnp.sum(before * hits, axis=0, keepdims=True)
    slots = place_ref.shape[1]
    slot = lax.broadcasted_iota(jnp.int32, (slots, blocks), 0).astype(F32)
    for k in range(2):
        inner = rank - float(k * rows)
        target = jnp.where((inner >= 0.0) & (inner < float(rows)), owner * float(width) + inner, -1.0)
        place_ref[k] = jnp.where(slot == target, 1.0, 0.0).astype(BF16)
    ranks = lax.broadcasted_iota(jnp.int32, (128, blocks), 0).astype(F32)
    ranked = jnp.where(ranks == rank, 1.0, 0.0).astype(BF16)
    named = (hits * (group + 1.0)).astype(BF16)
    ids_ref[...] = lax.dot_general(named, ranked, (((1,), (1,)), ((), ())), preferred_element_type=F32) - 1.0


def collect_kernel(planes, got_ref, coef_ref, ids_ref):
    total, line = got_ref.shape
    width = total // planes
    rows = width - 1
    ids_ref[...] = jnp.zeros(ids_ref.shape, F32)
    for d in range(planes):
        ids_ref[d:d + 1, :] = got_ref[d * width + rows:(d + 1) * width, :] + 1.0
    shape = (total, line)
    index = lax.broadcasted_iota(jnp.int32, shape, 0)
    source = jnp.zeros(shape, jnp.int32)
    for d in range(1, planes):
        source = source + jnp.where(index >= d * width, 1, 0)
    place, lane = index - source * width, lanes(shape)
    spread = jnp.where(source == lane, 1.0, 0.0).astype(BF16)
    ids = lax.dot_general(spread, ids_ref[...].astype(BF16), (((1,), (0,)), ((), ())), preferred_element_type=F32)
    values = got_ref[...].T
    high = values.astype(BF16)
    low = (values - high.astype(F32)).astype(BF16)
    parts = []
    for k in range(2):
        mine = jnp.sum(jnp.where(lane == place + k * rows, ids, 0.0), axis=1, keepdims=True)
        hits = jnp.where((mine == lane.astype(F32) + 1.0) & (place < rows), 1.0, 0.0).astype(BF16)
        dots = [lax.dot_general(part, hits, (((1,), (0,)), ((), ())), preferred_element_type=F32) for part in (high, low)]
        parts.append((dots[0] + dots[1])[k * KB:(k + 1) * KB])
    coef_ref[...] = parts[0] + parts[1]


def call(kernel, outs, ins, scratch=(), places=None, leave=0, limit=16, cost=None):
    spaces = places or [pltpu.VMEM] * len(ins)
    keep = lambda a, space: pltpu.with_memory_space_constraint(a, space) if space is pltpu.VMEM else a
    return pl.pallas_call(
        kernel,
        out_shape=[jax.ShapeDtypeStruct(*o) if i < leave else pltpu.VMEM(*o) for i, o in enumerate(outs)],
        in_specs=[pl.BlockSpec(memory_space=pltpu.VMEM if space is None else space) for space in spaces],
        out_specs=[pl.BlockSpec(memory_space=pltpu.VMEM) for _ in outs],
        scratch_shapes=list(scratch),
        compiler_params=pltpu.CompilerParams(vmem_limit_bytes=limit * 1024 * 1024),
        cost_estimate=cost,
    )(*[keep(a, space) for a, space in zip(ins, spaces)])


def swapped(first, second, axis, starts=(0, 1)):
    axes = ("bx", "by", "gz")
    sizes = [lax.axis_size(name) for name in axes]
    along = axes.index(axis)
    arrived = []
    for start, value in zip(starts, (first, second)):
        pairs = []
        for flat in range(sizes[0] * sizes[1] * sizes[2]):
            at = [flat // (sizes[1] * sizes[2]), flat // sizes[2] % sizes[1], flat % sizes[2]]
            other = at[along] + 1 if at[along] % 2 == start else at[along] - 1
            if 0 <= other < sizes[along]:
                at[along] = other
            else:
                at[2] = (at[2] + 1) % sizes[2]
            pairs.append((flat, (at[0] * sizes[1] + at[1]) * sizes[2] + at[2]))
        arrived.append(lax.ppermute(value, axes, pairs))
    return arrived


def local(electric_start, magnetic_start, current_start, cotangent, level_set, material, source_cell, basis,
          block_owner, block_group):
    ny, nx, nz = material.shape
    wy, wx = ny + 4, nx + 8
    field, scalar = ((3, ny, nx, nz), F32), ((ny, nx, nz), F32)
    blocks = basis.shape[0]
    planes = lax.axis_size("bx") * lax.axis_size("by")
    rows = rows_of(planes, blocks)
    width = rows + 1
    y_face, x_face, corner = ((UNITS, nx, nz), F32), ((UNITS, ny, nz), F32), ((CORNER_LINES, nz), F32)
    names = ((1, blocks), jnp.int32)
    fa, fb, xa, xb, own, w, j1, q, weight, owner, group = call(
        prepare_kernel,
        [y_face, y_face, x_face, x_face, ((ARRAYS, ny, nx, nz), F32), scalar, field, scalar, field, names, names],
        [source_cell, electric_start, magnetic_start, current_start, cotangent, level_set, material,
         block_owner.reshape(1, blocks), block_group.reshape(1, blocks)],
        places=[pltpu.SMEM] + [None] * 8,
        limit=58,
    )
    gb, ga = swapped(fb, fa, "by", (1, 0))
    xb, xa = swapped(xb, xa, "bx", (1, 0))
    cb, ca = call(corner_kernel, [corner, corner], [gb, ga])
    cb, ca, owner, group = lax.optimization_barrier((cb, ca, owner, group))
    cb, ca = swapped(cb, ca, "bx", (1, 0))
    flat_basis = basis.reshape(blocks * KB, basis.shape[2])
    chunk = 2 * nx * nz // basis.shape[2] * (2 * KB)
    body, acc, place, ids = call(
        functools.partial(widen_kernel, rows, width),
        [((ARRAYS, wy, nx, nz), F32), ((wy, nx, nz), F32), ((2, planes * width, blocks), BF16), ((planes, 128), F32)],
        [own, gb, ga, owner, group],
        cost=pl.CostEstimate(flops=5_000_000_000, transcendentals=0, bytes_accessed=1000),
    )
    cb, ca, ids, acc = lax.optimization_barrier((cb, ca, ids, acc))
    full = -(-wy * wx // 128) * 128
    side, zp = call(
        extend_kernel,
        [((ARRAYS, wy, wx - nx, nz), F32), ((Z_UNITS, full), F32)],
        [acc, xb, xa, cb, ca],
        scratch=[pltpu.VMEM((full, nz), F32)],
    )
    zg = lax.ppermute(zp, "gz", [(0, 1), (1, 0)])
    wide, inner = ((3, wy, wx, nz), F32), ((3, wy, nx, nz), F32)
    electric, adjoint, send = call(
        main_kernel,
        [field, field, ((planes * width, 2 * KB), F32)],
        [body, side, zp, zg, j1, weight, w, q, place, ids, flat_basis],
        scratch=[
            pltpu.VMEM((ARRAYS, 8, full), F32),
            pltpu.VMEM((128, full), F32),
            pltpu.VMEM((full, 8 * nz), F32),
            *[pltpu.VMEM(*wide)] * 6,
            pltpu.VMEM(*inner), pltpu.VMEM(*inner),
            pltpu.VMEM((ny * nx, nz), F32),
            pltpu.VMEM((ny * nx // 2, 2 * KB), F32),
        ],
        limit=20,
    )
    send = send.reshape(planes * width, 1, 2 * KB)
    got = lax.all_to_all(send, ("bx", "by"), split_axis=0, concat_axis=0, tiled=True)
    (coef,) = call(
        functools.partial(collect_kernel, planes),
        [((KB, GRP_DEV), F32)],
        [got.reshape(planes * width, 2 * KB)],
        scratch=[pltpu.VMEM((128, 2 * KB), F32)],
        leave=1,
    )
    return electric, adjoint, coef


def solution(mesh):
    field = P(None, "by", "bx", "gz")
    scalar = P("by", "bx", "gz")
    flat = ("bx", "by", "gz")
    return jax.shard_map(
        local,
        mesh=mesh,
        in_specs=(field, field, field, field, scalar, scalar, P(flat), P(flat, None, None), P(flat, None), P(flat)),
        out_specs=(field, field, P(None, flat)),
        check_vma=False,
    )
```

```python
import functools

import jax
import jax.numpy as jnp
from jax import lax
from jax.experimental import pallas as pl
from jax.experimental.pallas import tpu as pltpu
from jax.sharding import PartitionSpec as P

KB = 64
GRP_DEV = 128

time_step = 0.5
drude_keep = 0.9
drude_gain = 1.0
metal_permit = 3.0
design_contrast = 5.0
source_level = 3.0
source_wave = (1.0, -0.6, 0.8, -0.4)

PAIRS, ARRAYS = 9, 13
UNITS = ARRAYS + 4
CORNER = [(0, u) for u in (1, 7)] + [(1, u) for u in (0, 1, 2, 3, 4, 5, 6, 7, 8, 10, 12, 15)]
CORNER += [(2, u) for u in (0, 1, 2, 4, 5, 6, 7, 8, 9, 12, 13, 14)] + [(3, 6)]
CORNER_LINES = -(-len(CORNER) // 8) * 8
Z_UNITS = 24
F32 = jnp.float32
BF16 = jnp.bfloat16


def is_even(axis):
    return lax.rem(lax.axis_index(axis), 2) == 0


def lanes(shape):
    return lax.broadcasted_iota(jnp.int32, shape, len(shape) - 1)


def prepare_kernel(cells_ref, e_ref, h_ref, j_ref, c_ref, level_ref, mat_ref, owner_ref, group_ref,
                   fa_ref, fb_ref, xa_ref, xb_ref, own_ref, w_ref, j1_ref, q_ref, c_out_ref, owner_out_ref, group_out_ref):
    owner_out_ref[...] = owner_ref[...]
    group_out_ref[...] = group_ref[...]
    ny, nx, nz = mat_ref.shape
    flat = lax.broadcasted_iota(jnp.int32, (nx, nz), 0) * nz + lanes((nx, nz))

    def row(y, carry):
        mat = mat_ref[y]
        silver, design = mat == 2, mat == 1
        smooth = 1.0 / (1.0 + jnp.exp(-level_ref[y]))
        permit = jnp.where(silver, metal_permit, jnp.where(design, 1.0 + design_contrast * smooth, 1.0))
        ratio = time_step / permit
        own_ref[12, y] = jnp.where(silver, -ratio, ratio)
        w_ref[y] = jnp.where(design, (-design_contrast / time_step) * ratio * smooth * (1.0 - smooth), 0.0)
        count = jnp.zeros((nx, nz), F32)
        for i in range(cells_ref.shape[0]):
            count = count + jnp.where(flat + y * (nx * nz) == cells_ref[i], 1.0, 0.0)
        q_ref[y] = count
        for c in range(3):
            electric, weight = e_ref[c, y], c_ref[c, y]
            current = jnp.where(silver, drude_keep * j_ref[c, y] + drude_gain * electric, 0.0)
            j1_ref[c, y] = current
            start = electric - ratio * current
            if c == 2:
                start = start + (source_level * source_wave[0]) * count
            own_ref[c, y] = electric
            own_ref[3 + c, y] = h_ref[c, y]
            own_ref[6 + c, y] = ratio * weight
            own_ref[9 + c, y] = start
            c_out_ref[c, y] = weight
        return carry

    lax.fori_loop(0, ny, row, 0, unroll=8)

    def y_face(out, near, deep, up):
        layers = [[own_ref[i, y] for i in range(ARRAYS)] for y in (near, deep)]
        for u, unit in enumerate(face_units(*layers, 1, up)):
            out[u] = unit

    lines = own_ref.reshape(ARRAYS * ny * nx, nz)

    def x_face(out, near, deep, up):
        layers = [[lines[pl.ds(i * ny * nx + x, ny, stride=nx), :] for i in range(ARRAYS)] for x in (near, deep)]
        for u, unit in enumerate(face_units(*layers, 0, up)):
            out[u] = unit

    for face, even, a_ref, b_ref, n in ((y_face, is_even("by"), fa_ref, fb_ref, ny), (x_face, is_even("bx"), xa_ref, xb_ref, nx)):
        @pl.when(even)
        def _():
            face(a_ref, n - 1, n - 2, True)
            face(b_ref, 0, 1, False)

        @pl.when(jnp.logical_not(even))
        def _():
            face(b_ref, n - 1, n - 2, True)
            face(a_ref, 0, 1, False)


def face_units(near, deep, axis, up):
    first, second = (axis + 1) % 3, (axis + 2) % 3
    units = list(near)
    if up:
        ratio = jnp.abs(near[12])
        units[9 + first] = near[9 + first] + ratio * (deep[3 + second] + time_step * deep[first])
        units[9 + second] = near[9 + second] - ratio * (deep[3 + first] - time_step * deep[second])
    else:
        units[3 + first] = near[3 + first] + time_step * deep[second]
        units[3 + second] = near[3 + second] - time_step * deep[first]
    return units + [deep[axis], deep[6], deep[7], deep[8]]


def sides(axis, even, a, b):
    at, zero = lax.axis_index(axis), jnp.zeros(a.shape, F32)
    lower = jnp.where(at == 0, zero, jnp.where(even, b, a))
    upper = jnp.where(at == lax.axis_size(axis) - 1, zero, jnp.where(even, a, b))
    return lower, upper


def rows_along_y(ga_ref, gb_ref):
    even, zero = is_even("by"), jnp.zeros(ga_ref.shape[1:], F32)
    units = [sides("by", even, ga_ref[u], gb_ref[u]) for u in range(UNITS)]
    lower, upper = ([unit[k] for unit in units] for k in range(2))
    below = [zero, lower[13], zero] + [zero] * 3 + lower[14:] + [zero] * 4
    above = [zero] * 6 + upper[14:] + [zero] * 4
    return below, lower[:ARRAYS], upper[:ARRAYS], above


def corner_kernel(gb_ref, ga_ref, cb_ref, ca_ref):
    nx = ga_ref.shape[1]
    rows = rows_along_y(ga_ref, gb_ref)
    even = is_even("bx")
    for ref in (ca_ref, cb_ref):
        ref[len(CORNER):, :] = jnp.zeros((CORNER_LINES - len(CORNER), ref.shape[1]), F32)

    def face(out, near, deep, up):
        units = [face_units([a[near:near + 1] for a in row], [a[deep:deep + 1] for a in row], 0, up) for row in rows]
        for line, (k, u) in enumerate(CORNER):
            out[line:line + 1, :] = units[k][u]

    @pl.when(even)
    def _():
        face(ca_ref, nx - 1, nx - 2, True)
        face(cb_ref, 0, 1, False)

    @pl.when(jnp.logical_not(even))
    def _():
        face(cb_ref, nx - 1, nx - 2, True)
        face(ca_ref, 0, 1, False)


def gather_planes(ref, y, back):
    shape = ref.shape[2:]
    lane, acc = lanes(shape), jnp.zeros(shape, F32)
    for i in range(ARRAYS):
        if i < PAIRS:
            acc = jnp.where(lane // 2 == i, pltpu.roll(ref[i, y], 2 * i + 2 * back, 1), acc)
        else:
            acc = jnp.where(lane == 9 + i, pltpu.roll(ref[i, y], 9 + i + back, 1), acc)
    return acc


def widen_kernel(rows, width, own_ref, gb_ref, ga_ref, owner_ref, group_ref, body_ref, acc_ref, place_ref, ids_ref):
    make_places(rows, width, owner_ref, group_ref, place_ref, ids_ref)
    ny = own_ref.shape[1]
    body_ref[:, 2:ny + 2] = own_ref[...]
    for y, row in zip((0, 1, ny + 2, ny + 3), rows_along_y(ga_ref, gb_ref)):
        for i in range(ARRAYS):
            body_ref[i, y] = row[i]
    back = jnp.where(lax.axis_index("gz") == 0, 1, 0)

    for y in range(ny + 4):
        acc_ref[y] = gather_planes(body_ref, y, back)


def extend_kernel(acc_ref, xb_ref, xa_ref, cb_ref, ca_ref, side_ref, zp_ref, all_ref):
    wy, nx, nz = acc_ref.shape
    ny, ws = wy - 4, side_ref.shape[2]
    wx = nx + ws
    x_even = is_even("bx")
    side_ref[...] = jnp.zeros(side_ref.shape, F32)
    lines = side_ref.reshape(ARRAYS * wy * ws, nz)
    low_corner, up_corner = sides("bx", x_even, ca_ref[...], cb_ref[...])
    for u in range(UNITS):
        i, near = (u, True) if u < ARRAYS else ((0, 6, 7, 8)[u - ARRAYS], False)
        lower, upper = sides("bx", x_even, xa_ref[u], xb_ref[u])
        for x, rows, corner in ((ws - 1 if near else ws - 2, lower, low_corner), (0 if near else 1, upper, up_corner)):
            if u == ARRAYS and rows is upper:
                continue
            start = i * wy * ws + x
            lines[pl.ds(start + 2 * ws, ny, stride=ws), :] = rows
            for line, (k, unit) in enumerate(CORNER):
                if unit == u:
                    at = start + (0, 1, ny + 2, ny + 3)[k] * ws
                    lines[at:at + 1, :] = corner[line:line + 1]
    back = jnp.where(lax.axis_index("gz") == 0, 1, 0)

    for y in range(wy):
        all_ref[y * wx:y * wx + nx, :] = acc_ref[y]
        all_ref[y * wx + nx:(y + 1) * wx, :] = gather_planes(side_ref, y, back)
    full = all_ref.shape[0]
    all_ref[wy * wx:, :] = jnp.zeros((full - wy * wx, nz), F32)
    zp_ref[...] = all_ref[...].T[:Z_UNITS]


def curl_of(dx, dy, dz):
    return dy[2] - dz[1], dz[0] - dx[2], dx[1] - dy[0]


def slab_planes(slab_ref, wx, by0, bx0):
    full = slab_ref.shape[2]
    lane = lanes((8, full))
    line = (lane * 683) >> 14
    column = lane - line * wx
    half = jnp.where((by0 & (line < 2)) | (bx0 & (column >= wx - 2)), 0.0, time_step)

    def plus(f):
        ahead = lambda a: jnp.where(column == wx - 1, pltpu.roll(a, wx - 1, 1), pltpu.roll(a, full - 1, 1)) - a
        return curl_of(
            (None, ahead(f[1]), ahead(f[2])),
            (pltpu.roll(f[0], full - wx, 1) - f[0], None, pltpu.roll(f[2], full - wx, 1) - f[2]),
            (pltpu.roll(f[0], 7, 0) - f[0], pltpu.roll(f[1], 7, 0) - f[1]),
        )

    def minus(f):
        behind = lambda a: a - jnp.where(column == 0, pltpu.roll(a, full - wx + 1, 1), pltpu.roll(a, 1, 1))
        return curl_of(
            (None, behind(f[1]), behind(f[2])),
            (f[0] - pltpu.roll(f[0], wx, 1), None, f[2] - pltpu.roll(f[2], wx, 1)),
            (f[0] - pltpu.roll(f[0], 1, 0), f[1] - pltpu.roll(f[1], 1, 0)),
        )

    e, h, s, b = ([slab_ref[3 * k + c] for c in range(3)] for k in range(4))
    code = slab_ref[12]
    ratio = jnp.abs(code)
    h1 = [a - half * d for a, d in zip(h, plus(e))]
    g1 = [half * d for d in plus(s)]
    e1 = [a + ratio * d for a, d in zip(b, minus(h1))]
    s1 = [jnp.where(code < 0, a * (1.0 - ratio), a) - ratio * d for a, d in zip(s, minus(g1))]
    h2 = [a - half * d for a, d in zip(h1, plus(e1))]
    g2 = [a + half * d for a, d in zip(g1, plus(s1))]
    return (e, e1, s, s1), (h1, h2, g1, g2)


class Borders:
    def __init__(self, col_ref, wx, nz):
        self.col_ref, self.wx, self.nz, self.lane = col_ref, wx, nz, lanes((wx, nz))

    def beyond(self, y, k):
        return self.col_ref[pl.ds(pl.multiple_of(y * self.wx, 8), self.wx), k * self.nz:(k + 1) * self.nz]

    def plus(self, get, y, p):
        f, g = [get(c, y) for c in range(3)], [get(c, y + 1) for c in (0, 2)]
        dz = [pltpu.roll(jnp.where(self.lane == 0, self.beyond(y, 2 * p + c), f[c]), self.nz - 1, 1) - f[c] for c in range(2)]
        dx = [None] + [pltpu.roll(f[c], self.wx - 1, 0) - f[c] for c in (1, 2)]
        return curl_of(dx, (g[0] - f[0], None, g[1] - f[2]), dz)

    def minus(self, get, y, p):
        f, g = [get(c, y) for c in range(3)], [get(c, y - 1) for c in (0, 2)]
        dz = [f[c] - pltpu.roll(jnp.where(self.lane == self.nz - 1, self.beyond(y, 2 * p + c), f[c]), 1, 1) for c in range(2)]
        dx = [None] + [f[c] - pltpu.roll(f[c], 1, 0) for c in (1, 2)]
        return curl_of(dx, (f[0] - g[0], None, f[2] - g[1]), dz)


def halves(wx, nz):
    by0, bx0 = lax.axis_index("by") == 0, lax.axis_index("bx") == 0
    column = lax.broadcasted_iota(jnp.int32, (wx, nz), 0)
    along = jnp.where(bx0 & (column >= wx - 2), 0.0, time_step)
    return lambda y: along * jnp.where(by0 & (y < 2), 0.0, 1.0)


def main_kernel(body_ref, side_ref, zo_ref, zg_ref, j1_ref, c_ref, w_ref, q_ref, place_ref, ids_ref, blocks_ref,
                e2_ref, a0_ref, send_ref,
                slab_ref, plane_ref, col_ref, h1_ref, e1_ref, h2_ref, g1_ref, s1_ref, g2_ref,
                d1_ref, back_ref, cell_ref, partial_ref):
    size = 2 * w_ref.shape[1] * w_ref.shape[2] // blocks_ref.shape[1] * (2 * KB)
    ny, nx, nz = w_ref.shape
    tile_rows = size // nx
    wy, wx = ny + 4, nx + side_ref.shape[2]
    by0, bx0 = lax.axis_index("by") == 0, lax.axis_index("bx") == 0
    gz0 = lax.axis_index("gz") == 0

    for i in range(ARRAYS):
        u, deep = (2 * i, 2) if i < PAIRS else (9 + i, 1)
        mine, other = zo_ref[u:u + deep, :], zg_ref[u:u + deep, :]
        slab_ref[i] = jnp.zeros(slab_ref.shape[1:], F32)
        slab_ref[i, 2 - deep:2, :] = jnp.where(gz0, mine, other)
        slab_ref[i, 2:2 + deep, :] = jnp.where(gz0, other, mine)
    upper, lower = slab_planes(slab_ref, wx, by0, bx0)
    plane_ref[...] = jnp.zeros(plane_ref.shape, F32)
    for p in range(4):
        for c in range(2):
            plane_ref[2 * p + c:2 * p + c + 1, :] = jnp.where(gz0, upper[p][c][2:3], lower[p][c][1:2])
    rest = plane_ref[0:8, :]
    for k in range(3):
        part = rest.astype(BF16).astype(F32)
        plane_ref[8 * k:8 * k + 8, :] = part
        rest = rest - part
    wide = 8 * nz
    row, place = lax.broadcasted_iota(jnp.int32, (128, wide), 0), lanes((128, wide))
    border = place % nz == jnp.where(gz0, 0, nz - 1)
    chosen = jnp.where(border & (row % 8 == place // nz) & (row < 24), 1.0, 0.0).astype(BF16)
    col_ref[...] = lax.dot_general(plane_ref[...].T.astype(BF16), chosen, (((1,), (0,)), ((), ())), preferred_element_type=F32)

    borders, half = Borders(col_ref, wx, nz), halves(wx, nz)

    def array(k):
        return lambda c, y: jnp.concatenate([body_ref[3 * k + c, y], side_ref[3 * k + c, y]], axis=0)

    def row_of(ref):
        return lambda c, y: ref[c, y]

    electric, magnetic, scaled, start = (array(k) for k in range(4))

    def first_magnetic(y):
        factor = half(y)
        for c, d in enumerate(borders.plus(electric, y, 0)):
            h1_ref[c, y] = magnetic(c, y) - factor * d
        for c, d in enumerate(borders.plus(scaled, y, 2)):
            g1_ref[c, y] = factor * d

    def first_electric(y):
        code = array(4)(0, y)
        ratio = jnp.abs(code)
        kept = jnp.where(code < 0, 1.0 - ratio, 1.0)
        for c, d in enumerate(borders.minus(row_of(h1_ref), y, 0)):
            d1_ref[c, y] = d[:nx]
            e1_ref[c, y] = start(c, y) + ratio * d
        for c, d in enumerate(borders.minus(row_of(g1_ref), y, 2)):
            back_ref[c, y] = d[:nx]
            s1_ref[c, y] = scaled(c, y) * kept - ratio * d

    def second_magnetic(y):
        factor = half(y)
        for c, d in enumerate(borders.plus(row_of(e1_ref), y, 1)):
            h2_ref[c, y] = h1_ref[c, y] - factor * d

    def second_electric(y):
        at = y - 2
        code = body_ref[12, y]
        ratio, silver = jnp.abs(code), code < 0
        eps = jnp.zeros((nx, nz), F32)
        for c, d in enumerate(borders.minus(row_of(h2_ref), y, 1)):
            e1, j1 = e1_ref[c, y, 0:nx, :], j1_ref[c, at]
            drive = d[:nx] - jnp.where(silver, drude_keep * j1 + drude_gain * e1, 0.0)
            final = e1 + ratio * drive
            if c == 2:
                final = final + (source_level * source_wave[1]) * q_ref[at]
            e2_ref[c, at] = final
            eps = eps + body_ref[6 + c, y] * drive + s1_ref[c, y, 0:nx, :] * (d1_ref[c, y] - j1)
        cell_ref[pl.ds(pl.multiple_of(at * nx, 8), nx), :] = w_ref[at] * eps

    def last_magnetic(y):
        factor = half(y)
        for c, d in enumerate(borders.plus(row_of(s1_ref), y, 3)):
            g2_ref[c, y] = g1_ref[c, y] + factor * d

    def last_electric(y):
        silver = body_ref[12, y] < 0
        for c, d in enumerate(borders.minus(row_of(g2_ref), y, 3)):
            lost = jnp.where(silver, drude_gain * ((1.0 + drude_keep) * body_ref[6 + c, y] + s1_ref[c, y, 0:nx, :]), 0.0)
            a0_ref[c, y - 2] = c_ref[c, y - 2] - back_ref[c, y] - d[:nx] - lost

    for y in range(wy - 1):
        first_magnetic(y)
    for y in range(1, wy - 1):
        first_electric(y)
    for y in range(1, wy - 2):
        second_magnetic(y)

    group = nx
    sub = lax.broadcasted_iota(jnp.int32, (group, tile_rows), 0)

    def project(n):
        parts = [cell_ref[pl.ds(n * 2 * group + k, group, stride=2), :] for k in range(2)]
        cells = jnp.concatenate(parts, axis=1).astype(BF16)
        prods = lax.dot_general(cells, blocks_ref[n * size:(n + 1) * size, :], (((1,), (1,)), ((), ())), preferred_element_type=F32)
        acc = jnp.zeros((group, tile_rows), F32)
        for i in range(group):
            acc = jnp.where(sub == i, prods[:, i * tile_rows:(i + 1) * tile_rows], acc)
        partial_ref[n * group:(n + 1) * group, :] = acc

    second_electric(2)
    second_electric(3)
    last_magnetic(1)
    for n in range(1, ny // 2):
        for y in (2 * n + 2, 2 * n + 3):
            second_electric(y)
        for y in (2 * n, 2 * n + 1):
            last_magnetic(y)
        for y in (2 * n, 2 * n + 1):
            last_electric(y)
        project(n - 1)
    for y in (ny, ny + 1):
        last_magnetic(y)
    for y in (ny, ny + 1):
        last_electric(y)
    project(ny // 2 - 1)

    partial = partial_ref[...]
    turned = pltpu.roll(partial, KB, 1)
    low_lanes = lanes(partial.shape) < KB
    low = [jnp.where(low_lanes, a, 0.0) for a in (partial, turned)]
    high = [jnp.where(low_lanes, 0.0, a) for a in (turned, partial)]
    rhs = jnp.concatenate(low + high, axis=0)
    most = rhs.astype(BF16)
    rhs = jnp.concatenate([most, (rhs - most.astype(F32)).astype(BF16)], axis=0)
    lhs = jnp.concatenate([place_ref[0], place_ref[1], place_ref[0], place_ref[1]], axis=1)
    send_ref[...] = lax.dot_general(lhs, rhs, (((1,), (0,)), ((), ())), preferred_element_type=F32)
    planes = ids_ref.shape[0]
    width = send_ref.shape[0] // planes
    for d in range(planes):
        send_ref[d * width + width - 1:(d + 1) * width, :] = ids_ref[d:d + 1, :]


def capacity_of(planes, blocks):
    return max(2, 2 * blocks // planes)


def rows_of(planes, blocks):
    return capacity_of(planes, blocks) // 2


def make_places(rows, width, owner_ref, group_ref, place_ref, ids_ref):
    blocks = owner_ref.shape[1]
    planes = ids_ref.shape[0]
    row, column = (lax.broadcasted_iota(jnp.int32, (blocks, blocks), k) for k in range(2))
    half = blocks // 2
    swap = jnp.where(row == jnp.where(column < half, 2 * column, 2 * (column - half) + 1), 1.0, 0.0).astype(BF16)

    def arranged(ref):
        wide = jnp.broadcast_to(ref[...].astype(F32), (8, blocks)).astype(BF16)
        return lax.dot_general(wide, swap, (((1,), (0,)), ((), ())), preferred_element_type=F32)[:1]

    owner, group = arranged(owner_ref), arranged(group_ref)
    plane = lax.broadcasted_iota(jnp.int32, (planes, blocks), 0).astype(F32)
    hits = jnp.where(plane == owner, 1.0, 0.0)
    earlier = jnp.where(row < column, 1.0, 0.0).astype(BF16)
    before = lax.dot_general(hits.astype(BF16), earlier, (((1,), (0,)), ((), ())), preferred_element_type=F32)
    rank = jnp.sum(before * hits, axis=0, keepdims=True)
    slots = place_ref.shape[1]
    slot = lax.broadcasted_iota(jnp.int32, (slots, blocks), 0).astype(F32)
    for k in range(2):
        inner = rank - float(k * rows)
        target = jnp.where((inner >= 0.0) & (inner < float(rows)), owner * float(width) + inner, -1.0)
        place_ref[k] = jnp.where(slot == target, 1.0, 0.0).astype(BF16)
    ranks = lax.broadcasted_iota(jnp.int32, (128, blocks), 0).astype(F32)
    ranked = jnp.where(ranks == rank, 1.0, 0.0).astype(BF16)
    named = (hits * (group + 1.0)).astype(BF16)
    ids_ref[...] = lax.dot_general(named, ranked, (((1,), (1,)), ((), ())), preferred_element_type=F32) - 1.0


def collect_kernel(planes, got_ref, coef_ref, ids_ref):
    total, line = got_ref.shape
    width = total // planes
    rows = width - 1
    ids_ref[...] = jnp.zeros(ids_ref.shape, F32)
    for d in range(planes):
        ids_ref[d:d + 1, :] = got_ref[d * width + rows:(d + 1) * width, :] + 1.0
    shape = (total, line)
    index = lax.broadcasted_iota(jnp.int32, shape, 0)
    source = jnp.zeros(shape, jnp.int32)
    for d in range(1, planes):
        source = source + jnp.where(index >= d * width, 1, 0)
    place, lane = index - source * width, lanes(shape)
    spread = jnp.where(source == lane, 1.0, 0.0).astype(BF16)
    ids = lax.dot_general(spread, ids_ref[...].astype(BF16), (((1,), (0,)), ((), ())), preferred_element_type=F32)
    values = got_ref[...].T
    high = values.astype(BF16)
    low = (values - high.astype(F32)).astype(BF16)
    parts = []
    for k in range(2):
        mine = jnp.sum(jnp.where(lane == place + k * rows, ids, 0.0), axis=1, keepdims=True)
        hits = jnp.where((mine == lane.astype(F32) + 1.0) & (place < rows), 1.0, 0.0).astype(BF16)
        dots = [lax.dot_general(part, hits, (((1,), (0,)), ((), ())), preferred_element_type=F32) for part in (high, low)]
        parts.append((dots[0] + dots[1])[k * KB:(k + 1) * KB])
    coef_ref[...] = parts[0] + parts[1]


def call(kernel, outs, ins, scratch=(), places=None, leave=0, limit=16, cost=None):
    spaces = places or [pltpu.VMEM] * len(ins)
    keep = lambda a, space: pltpu.with_memory_space_constraint(a, space) if space is pltpu.VMEM else a
    return pl.pallas_call(
        kernel,
        out_shape=[jax.ShapeDtypeStruct(*o) if i < leave else pltpu.VMEM(*o) for i, o in enumerate(outs)],
        in_specs=[pl.BlockSpec(memory_space=pltpu.VMEM if space is None else space) for space in spaces],
        out_specs=[pl.BlockSpec(memory_space=pltpu.VMEM) for _ in outs],
        scratch_shapes=list(scratch),
        compiler_params=pltpu.CompilerParams(vmem_limit_bytes=limit * 1024 * 1024),
        cost_estimate=cost,
    )(*[keep(a, space) for a, space in zip(ins, spaces)])


def swapped(first, second, axis, starts=(0, 1)):
    axes = ("bx", "by", "gz")
    sizes = [lax.axis_size(name) for name in axes]
    along = axes.index(axis)
    arrived = []
    for start, value in zip(starts, (first, second)):
        pairs = []
        for flat in range(sizes[0] * sizes[1] * sizes[2]):
            at = [flat // (sizes[1] * sizes[2]), flat // sizes[2] % sizes[1], flat % sizes[2]]
            other = at[along] + 1 if at[along] % 2 == start else at[along] - 1
            if 0 <= other < sizes[along]:
                at[along] = other
            else:
                at[2] = (at[2] + 1) % sizes[2]
            pairs.append((flat, (at[0] * sizes[1] + at[1]) * sizes[2] + at[2]))
        arrived.append(lax.ppermute(value, axes, pairs))
    return arrived


def local(electric_start, magnetic_start, current_start, cotangent, level_set, material, source_cell, basis,
          block_owner, block_group):
    ny, nx, nz = material.shape
    wy, wx = ny + 4, nx + 8
    field, scalar = ((3, ny, nx, nz), F32), ((ny, nx, nz), F32)
    blocks = basis.shape[0]
    planes = lax.axis_size("bx") * lax.axis_size("by")
    rows = rows_of(planes, blocks)
    width = rows + 1
    y_face, x_face, corner = ((UNITS, nx, nz), F32), ((UNITS, ny, nz), F32), ((CORNER_LINES, nz), F32)
    names = ((1, blocks), jnp.int32)
    fa, fb, xa, xb, own, w, j1, q, weight, owner, group = call(
        prepare_kernel,
        [y_face, y_face, x_face, x_face, ((ARRAYS, ny, nx, nz), F32), scalar, field, scalar, field, names, names],
        [source_cell, electric_start, magnetic_start, current_start, cotangent, level_set, material,
         block_owner.reshape(1, blocks), block_group.reshape(1, blocks)],
        places=[pltpu.SMEM] + [None] * 8,
        limit=58,
    )
    gb, ga = swapped(fb, fa, "by", (1, 0))
    xb, xa = swapped(xb, xa, "bx", (1, 0))
    cb, ca = call(corner_kernel, [corner, corner], [gb, ga])
    cb, ca, owner, group = lax.optimization_barrier((cb, ca, owner, group))
    cb, ca = swapped(cb, ca, "bx", (1, 0))
    flat_basis = basis.reshape(blocks * KB, basis.shape[2])
    chunk = 2 * nx * nz // basis.shape[2] * (2 * KB)
    body, acc, place, ids = call(
        functools.partial(widen_kernel, rows, width),
        [((ARRAYS, wy, nx, nz), F32), ((wy, nx, nz), F32), ((2, planes * width, blocks), BF16), ((planes, 128), F32)],
        [own, gb, ga, owner, group],
        cost=pl.CostEstimate(flops=5_000_000_000, transcendentals=0, bytes_accessed=1000),
    )
    cb, ca, ids, acc = lax.optimization_barrier((cb, ca, ids, acc))
    full = -(-wy * wx // 128) * 128
    side, zp = call(
        extend_kernel,
        [((ARRAYS, wy, wx - nx, nz), F32), ((Z_UNITS, full), F32)],
        [acc, xb, xa, cb, ca],
        scratch=[pltpu.VMEM((full, nz), F32)],
    )
    zg = lax.ppermute(zp, "gz", [(0, 1), (1, 0)])
    wide, inner = ((3, wy, wx, nz), F32), ((3, wy, nx, nz), F32)
    electric, adjoint, send = call(
        main_kernel,
        [field, field, ((planes * width, 2 * KB), F32)],
        [body, side, zp, zg, j1, weight, w, q, place, ids, flat_basis],
        scratch=[
            pltpu.VMEM((ARRAYS, 8, full), F32),
            pltpu.VMEM((128, full), F32),
            pltpu.VMEM((full, 8 * nz), F32),
            *[pltpu.VMEM(*wide)] * 6,
            pltpu.VMEM(*inner), pltpu.VMEM(*inner),
            pltpu.VMEM((ny * nx, nz), F32),
            pltpu.VMEM((ny * nx // 2, 2 * KB), F32),
        ],
        limit=20,
    )
    send = send.reshape(planes * width, 1, 2 * KB)
    got = lax.all_to_all(send, ("bx", "by"), split_axis=0, concat_axis=0, tiled=True)
    (coef,) = call(
        functools.partial(collect_kernel, planes),
        [((KB, GRP_DEV), F32)],
        [got.reshape(planes * width, 2 * KB)],
        scratch=[pltpu.VMEM((128, 2 * KB), F32)],
        leave=1,
    )
    return electric, adjoint, coef


def solution(mesh):
    field = P(None, "by", "bx", "gz")
    scalar = P("by", "bx", "gz")
    flat = ("bx", "by", "gz")
    return jax.shard_map(
        local,
        mesh=mesh,
        in_specs=(field, field, field, field, scalar, scalar, P(flat), P(flat, None, None), P(flat, None), P(flat)),
        out_specs=(field, field, P(None, flat)),
        check_vma=False,
    )
```

```python
import functools

import jax
import jax.numpy as jnp
from jax import lax
from jax.experimental import pallas as pl
from jax.experimental.pallas import tpu as pltpu
from jax.sharding import PartitionSpec as P

KB = 64
GRP_DEV = 128

time_step = 0.5
drude_keep = 0.9
drude_gain = 1.0
metal_permit = 3.0
design_contrast = 5.0
source_level = 3.0
source_wave = (1.0, -0.6, 0.8, -0.4)

PAIRS, ARRAYS = 9, 13
UNITS = ARRAYS + 4
CORNER = [(0, u) for u in (1, 7)] + [(1, u) for u in (0, 1, 2, 3, 4, 5, 6, 7, 8, 10, 12, 15)]
CORNER += [(2, u) for u in (0, 1, 2, 4, 5, 6, 7, 8, 9, 12, 13, 14)] + [(3, 6)]
CORNER_LINES = -(-len(CORNER) // 8) * 8
Z_UNITS = 24
F32 = jnp.float32
BF16 = jnp.bfloat16


def is_even(axis):
    return lax.rem(lax.axis_index(axis), 2) == 0


def lanes(shape):
    return lax.broadcasted_iota(jnp.int32, shape, len(shape) - 1)


def prepare_kernel(cells_ref, e_ref, h_ref, j_ref, c_ref, level_ref, mat_ref, owner_ref, group_ref,
                   fa_ref, fb_ref, xa_ref, xb_ref, own_ref, w_ref, j1_ref, q_ref, c_out_ref, owner_out_ref, group_out_ref):
    owner_out_ref[...] = owner_ref[...]
    group_out_ref[...] = group_ref[...]
    ny, nx, nz = mat_ref.shape
    flat = lax.broadcasted_iota(jnp.int32, (nx, nz), 0) * nz + lanes((nx, nz))

    def row(y, carry):
        mat = mat_ref[y]
        silver, design = mat == 2, mat == 1
        smooth = 1.0 / (1.0 + jnp.exp(-level_ref[y]))
        permit = jnp.where(silver, metal_permit, jnp.where(design, 1.0 + design_contrast * smooth, 1.0))
        ratio = time_step / permit
        own_ref[12, y] = jnp.where(silver, -ratio, ratio)
        w_ref[y] = jnp.where(design, (-design_contrast / time_step) * ratio * smooth * (1.0 - smooth), 0.0)
        count = jnp.zeros((nx, nz), F32)
        for i in range(cells_ref.shape[0]):
            count = count + jnp.where(flat + y * (nx * nz) == cells_ref[i], 1.0, 0.0)
        q_ref[y] = count
        for c in range(3):
            electric, weight = e_ref[c, y], c_ref[c, y]
            current = jnp.where(silver, drude_keep * j_ref[c, y] + drude_gain * electric, 0.0)
            j1_ref[c, y] = current
            start = electric - ratio * current
            if c == 2:
                start = start + (source_level * source_wave[0]) * count
            own_ref[c, y] = electric
            own_ref[3 + c, y] = h_ref[c, y]
            own_ref[6 + c, y] = ratio * weight
            own_ref[9 + c, y] = start
            c_out_ref[c, y] = weight
        return carry

    lax.fori_loop(0, ny, row, 0, unroll=16)

    def y_face(out, near, deep, up):
        layers = [[own_ref[i, y] for i in range(ARRAYS)] for y in (near, deep)]
        for u, unit in enumerate(face_units(*layers, 1, up)):
            out[u] = unit

    lines = own_ref.reshape(ARRAYS * ny * nx, nz)

    def x_face(out, near, deep, up):
        layers = [[lines[pl.ds(i * ny * nx + x, ny, stride=nx), :] for i in range(ARRAYS)] for x in (near, deep)]
        for u, unit in enumerate(face_units(*layers, 0, up)):
            out[u] = unit

    for face, even, a_ref, b_ref, n in ((y_face, is_even("by"), fa_ref, fb_ref, ny), (x_face, is_even("bx"), xa_ref, xb_ref, nx)):
        @pl.when(even)
        def _():
            face(a_ref, n - 1, n - 2, True)
            face(b_ref, 0, 1, False)

        @pl.when(jnp.logical_not(even))
        def _():
            face(b_ref, n - 1, n - 2, True)
            face(a_ref, 0, 1, False)


def face_units(near, deep, axis, up):
    first, second = (axis + 1) % 3, (axis + 2) % 3
    units = list(near)
    if up:
        ratio = jnp.abs(near[12])
        units[9 + first] = near[9 + first] + ratio * (deep[3 + second] + time_step * deep[first])
        units[9 + second] = near[9 + second] - ratio * (deep[3 + first] - time_step * deep[second])
    else:
        units[3 + first] = near[3 + first] + time_step * deep[second]
        units[3 + second] = near[3 + second] - time_step * deep[first]
    return units + [deep[axis], deep[6], deep[7], deep[8]]


def sides(axis, even, a, b):
    at, zero = lax.axis_index(axis), jnp.zeros(a.shape, F32)
    lower = jnp.where(at == 0, zero, jnp.where(even, b, a))
    upper = jnp.where(at == lax.axis_size(axis) - 1, zero, jnp.where(even, a, b))
    return lower, upper


def rows_along_y(ga_ref, gb_ref):
    even, zero = is_even("by"), jnp.zeros(ga_ref.shape[1:], F32)
    units = [sides("by", even, ga_ref[u], gb_ref[u]) for u in range(UNITS)]
    lower, upper = ([unit[k] for unit in units] for k in range(2))
    below = [zero, lower[13], zero] + [zero] * 3 + lower[14:] + [zero] * 4
    above = [zero] * 6 + upper[14:] + [zero] * 4
    return below, lower[:ARRAYS], upper[:ARRAYS], above


def corner_kernel(gb_ref, ga_ref, cb_ref, ca_ref):
    nx = ga_ref.shape[1]
    rows = rows_along_y(ga_ref, gb_ref)
    even = is_even("bx")
    for ref in (ca_ref, cb_ref):
        ref[len(CORNER):, :] = jnp.zeros((CORNER_LINES - len(CORNER), ref.shape[1]), F32)

    def face(out, near, deep, up):
        units = [face_units([a[near:near + 1] for a in row], [a[deep:deep + 1] for a in row], 0, up) for row in rows]
        for line, (k, u) in enumerate(CORNER):
            out[line:line + 1, :] = units[k][u]

    @pl.when(even)
    def _():
        face(ca_ref, nx - 1, nx - 2, True)
        face(cb_ref, 0, 1, False)

    @pl.when(jnp.logical_not(even))
    def _():
        face(cb_ref, nx - 1, nx - 2, True)
        face(ca_ref, 0, 1, False)


def gather_planes(ref, y, back):
    shape = ref.shape[2:]
    lane, acc = lanes(shape), jnp.zeros(shape, F32)
    for i in range(ARRAYS):
        if i < PAIRS:
            acc = jnp.where(lane // 2 == i, pltpu.roll(ref[i, y], 2 * i + 2 * back, 1), acc)
        else:
            acc = jnp.where(lane == 9 + i, pltpu.roll(ref[i, y], 9 + i + back, 1), acc)
    return acc


def widen_kernel(rows, width, own_ref, gb_ref, ga_ref, owner_ref, group_ref, body_ref, acc_ref, place_ref, ids_ref):
    make_places(rows, width, owner_ref, group_ref, place_ref, ids_ref)
    ny = own_ref.shape[1]
    body_ref[:, 2:ny + 2] = own_ref[...]
    for y, row in zip((0, 1, ny + 2, ny + 3), rows_along_y(ga_ref, gb_ref)):
        for i in range(ARRAYS):
            body_ref[i, y] = row[i]
    back = jnp.where(lax.axis_index("gz") == 0, 1, 0)

    for y in range(ny + 4):
        acc_ref[y] = gather_planes(body_ref, y, back)


def extend_kernel(acc_ref, xb_ref, xa_ref, cb_ref, ca_ref, side_ref, zp_ref, all_ref):
    wy, nx, nz = acc_ref.shape
    ny, ws = wy - 4, side_ref.shape[2]
    wx = nx + ws
    x_even = is_even("bx")
    side_ref[...] = jnp.zeros(side_ref.shape, F32)
    lines = side_ref.reshape(ARRAYS * wy * ws, nz)
    low_corner, up_corner = sides("bx", x_even, ca_ref[...], cb_ref[...])
    for u in range(UNITS):
        i, near = (u, True) if u < ARRAYS else ((0, 6, 7, 8)[u - ARRAYS], False)
        lower, upper = sides("bx", x_even, xa_ref[u], xb_ref[u])
        for x, rows, corner in ((ws - 1 if near else ws - 2, lower, low_corner), (0 if near else 1, upper, up_corner)):
            if u == ARRAYS and rows is upper:
                continue
            start = i * wy * ws + x
            lines[pl.ds(start + 2 * ws, ny, stride=ws), :] = rows
            for line, (k, unit) in enumerate(CORNER):
                if unit == u:
                    at = start + (0, 1, ny + 2, ny + 3)[k] * ws
                    lines[at:at + 1, :] = corner[line:line + 1]
    back = jnp.where(lax.axis_index("gz") == 0, 1, 0)

    for y in range(wy):
        all_ref[y * wx:y * wx + nx, :] = acc_ref[y]
        all_ref[y * wx + nx:(y + 1) * wx, :] = gather_planes(side_ref, y, back)
    full = all_ref.shape[0]
    all_ref[wy * wx:, :] = jnp.zeros((full - wy * wx, nz), F32)
    zp_ref[...] = all_ref[...].T[:Z_UNITS]


def curl_of(dx, dy, dz):
    return dy[2] - dz[1], dz[0] - dx[2], dx[1] - dy[0]


def slab_planes(slab_ref, wx, by0, bx0):
    full = slab_ref.shape[2]
    lane = lanes((8, full))
    line = (lane * 683) >> 14
    column = lane - line * wx
    half = jnp.where((by0 & (line < 2)) | (bx0 & (column >= wx - 2)), 0.0, time_step)

    def plus(f):
        ahead = lambda a: jnp.where(column == wx - 1, pltpu.roll(a, wx - 1, 1), pltpu.roll(a, full - 1, 1)) - a
        return curl_of(
            (None, ahead(f[1]), ahead(f[2])),
            (pltpu.roll(f[0], full - wx, 1) - f[0], None, pltpu.roll(f[2], full - wx, 1) - f[2]),
            (pltpu.roll(f[0], 7, 0) - f[0], pltpu.roll(f[1], 7, 0) - f[1]),
        )

    def minus(f):
        behind = lambda a: a - jnp.where(column == 0, pltpu.roll(a, full - wx + 1, 1), pltpu.roll(a, 1, 1))
        return curl_of(
            (None, behind(f[1]), behind(f[2])),
            (f[0] - pltpu.roll(f[0], wx, 1), None, f[2] - pltpu.roll(f[2], wx, 1)),
            (f[0] - pltpu.roll(f[0], 1, 0), f[1] - pltpu.roll(f[1], 1, 0)),
        )

    e, h, s, b = ([slab_ref[3 * k + c] for c in range(3)] for k in range(4))
    code = slab_ref[12]
    ratio = jnp.abs(code)
    h1 = [a - half * d for a, d in zip(h, plus(e))]
    g1 = [half * d for d in plus(s)]
    e1 = [a + ratio * d for a, d in zip(b, minus(h1))]
    s1 = [jnp.where(code < 0, a * (1.0 - ratio), a) - ratio * d for a, d in zip(s, minus(g1))]
    h2 = [a - half * d for a, d in zip(h1, plus(e1))]
    g2 = [a + half * d for a, d in zip(g1, plus(s1))]
    return (e, e1, s, s1), (h1, h2, g1, g2)


class Borders:
    def __init__(self, col_ref, wx, nz):
        self.col_ref, self.wx, self.nz, self.lane = col_ref, wx, nz, lanes((wx, nz))

    def beyond(self, y, k):
        return self.col_ref[pl.ds(pl.multiple_of(y * self.wx, 8), self.wx), k * self.nz:(k + 1) * self.nz]

    def plus(self, get, y, p):
        f, g = [get(c, y) for c in range(3)], [get(c, y + 1) for c in (0, 2)]
        dz = [pltpu.roll(jnp.where(self.lane == 0, self.beyond(y, 2 * p + c), f[c]), self.nz - 1, 1) - f[c] for c in range(2)]
        dx = [None] + [pltpu.roll(f[c], self.wx - 1, 0) - f[c] for c in (1, 2)]
        return curl_of(dx, (g[0] - f[0], None, g[1] - f[2]), dz)

    def minus(self, get, y, p):
        f, g = [get(c, y) for c in range(3)], [get(c, y - 1) for c in (0, 2)]
        dz = [f[c] - pltpu.roll(jnp.where(self.lane == self.nz - 1, self.beyond(y, 2 * p + c), f[c]), 1, 1) for c in range(2)]
        dx = [None] + [f[c] - pltpu.roll(f[c], 1, 0) for c in (1, 2)]
        return curl_of(dx, (f[0] - g[0], None, f[2] - g[1]), dz)


def halves(wx, nz):
    by0, bx0 = lax.axis_index("by") == 0, lax.axis_index("bx") == 0
    column = lax.broadcasted_iota(jnp.int32, (wx, nz), 0)
    along = jnp.where(bx0 & (column >= wx - 2), 0.0, time_step)
    return lambda y: along * jnp.where(by0 & (y < 2), 0.0, 1.0)


def main_kernel(body_ref, side_ref, zo_ref, zg_ref, j1_ref, c_ref, w_ref, q_ref, place_ref, ids_ref, blocks_ref,
                e2_ref, a0_ref, send_ref,
                slab_ref, plane_ref, col_ref, h1_ref, e1_ref, h2_ref, g1_ref, s1_ref, g2_ref,
                d1_ref, back_ref, cell_ref, partial_ref):
    size = 2 * w_ref.shape[1] * w_ref.shape[2] // blocks_ref.shape[1] * (2 * KB)
    ny, nx, nz = w_ref.shape
    tile_rows = size // nx
    wy, wx = ny + 4, nx + side_ref.shape[2]
    by0, bx0 = lax.axis_index("by") == 0, lax.axis_index("bx") == 0
    gz0 = lax.axis_index("gz") == 0

    for i in range(ARRAYS):
        u, deep = (2 * i, 2) if i < PAIRS else (9 + i, 1)
        mine, other = zo_ref[u:u + deep, :], zg_ref[u:u + deep, :]
        slab_ref[i] = jnp.zeros(slab_ref.shape[1:], F32)
        slab_ref[i, 2 - deep:2, :] = jnp.where(gz0, mine, other)
        slab_ref[i, 2:2 + deep, :] = jnp.where(gz0, other, mine)
    upper, lower = slab_planes(slab_ref, wx, by0, bx0)
    plane_ref[...] = jnp.zeros(plane_ref.shape, F32)
    for p in range(4):
        for c in range(2):
            plane_ref[2 * p + c:2 * p + c + 1, :] = jnp.where(gz0, upper[p][c][2:3], lower[p][c][1:2])
    rest = plane_ref[0:8, :]
    for k in range(3):
        part = rest.astype(BF16).astype(F32)
        plane_ref[8 * k:8 * k + 8, :] = part
        rest = rest - part
    wide = 8 * nz
    row, place = lax.broadcasted_iota(jnp.int32, (128, wide), 0), lanes((128, wide))
    border = place % nz == jnp.where(gz0, 0, nz - 1)
    chosen = jnp.where(border & (row % 8 == place // nz) & (row < 24), 1.0, 0.0).astype(BF16)
    col_ref[...] = lax.dot_general(plane_ref[...].T.astype(BF16), chosen, (((1,), (0,)), ((), ())), preferred_element_type=F32)

    borders, half = Borders(col_ref, wx, nz), halves(wx, nz)

    def array(k):
        return lambda c, y: jnp.concatenate([body_ref[3 * k + c, y], side_ref[3 * k + c, y]], axis=0)

    def row_of(ref):
        return lambda c, y: ref[c, y]

    electric, magnetic, scaled, start = (array(k) for k in range(4))

    def first_magnetic(y):
        factor = half(y)
        for c, d in enumerate(borders.plus(electric, y, 0)):
            h1_ref[c, y] = magnetic(c, y) - factor * d
        for c, d in enumerate(borders.plus(scaled, y, 2)):
            g1_ref[c, y] = factor * d

    def first_electric(y):
        code = array(4)(0, y)
        ratio = jnp.abs(code)
        kept = jnp.where(code < 0, 1.0 - ratio, 1.0)
        for c, d in enumerate(borders.minus(row_of(h1_ref), y, 0)):
            d1_ref[c, y] = d[:nx]
            e1_ref[c, y] = start(c, y) + ratio * d
        for c, d in enumerate(borders.minus(row_of(g1_ref), y, 2)):
            back_ref[c, y] = d[:nx]
            s1_ref[c, y] = scaled(c, y) * kept - ratio * d

    def second_magnetic(y):
        factor = half(y)
        for c, d in enumerate(borders.plus(row_of(e1_ref), y, 1)):
            h2_ref[c, y] = h1_ref[c, y] - factor * d

    def second_electric(y):
        at = y - 2
        code = body_ref[12, y]
        ratio, silver = jnp.abs(code), code < 0
        eps = jnp.zeros((nx, nz), F32)
        for c, d in enumerate(borders.minus(row_of(h2_ref), y, 1)):
            e1, j1 = e1_ref[c, y, 0:nx, :], j1_ref[c, at]
            drive = d[:nx] - jnp.where(silver, drude_keep * j1 + drude_gain * e1, 0.0)
            final = e1 + ratio * drive
            if c == 2:
                final = final + (source_level * source_wave[1]) * q_ref[at]
            e2_ref[c, at] = final
            eps = eps + body_ref[6 + c, y] * drive + s1_ref[c, y, 0:nx, :] * (d1_ref[c, y] - j1)
        cell_ref[pl.ds(pl.multiple_of(at * nx, 8), nx), :] = w_ref[at] * eps

    def last_magnetic(y):
        factor = half(y)
        for c, d in enumerate(borders.plus(row_of(s1_ref), y, 3)):
            g2_ref[c, y] = g1_ref[c, y] + factor * d

    def last_electric(y):
        silver = body_ref[12, y] < 0
        for c, d in enumerate(borders.minus(row_of(g2_ref), y, 3)):
            lost = jnp.where(silver, drude_gain * ((1.0 + drude_keep) * body_ref[6 + c, y] + s1_ref[c, y, 0:nx, :]), 0.0)
            a0_ref[c, y - 2] = c_ref[c, y - 2] - back_ref[c, y] - d[:nx] - lost

    for y in range(wy - 1):
        first_magnetic(y)
    for y in range(1, wy - 1):
        first_electric(y)
    for y in range(1, wy - 2):
        second_magnetic(y)

    group = nx
    sub = lax.broadcasted_iota(jnp.int32, (group, tile_rows), 0)

    def project(n):
        parts = [cell_ref[pl.ds(n * 2 * group + k, group, stride=2), :] for k in range(2)]
        cells = jnp.concatenate(parts, axis=1).astype(BF16)
        prods = lax.dot_general(cells, blocks_ref[n * size:(n + 1) * size, :], (((1,), (1,)), ((), ())), preferred_element_type=F32)
        acc = jnp.zeros((group, tile_rows), F32)
        for i in range(group):
            acc = jnp.where(sub == i, prods[:, i * tile_rows:(i + 1) * tile_rows], acc)
        partial_ref[n * group:(n + 1) * group, :] = acc

    second_electric(2)
    second_electric(3)
    last_magnetic(1)
    for n in range(1, ny // 2):
        for y in (2 * n + 2, 2 * n + 3):
            second_electric(y)
        for y in (2 * n, 2 * n + 1):
            last_magnetic(y)
        for y in (2 * n, 2 * n + 1):
            last_electric(y)
        project(n - 1)
    for y in (ny, ny + 1):
        last_magnetic(y)
    for y in (ny, ny + 1):
        last_electric(y)
    project(ny // 2 - 1)

    partial = partial_ref[...]
    turned = pltpu.roll(partial, KB, 1)
    low_lanes = lanes(partial.shape) < KB
    low = [jnp.where(low_lanes, a, 0.0) for a in (partial, turned)]
    high = [jnp.where(low_lanes, 0.0, a) for a in (turned, partial)]
    rhs = jnp.concatenate(low + high, axis=0)
    most = rhs.astype(BF16)
    rhs = jnp.concatenate([most, (rhs - most.astype(F32)).astype(BF16)], axis=0)
    lhs = jnp.concatenate([place_ref[0], place_ref[1], place_ref[0], place_ref[1]], axis=1)
    send_ref[...] = lax.dot_general(lhs, rhs, (((1,), (0,)), ((), ())), preferred_element_type=F32)
    planes = ids_ref.shape[0]
    width = send_ref.shape[0] // planes
    for d in range(planes):
        send_ref[d * width + width - 1:(d + 1) * width, :] = ids_ref[d:d + 1, :]


def capacity_of(planes, blocks):
    return max(2, 2 * blocks // planes)


def rows_of(planes, blocks):
    return capacity_of(planes, blocks) // 2


def make_places(rows, width, owner_ref, group_ref, place_ref, ids_ref):
    blocks = owner_ref.shape[1]
    planes = ids_ref.shape[0]
    row, column = (lax.broadcasted_iota(jnp.int32, (blocks, blocks), k) for k in range(2))
    half = blocks // 2
    swap = jnp.where(row == jnp.where(column < half, 2 * column, 2 * (column - half) + 1), 1.0, 0.0).astype(BF16)

    def arranged(ref):
        wide = jnp.broadcast_to(ref[...].astype(F32), (8, blocks)).astype(BF16)
        return lax.dot_general(wide, swap, (((1,), (0,)), ((), ())), preferred_element_type=F32)[:1]

    owner, group = arranged(owner_ref), arranged(group_ref)
    plane = lax.broadcasted_iota(jnp.int32, (planes, blocks), 0).astype(F32)
    hits = jnp.where(plane == owner, 1.0, 0.0)
    earlier = jnp.where(row < column, 1.0, 0.0).astype(BF16)
    before = lax.dot_general(hits.astype(BF16), earlier, (((1,), (0,)), ((), ())), preferred_element_type=F32)
    rank = jnp.sum(before * hits, axis=0, keepdims=True)
    slots = place_ref.shape[1]
    slot = lax.broadcasted_iota(jnp.int32, (slots, blocks), 0).astype(F32)
    for k in range(2):
        inner = rank - float(k * rows)
        target = jnp.where((inner >= 0.0) & (inner < float(rows)), owner * float(width) + inner, -1.0)
        place_ref[k] = jnp.where(slot == target, 1.0, 0.0).astype(BF16)
    ranks = lax.broadcasted_iota(jnp.int32, (128, blocks), 0).astype(F32)
    ranked = jnp.where(ranks == rank, 1.0, 0.0).astype(BF16)
    named = (hits * (group + 1.0)).astype(BF16)
    ids_ref[...] = lax.dot_general(named, ranked, (((1,), (1,)), ((), ())), preferred_element_type=F32) - 1.0


def collect_kernel(planes, got_ref, coef_ref, ids_ref):
    total, line = got_ref.shape
    width = total // planes
    rows = width - 1
    ids_ref[...] = jnp.zeros(ids_ref.shape, F32)
    for d in range(planes):
        ids_ref[d:d + 1, :] = got_ref[d * width + rows:(d + 1) * width, :] + 1.0
    shape = (total, line)
    index = lax.broadcasted_iota(jnp.int32, shape, 0)
    source = jnp.zeros(shape, jnp.int32)
    for d in range(1, planes):
        source = source + jnp.where(index >= d * width, 1, 0)
    place, lane = index - source * width, lanes(shape)
    spread = jnp.where(source == lane, 1.0, 0.0).astype(BF16)
    ids = lax.dot_general(spread, ids_ref[...].astype(BF16), (((1,), (0,)), ((), ())), preferred_element_type=F32)
    values = got_ref[...].T
    high = values.astype(BF16)
    low = (values - high.astype(F32)).astype(BF16)
    parts = []
    for k in range(2):
        mine = jnp.sum(jnp.where(lane == place + k * rows, ids, 0.0), axis=1, keepdims=True)
        hits = jnp.where((mine == lane.astype(F32) + 1.0) & (place < rows), 1.0, 0.0).astype(BF16)
        dots = [lax.dot_general(part, hits, (((1,), (0,)), ((), ())), preferred_element_type=F32) for part in (high, low)]
        parts.append((dots[0] + dots[1])[k * KB:(k + 1) * KB])
    coef_ref[...] = parts[0] + parts[1]


def call(kernel, outs, ins, scratch=(), places=None, leave=0, limit=16, cost=None):
    spaces = places or [pltpu.VMEM] * len(ins)
    keep = lambda a, space: pltpu.with_memory_space_constraint(a, space) if space is pltpu.VMEM else a
    return pl.pallas_call(
        kernel,
        out_shape=[jax.ShapeDtypeStruct(*o) if i < leave else pltpu.VMEM(*o) for i, o in enumerate(outs)],
        in_specs=[pl.BlockSpec(memory_space=pltpu.VMEM if space is None else space) for space in spaces],
        out_specs=[pl.BlockSpec(memory_space=pltpu.VMEM) for _ in outs],
        scratch_shapes=list(scratch),
        compiler_params=pltpu.CompilerParams(vmem_limit_bytes=limit * 1024 * 1024),
        cost_estimate=cost,
    )(*[keep(a, space) for a, space in zip(ins, spaces)])


def swapped(first, second, axis, starts=(0, 1)):
    axes = ("bx", "by", "gz")
    sizes = [lax.axis_size(name) for name in axes]
    along = axes.index(axis)
    arrived = []
    for start, value in zip(starts, (first, second)):
        pairs = []
        for flat in range(sizes[0] * sizes[1] * sizes[2]):
            at = [flat // (sizes[1] * sizes[2]), flat // sizes[2] % sizes[1], flat % sizes[2]]
            other = at[along] + 1 if at[along] % 2 == start else at[along] - 1
            if 0 <= other < sizes[along]:
                at[along] = other
            else:
                at[2] = (at[2] + 1) % sizes[2]
            pairs.append((flat, (at[0] * sizes[1] + at[1]) * sizes[2] + at[2]))
        arrived.append(lax.ppermute(value, axes, pairs))
    return arrived


def local(electric_start, magnetic_start, current_start, cotangent, level_set, material, source_cell, basis,
          block_owner, block_group):
    ny, nx, nz = material.shape
    wy, wx = ny + 4, nx + 8
    field, scalar = ((3, ny, nx, nz), F32), ((ny, nx, nz), F32)
    blocks = basis.shape[0]
    planes = lax.axis_size("bx") * lax.axis_size("by")
    rows = rows_of(planes, blocks)
    width = rows + 1
    y_face, x_face, corner = ((UNITS, nx, nz), F32), ((UNITS, ny, nz), F32), ((CORNER_LINES, nz), F32)
    names = ((1, blocks), jnp.int32)
    fa, fb, xa, xb, own, w, j1, q, weight, owner, group = call(
        prepare_kernel,
        [y_face, y_face, x_face, x_face, ((ARRAYS, ny, nx, nz), F32), scalar, field, scalar, field, names, names],
        [source_cell, electric_start, magnetic_start, current_start, cotangent, level_set, material,
         block_owner.reshape(1, blocks), block_group.reshape(1, blocks)],
        places=[pltpu.SMEM] + [None] * 8,
        limit=58,
    )
    gb, ga = swapped(fb, fa, "by", (1, 0))
    xb, xa = swapped(xb, xa, "bx", (1, 0))
    cb, ca = call(corner_kernel, [corner, corner], [gb, ga], cost=pl.CostEstimate(flops=5_000_000_000, transcendentals=0, bytes_accessed=1000))
    cb, ca, owner, group = lax.optimization_barrier((cb, ca, owner, group))
    cb, ca = swapped(cb, ca, "bx", (1, 0))
    flat_basis = basis.reshape(blocks * KB, basis.shape[2])
    chunk = 2 * nx * nz // basis.shape[2] * (2 * KB)
    body, acc, place, ids = call(
        functools.partial(widen_kernel, rows, width),
        [((ARRAYS, wy, nx, nz), F32), ((wy, nx, nz), F32), ((2, planes * width, blocks), BF16), ((planes, 128), F32)],
        [own, gb, ga, owner, group],
    )
    cb, ca, ids, acc = lax.optimization_barrier((cb, ca, ids, acc))
    full = -(-wy * wx // 128) * 128
    side, zp = call(
        extend_kernel,
        [((ARRAYS, wy, wx - nx, nz), F32), ((Z_UNITS, full), F32)],
        [acc, xb, xa, cb, ca],
        scratch=[pltpu.VMEM((full, nz), F32)],
    )
    zg = lax.ppermute(zp, "gz", [(0, 1), (1, 0)])
    wide, inner = ((3, wy, wx, nz), F32), ((3, wy, nx, nz), F32)
    electric, adjoint, send = call(
        main_kernel,
        [field, field, ((planes * width, 2 * KB), F32)],
        [body, side, zp, zg, j1, weight, w, q, place, ids, flat_basis],
        scratch=[
            pltpu.VMEM((ARRAYS, 8, full), F32),
            pltpu.VMEM((128, full), F32),
            pltpu.VMEM((full, 8 * nz), F32),
            *[pltpu.VMEM(*wide)] * 6,
            pltpu.VMEM(*inner), pltpu.VMEM(*inner),
            pltpu.VMEM((ny * nx, nz), F32),
            pltpu.VMEM((ny * nx // 2, 2 * KB), F32),
        ],
        limit=20,
    )
    send = send.reshape(planes * width, 1, 2 * KB)
    got = lax.all_to_all(send, ("bx", "by"), split_axis=0, concat_axis=0, tiled=True)
    (coef,) = call(
        functools.partial(collect_kernel, planes),
        [((KB, GRP_DEV), F32)],
        [got.reshape(planes * width, 2 * KB)],
        scratch=[pltpu.VMEM((128, 2 * KB), F32)],
        leave=1,
    )
    return electric, adjoint, coef


def solution(mesh):
    field = P(None, "by", "bx", "gz")
    scalar = P("by", "bx", "gz")
    flat = ("bx", "by", "gz")
    return jax.shard_map(
        local,
        mesh=mesh,
        in_specs=(field, field, field, field, scalar, scalar, P(flat), P(flat, None, None), P(flat, None), P(flat)),
        out_specs=(field, field, P(None, flat)),
        check_vma=False,
    )
```

```python
import functools

import jax
import jax.numpy as jnp
from jax import lax
from jax.experimental import pallas as pl
from jax.experimental.pallas import tpu as pltpu
from jax.sharding import PartitionSpec as P

KB = 64
GRP_DEV = 128

time_step = 0.5
drude_keep = 0.9
drude_gain = 1.0
metal_permit = 3.0
design_contrast = 5.0
source_level = 3.0
source_wave = (1.0, -0.6, 0.8, -0.4)

PAIRS, ARRAYS = 9, 13
UNITS = ARRAYS + 4
CORNER = [(0, u) for u in (1, 7)] + [(1, u) for u in (0, 1, 2, 3, 4, 5, 6, 7, 8, 10, 12, 15)]
CORNER += [(2, u) for u in (0, 1, 2, 4, 5, 6, 7, 8, 9, 12, 13, 14)] + [(3, 6)]
CORNER_LINES = -(-len(CORNER) // 8) * 8
Z_UNITS = 24
F32 = jnp.float32
BF16 = jnp.bfloat16


def is_even(axis):
    return lax.rem(lax.axis_index(axis), 2) == 0


def lanes(shape):
    return lax.broadcasted_iota(jnp.int32, shape, len(shape) - 1)


def prepare_kernel(cells_ref, e_ref, h_ref, j_ref, c_ref, level_ref, mat_ref, owner_ref, group_ref,
                   fa_ref, fb_ref, xa_ref, xb_ref, own_ref, w_ref, j1_ref, q_ref, c_out_ref, owner_out_ref, group_out_ref):
    owner_out_ref[...] = owner_ref[...]
    group_out_ref[...] = group_ref[...]
    ny, nx, nz = mat_ref.shape
    flat = lax.broadcasted_iota(jnp.int32, (nx, nz), 0) * nz + lanes((nx, nz))

    def row(y, carry):
        mat = mat_ref[y]
        silver, design = mat == 2, mat == 1
        smooth = 1.0 / (1.0 + jnp.exp(-level_ref[y]))
        permit = jnp.where(silver, metal_permit, jnp.where(design, 1.0 + design_contrast * smooth, 1.0))
        ratio = time_step / permit
        own_ref[12, y] = jnp.where(silver, -ratio, ratio)
        w_ref[y] = jnp.where(design, (-design_contrast / time_step) * ratio * smooth * (1.0 - smooth), 0.0)
        count = jnp.zeros((nx, nz), F32)
        for i in range(cells_ref.shape[0]):
            count = count + jnp.where(flat + y * (nx * nz) == cells_ref[i], 1.0, 0.0)
        q_ref[y] = count
        for c in range(3):
            electric, weight = e_ref[c, y], c_ref[c, y]
            current = jnp.where(silver, drude_keep * j_ref[c, y] + drude_gain * electric, 0.0)
            j1_ref[c, y] = current
            start = electric - ratio * current
            if c == 2:
                start = start + (source_level * source_wave[0]) * count
            own_ref[c, y] = electric
            own_ref[3 + c, y] = h_ref[c, y]
            own_ref[6 + c, y] = ratio * weight
            own_ref[9 + c, y] = start
            c_out_ref[c, y] = weight
        return carry

    lax.fori_loop(0, ny, row, 0, unroll=16)

    def y_face(out, near, deep, up):
        layers = [[own_ref[i, y] for i in range(ARRAYS)] for y in (near, deep)]
        for u, unit in enumerate(face_units(*layers, 1, up)):
            out[u] = unit

    lines = own_ref.reshape(ARRAYS * ny * nx, nz)

    def x_face(out, near, deep, up):
        layers = [[lines[pl.ds(i * ny * nx + x, ny, stride=nx), :] for i in range(ARRAYS)] for x in (near, deep)]
        for u, unit in enumerate(face_units(*layers, 0, up)):
            out[u] = unit

    for face, even, a_ref, b_ref, n in ((y_face, is_even("by"), fa_ref, fb_ref, ny), (x_face, is_even("bx"), xa_ref, xb_ref, nx)):
        @pl.when(even)
        def _():
            face(a_ref, n - 1, n - 2, True)
            face(b_ref, 0, 1, False)

        @pl.when(jnp.logical_not(even))
        def _():
            face(b_ref, n - 1, n - 2, True)
            face(a_ref, 0, 1, False)


def face_units(near, deep, axis, up):
    first, second = (axis + 1) % 3, (axis + 2) % 3
    units = list(near)
    if up:
        ratio = jnp.abs(near[12])
        units[9 + first] = near[9 + first] + ratio * (deep[3 + second] + time_step * deep[first])
        units[9 + second] = near[9 + second] - ratio * (deep[3 + first] - time_step * deep[second])
    else:
        units[3 + first] = near[3 + first] + time_step * deep[second]
        units[3 + second] = near[3 + second] - time_step * deep[first]
    return units + [deep[axis], deep[6], deep[7], deep[8]]


def sides(axis, even, a, b):
    at, zero = lax.axis_index(axis), jnp.zeros(a.shape, F32)
    lower = jnp.where(at == 0, zero, jnp.where(even, b, a))
    upper = jnp.where(at == lax.axis_size(axis) - 1, zero, jnp.where(even, a, b))
    return lower, upper


def rows_along_y(ga_ref, gb_ref):
    even, zero = is_even("by"), jnp.zeros(ga_ref.shape[1:], F32)
    units = [sides("by", even, ga_ref[u], gb_ref[u]) for u in range(UNITS)]
    lower, upper = ([unit[k] for unit in units] for k in range(2))
    below = [zero, lower[13], zero] + [zero] * 3 + lower[14:] + [zero] * 4
    above = [zero] * 6 + upper[14:] + [zero] * 4
    return below, lower[:ARRAYS], upper[:ARRAYS], above


def corner_kernel(gb_ref, ga_ref, cb_ref, ca_ref):
    nx = ga_ref.shape[1]
    rows = rows_along_y(ga_ref, gb_ref)
    even = is_even("bx")
    for ref in (ca_ref, cb_ref):
        ref[len(CORNER):, :] = jnp.zeros((CORNER_LINES - len(CORNER), ref.shape[1]), F32)

    def face(out, near, deep, up):
        units = [face_units([a[near:near + 1] for a in row], [a[deep:deep + 1] for a in row], 0, up) for row in rows]
        for line, (k, u) in enumerate(CORNER):
            out[line:line + 1, :] = units[k][u]

    @pl.when(even)
    def _():
        face(ca_ref, nx - 1, nx - 2, True)
        face(cb_ref, 0, 1, False)

    @pl.when(jnp.logical_not(even))
    def _():
        face(cb_ref, nx - 1, nx - 2, True)
        face(ca_ref, 0, 1, False)


def gather_planes(ref, y, back):
    shape = ref.shape[2:]
    lane, acc = lanes(shape), jnp.zeros(shape, F32)
    for i in range(ARRAYS):
        if i < PAIRS:
            acc = jnp.where(lane // 2 == i, pltpu.roll(ref[i, y], 2 * i + 2 * back, 1), acc)
        else:
            acc = jnp.where(lane == 9 + i, pltpu.roll(ref[i, y], 9 + i + back, 1), acc)
    return acc


def widen_kernel(rows, width, own_ref, gb_ref, ga_ref, owner_ref, group_ref, body_ref, acc_ref, place_ref, ids_ref):
    make_places(rows, width, owner_ref, group_ref, place_ref, ids_ref)
    ny = own_ref.shape[1]
    body_ref[:, 2:ny + 2] = own_ref[...]
    for y, row in zip((0, 1, ny + 2, ny + 3), rows_along_y(ga_ref, gb_ref)):
        for i in range(ARRAYS):
            body_ref[i, y] = row[i]
    back = jnp.where(lax.axis_index("gz") == 0, 1, 0)

    for y in range(ny + 4):
        acc_ref[y] = gather_planes(body_ref, y, back)


def extend_kernel(acc_ref, xb_ref, xa_ref, cb_ref, ca_ref, side_ref, zp_ref, all_ref):
    wy, nx, nz = acc_ref.shape
    ny, ws = wy - 4, side_ref.shape[2]
    wx = nx + ws
    x_even = is_even("bx")
    side_ref[...] = jnp.zeros(side_ref.shape, F32)
    lines = side_ref.reshape(ARRAYS * wy * ws, nz)
    low_corner, up_corner = sides("bx", x_even, ca_ref[...], cb_ref[...])
    for u in range(UNITS):
        i, near = (u, True) if u < ARRAYS else ((0, 6, 7, 8)[u - ARRAYS], False)
        lower, upper = sides("bx", x_even, xa_ref[u], xb_ref[u])
        for x, rows, corner in ((ws - 1 if near else ws - 2, lower, low_corner), (0 if near else 1, upper, up_corner)):
            if u == ARRAYS and rows is upper:
                continue
            start = i * wy * ws + x
            lines[pl.ds(start + 2 * ws, ny, stride=ws), :] = rows
            for line, (k, unit) in enumerate(CORNER):
                if unit == u:
                    at = start + (0, 1, ny + 2, ny + 3)[k] * ws
                    lines[at:at + 1, :] = corner[line:line + 1]
    back = jnp.where(lax.axis_index("gz") == 0, 1, 0)

    for y in range(wy):
        all_ref[y * wx:y * wx + nx, :] = acc_ref[y]
        all_ref[y * wx + nx:(y + 1) * wx, :] = gather_planes(side_ref, y, back)
    full = all_ref.shape[0]
    all_ref[wy * wx:, :] = jnp.zeros((full - wy * wx, nz), F32)
    zp_ref[...] = all_ref[...].T[:Z_UNITS]


def curl_of(dx, dy, dz):
    return dy[2] - dz[1], dz[0] - dx[2], dx[1] - dy[0]


def slab_planes(slab_ref, wx, by0, bx0):
    full = slab_ref.shape[2]
    lane = lanes((8, full))
    line = (lane * 683) >> 14
    column = lane - line * wx
    half = jnp.where((by0 & (line < 2)) | (bx0 & (column >= wx - 2)), 0.0, time_step)

    def plus(f):
        ahead = lambda a: jnp.where(column == wx - 1, pltpu.roll(a, wx - 1, 1), pltpu.roll(a, full - 1, 1)) - a
        return curl_of(
            (None, ahead(f[1]), ahead(f[2])),
            (pltpu.roll(f[0], full - wx, 1) - f[0], None, pltpu.roll(f[2], full - wx, 1) - f[2]),
            (pltpu.roll(f[0], 7, 0) - f[0], pltpu.roll(f[1], 7, 0) - f[1]),
        )

    def minus(f):
        behind = lambda a: a - jnp.where(column == 0, pltpu.roll(a, full - wx + 1, 1), pltpu.roll(a, 1, 1))
        return curl_of(
            (None, behind(f[1]), behind(f[2])),
            (f[0] - pltpu.roll(f[0], wx, 1), None, f[2] - pltpu.roll(f[2], wx, 1)),
            (f[0] - pltpu.roll(f[0], 1, 0), f[1] - pltpu.roll(f[1], 1, 0)),
        )

    e, h, s, b = ([slab_ref[3 * k + c] for c in range(3)] for k in range(4))
    code = slab_ref[12]
    ratio = jnp.abs(code)
    h1 = [a - half * d for a, d in zip(h, plus(e))]
    g1 = [half * d for d in plus(s)]
    e1 = [a + ratio * d for a, d in zip(b, minus(h1))]
    s1 = [jnp.where(code < 0, a * (1.0 - ratio), a) - ratio * d for a, d in zip(s, minus(g1))]
    h2 = [a - half * d for a, d in zip(h1, plus(e1))]
    g2 = [a + half * d for a, d in zip(g1, plus(s1))]
    return (e, e1, s, s1), (h1, h2, g1, g2)


class Borders:
    def __init__(self, col_ref, wx, nz):
        self.col_ref, self.wx, self.nz, self.lane = col_ref, wx, nz, lanes((wx, nz))

    def beyond(self, y, k):
        return self.col_ref[pl.ds(pl.multiple_of(y * self.wx, 8), self.wx), k * self.nz:(k + 1) * self.nz]

    def plus(self, get, y, p):
        f, g = [get(c, y) for c in range(3)], [get(c, y + 1) for c in (0, 2)]
        dz = [pltpu.roll(jnp.where(self.lane == 0, self.beyond(y, 2 * p + c), f[c]), self.nz - 1, 1) - f[c] for c in range(2)]
        dx = [None] + [pltpu.roll(f[c], self.wx - 1, 0) - f[c] for c in (1, 2)]
        return curl_of(dx, (g[0] - f[0], None, g[1] - f[2]), dz)

    def minus(self, get, y, p):
        f, g = [get(c, y) for c in range(3)], [get(c, y - 1) for c in (0, 2)]
        dz = [f[c] - pltpu.roll(jnp.where(self.lane == self.nz - 1, self.beyond(y, 2 * p + c), f[c]), 1, 1) for c in range(2)]
        dx = [None] + [f[c] - pltpu.roll(f[c], 1, 0) for c in (1, 2)]
        return curl_of(dx, (f[0] - g[0], None, f[2] - g[1]), dz)


def halves(wx, nz):
    by0, bx0 = lax.axis_index("by") == 0, lax.axis_index("bx") == 0
    column = lax.broadcasted_iota(jnp.int32, (wx, nz), 0)
    along = jnp.where(bx0 & (column >= wx - 2), 0.0, time_step)
    return lambda y: along * jnp.where(by0 & (y < 2), 0.0, 1.0)


def main_kernel(body_ref, side_ref, zo_ref, zg_ref, j1_ref, c_ref, w_ref, q_ref, place_ref, ids_ref, blocks_ref,
                e2_ref, a0_ref, send_ref,
                slab_ref, plane_ref, col_ref, h1_ref, e1_ref, h2_ref, g1_ref, s1_ref, g2_ref,
                d1_ref, back_ref, cell_ref, partial_ref):
    size = 2 * w_ref.shape[1] * w_ref.shape[2] // blocks_ref.shape[1] * (2 * KB)
    ny, nx, nz = w_ref.shape
    tile_rows = size // nx
    wy, wx = ny + 4, nx + side_ref.shape[2]
    by0, bx0 = lax.axis_index("by") == 0, lax.axis_index("bx") == 0
    gz0 = lax.axis_index("gz") == 0

    for i in range(ARRAYS):
        u, deep = (2 * i, 2) if i < PAIRS else (9 + i, 1)
        mine, other = zo_ref[u:u + deep, :], zg_ref[u:u + deep, :]
        slab_ref[i] = jnp.zeros(slab_ref.shape[1:], F32)
        slab_ref[i, 2 - deep:2, :] = jnp.where(gz0, mine, other)
        slab_ref[i, 2:2 + deep, :] = jnp.where(gz0, other, mine)
    upper, lower = slab_planes(slab_ref, wx, by0, bx0)
    plane_ref[...] = jnp.zeros(plane_ref.shape, F32)
    for p in range(4):
        for c in range(2):
            plane_ref[2 * p + c:2 * p + c + 1, :] = jnp.where(gz0, upper[p][c][2:3], lower[p][c][1:2])
    rest = plane_ref[0:8, :]
    for k in range(3):
        part = rest.astype(BF16).astype(F32)
        plane_ref[8 * k:8 * k + 8, :] = part
        rest = rest - part
    wide = 8 * nz
    row, place = lax.broadcasted_iota(jnp.int32, (128, wide), 0), lanes((128, wide))
    border = place % nz == jnp.where(gz0, 0, nz - 1)
    chosen = jnp.where(border & (row % 8 == place // nz) & (row < 24), 1.0, 0.0).astype(BF16)
    col_ref[...] = lax.dot_general(plane_ref[...].T.astype(BF16), chosen, (((1,), (0,)), ((), ())), preferred_element_type=F32)

    borders, half = Borders(col_ref, wx, nz), halves(wx, nz)

    def array(k):
        return lambda c, y: jnp.concatenate([body_ref[3 * k + c, y], side_ref[3 * k + c, y]], axis=0)

    def row_of(ref):
        return lambda c, y: ref[c, y]

    electric, magnetic, scaled, start = (array(k) for k in range(4))

    def first_magnetic(y):
        factor = half(y)
        for c, d in enumerate(borders.plus(electric, y, 0)):
            h1_ref[c, y] = magnetic(c, y) - factor * d
        for c, d in enumerate(borders.plus(scaled, y, 2)):
            g1_ref[c, y] = factor * d

    def first_electric(y):
        code = array(4)(0, y)
        ratio = jnp.abs(code)
        kept = jnp.where(code < 0, 1.0 - ratio, 1.0)
        for c, d in enumerate(borders.minus(row_of(h1_ref), y, 0)):
            d1_ref[c, y] = d[:nx]
            e1_ref[c, y] = start(c, y) + ratio * d
        for c, d in enumerate(borders.minus(row_of(g1_ref), y, 2)):
            back_ref[c, y] = d[:nx]
            s1_ref[c, y] = scaled(c, y) * kept - ratio * d

    def second_magnetic(y):
        factor = half(y)
        for c, d in enumerate(borders.plus(row_of(e1_ref), y, 1)):
            h2_ref[c, y] = h1_ref[c, y] - factor * d

    def second_electric(y):
        at = y - 2
        code = body_ref[12, y]
        ratio, silver = jnp.abs(code), code < 0
        eps = jnp.zeros((nx, nz), F32)
        for c, d in enumerate(borders.minus(row_of(h2_ref), y, 1)):
            e1, j1 = e1_ref[c, y, 0:nx, :], j1_ref[c, at]
            drive = d[:nx] - jnp.where(silver, drude_keep * j1 + drude_gain * e1, 0.0)
            final = e1 + ratio * drive
            if c == 2:
                final = final + (source_level * source_wave[1]) * q_ref[at]
            e2_ref[c, at] = final
            eps = eps + body_ref[6 + c, y] * drive + s1_ref[c, y, 0:nx, :] * (d1_ref[c, y] - j1)
        cell_ref[pl.ds(pl.multiple_of(at * nx, 8), nx), :] = w_ref[at] * eps

    def last_magnetic(y):
        factor = half(y)
        for c, d in enumerate(borders.plus(row_of(s1_ref), y, 3)):
            g2_ref[c, y] = g1_ref[c, y] + factor * d

    def last_electric(y):
        silver = body_ref[12, y] < 0
        for c, d in enumerate(borders.minus(row_of(g2_ref), y, 3)):
            lost = jnp.where(silver, drude_gain * ((1.0 + drude_keep) * body_ref[6 + c, y] + s1_ref[c, y, 0:nx, :]), 0.0)
            a0_ref[c, y - 2] = c_ref[c, y - 2] - back_ref[c, y] - d[:nx] - lost

    for y in range(wy - 1):
        first_magnetic(y)
    for y in range(1, wy - 1):
        first_electric(y)
    for y in range(1, wy - 2):
        second_magnetic(y)

    group = nx
    sub = lax.broadcasted_iota(jnp.int32, (group, tile_rows), 0)

    def project(n):
        parts = [cell_ref[pl.ds(n * 2 * group + k, group, stride=2), :] for k in range(2)]
        cells = jnp.concatenate(parts, axis=1).astype(BF16)
        prods = lax.dot_general(cells, blocks_ref[n * size:(n + 1) * size, :], (((1,), (1,)), ((), ())), preferred_element_type=F32)
        acc = jnp.zeros((group, tile_rows), F32)
        for i in range(group):
            acc = jnp.where(sub == i, prods[:, i * tile_rows:(i + 1) * tile_rows], acc)
        partial_ref[n * group:(n + 1) * group, :] = acc

    second_electric(2)
    second_electric(3)
    last_magnetic(1)
    for n in range(1, ny // 2):
        for y in (2 * n + 2, 2 * n + 3):
            second_electric(y)
        project(n - 1)
    for y in range(2, ny + 2):
        last_magnetic(y)
    for y in range(2, ny + 2):
        last_electric(y)
    project(ny // 2 - 1)

    partial = partial_ref[...]
    turned = pltpu.roll(partial, KB, 1)
    low_lanes = lanes(partial.shape) < KB
    low = [jnp.where(low_lanes, a, 0.0) for a in (partial, turned)]
    high = [jnp.where(low_lanes, 0.0, a) for a in (turned, partial)]
    rhs = jnp.concatenate(low + high, axis=0)
    most = rhs.astype(BF16)
    rhs = jnp.concatenate([most, (rhs - most.astype(F32)).astype(BF16)], axis=0)
    lhs = jnp.concatenate([place_ref[0], place_ref[1], place_ref[0], place_ref[1]], axis=1)
    send_ref[...] = lax.dot_general(lhs, rhs, (((1,), (0,)), ((), ())), preferred_element_type=F32)
    planes = ids_ref.shape[0]
    width = send_ref.shape[0] // planes
    for d in range(planes):
        send_ref[d * width + width - 1:(d + 1) * width, :] = ids_ref[d:d + 1, :]


def capacity_of(planes, blocks):
    return max(2, 2 * blocks // planes)


def rows_of(planes, blocks):
    return capacity_of(planes, blocks) // 2


def make_places(rows, width, owner_ref, group_ref, place_ref, ids_ref):
    blocks = owner_ref.shape[1]
    planes = ids_ref.shape[0]
    row, column = (lax.broadcasted_iota(jnp.int32, (blocks, blocks), k) for k in range(2))
    half = blocks // 2
    swap = jnp.where(row == jnp.where(column < half, 2 * column, 2 * (column - half) + 1), 1.0, 0.0).astype(BF16)

    def arranged(ref):
        wide = jnp.broadcast_to(ref[...].astype(F32), (8, blocks)).astype(BF16)
        return lax.dot_general(wide, swap, (((1,), (0,)), ((), ())), preferred_element_type=F32)[:1]

    owner, group = arranged(owner_ref), arranged(group_ref)
    plane = lax.broadcasted_iota(jnp.int32, (planes, blocks), 0).astype(F32)
    hits = jnp.where(plane == owner, 1.0, 0.0)
    earlier = jnp.where(row < column, 1.0, 0.0).astype(BF16)
    before = lax.dot_general(hits.astype(BF16), earlier, (((1,), (0,)), ((), ())), preferred_element_type=F32)
    rank = jnp.sum(before * hits, axis=0, keepdims=True)
    slots = place_ref.shape[1]
    slot = lax.broadcasted_iota(jnp.int32, (slots, blocks), 0).astype(F32)
    for k in range(2):
        inner = rank - float(k * rows)
        target = jnp.where((inner >= 0.0) & (inner < float(rows)), owner * float(width) + inner, -1.0)
        place_ref[k] = jnp.where(slot == target, 1.0, 0.0).astype(BF16)
    ranks = lax.broadcasted_iota(jnp.int32, (128, blocks), 0).astype(F32)
    ranked = jnp.where(ranks == rank, 1.0, 0.0).astype(BF16)
    named = (hits * (group + 1.0)).astype(BF16)
    ids_ref[...] = lax.dot_general(named, ranked, (((1,), (1,)), ((), ())), preferred_element_type=F32) - 1.0


def collect_kernel(planes, got_ref, coef_ref, ids_ref):
    total, line = got_ref.shape
    width = total // planes
    rows = width - 1
    ids_ref[...] = jnp.zeros(ids_ref.shape, F32)
    for d in range(planes):
        ids_ref[d:d + 1, :] = got_ref[d * width + rows:(d + 1) * width, :] + 1.0
    shape = (total, line)
    index = lax.broadcasted_iota(jnp.int32, shape, 0)
    source = jnp.zeros(shape, jnp.int32)
    for d in range(1, planes):
        source = source + jnp.where(index >= d * width, 1, 0)
    place, lane = index - source * width, lanes(shape)
    spread = jnp.where(source == lane, 1.0, 0.0).astype(BF16)
    ids = lax.dot_general(spread, ids_ref[...].astype(BF16), (((1,), (0,)), ((), ())), preferred_element_type=F32)
    values = got_ref[...].T
    high = values.astype(BF16)
    low = (values - high.astype(F32)).astype(BF16)
    parts = []
    for k in range(2):
        mine = jnp.sum(jnp.where(lane == place + k * rows, ids, 0.0), axis=1, keepdims=True)
        hits = jnp.where((mine == lane.astype(F32) + 1.0) & (place < rows), 1.0, 0.0).astype(BF16)
        dots = [lax.dot_general(part, hits, (((1,), (0,)), ((), ())), preferred_element_type=F32) for part in (high, low)]
        parts.append((dots[0] + dots[1])[k * KB:(k + 1) * KB])
    coef_ref[...] = parts[0] + parts[1]


def call(kernel, outs, ins, scratch=(), places=None, leave=0, limit=16, cost=None):
    spaces = places or [pltpu.VMEM] * len(ins)
    keep = lambda a, space: pltpu.with_memory_space_constraint(a, space) if space is pltpu.VMEM else a
    return pl.pallas_call(
        kernel,
        out_shape=[jax.ShapeDtypeStruct(*o) if i < leave else pltpu.VMEM(*o) for i, o in enumerate(outs)],
        in_specs=[pl.BlockSpec(memory_space=pltpu.VMEM if space is None else space) for space in spaces],
        out_specs=[pl.BlockSpec(memory_space=pltpu.VMEM) for _ in outs],
        scratch_shapes=list(scratch),
        compiler_params=pltpu.CompilerParams(vmem_limit_bytes=limit * 1024 * 1024),
        cost_estimate=cost,
    )(*[keep(a, space) for a, space in zip(ins, spaces)])


def swapped(first, second, axis, starts=(0, 1)):
    axes = ("bx", "by", "gz")
    sizes = [lax.axis_size(name) for name in axes]
    along = axes.index(axis)
    arrived = []
    for start, value in zip(starts, (first, second)):
        pairs = []
        for flat in range(sizes[0] * sizes[1] * sizes[2]):
            at = [flat // (sizes[1] * sizes[2]), flat // sizes[2] % sizes[1], flat % sizes[2]]
            other = at[along] + 1 if at[along] % 2 == start else at[along] - 1
            if 0 <= other < sizes[along]:
                at[along] = other
            else:
                at[2] = (at[2] + 1) % sizes[2]
            pairs.append((flat, (at[0] * sizes[1] + at[1]) * sizes[2] + at[2]))
        arrived.append(lax.ppermute(value, axes, pairs))
    return arrived


def local(electric_start, magnetic_start, current_start, cotangent, level_set, material, source_cell, basis,
          block_owner, block_group):
    ny, nx, nz = material.shape
    wy, wx = ny + 4, nx + 8
    field, scalar = ((3, ny, nx, nz), F32), ((ny, nx, nz), F32)
    blocks = basis.shape[0]
    planes = lax.axis_size("bx") * lax.axis_size("by")
    rows = rows_of(planes, blocks)
    width = rows + 1
    y_face, x_face, corner = ((UNITS, nx, nz), F32), ((UNITS, ny, nz), F32), ((CORNER_LINES, nz), F32)
    names = ((1, blocks), jnp.int32)
    fa, fb, xa, xb, own, w, j1, q, weight, owner, group = call(
        prepare_kernel,
        [y_face, y_face, x_face, x_face, ((ARRAYS, ny, nx, nz), F32), scalar, field, scalar, field, names, names],
        [source_cell, electric_start, magnetic_start, current_start, cotangent, level_set, material,
         block_owner.reshape(1, blocks), block_group.reshape(1, blocks)],
        places=[pltpu.SMEM] + [None] * 8,
        limit=58,
    )
    gb, ga = swapped(fb, fa, "by", (1, 0))
    xb, xa = swapped(xb, xa, "bx", (1, 0))
    cb, ca = call(corner_kernel, [corner, corner], [gb, ga], cost=pl.CostEstimate(flops=5_000_000_000, transcendentals=0, bytes_accessed=1000))
    cb, ca, owner, group = lax.optimization_barrier((cb, ca, owner, group))
    cb, ca = swapped(cb, ca, "bx", (1, 0))
    flat_basis = basis.reshape(blocks * KB, basis.shape[2])
    chunk = 2 * nx * nz // basis.shape[2] * (2 * KB)
    body, acc, place, ids = call(
        functools.partial(widen_kernel, rows, width),
        [((ARRAYS, wy, nx, nz), F32), ((wy, nx, nz), F32), ((2, planes * width, blocks), BF16), ((planes, 128), F32)],
        [own, gb, ga, owner, group],
    )
    cb, ca, ids, acc = lax.optimization_barrier((cb, ca, ids, acc))
    full = -(-wy * wx // 128) * 128
    side, zp = call(
        extend_kernel,
        [((ARRAYS, wy, wx - nx, nz), F32), ((Z_UNITS, full), F32)],
        [acc, xb, xa, cb, ca],
        scratch=[pltpu.VMEM((full, nz), F32)],
    )
    zg = lax.ppermute(zp, "gz", [(0, 1), (1, 0)])
    wide, inner = ((3, wy, wx, nz), F32), ((3, wy, nx, nz), F32)
    electric, adjoint, send = call(
        main_kernel,
        [field, field, ((planes * width, 2 * KB), F32)],
        [body, side, zp, zg, j1, weight, w, q, place, ids, flat_basis],
        scratch=[
            pltpu.VMEM((ARRAYS, 8, full), F32),
            pltpu.VMEM((128, full), F32),
            pltpu.VMEM((full, 8 * nz), F32),
            *[pltpu.VMEM(*wide)] * 6,
            pltpu.VMEM(*inner), pltpu.VMEM(*inner),
            pltpu.VMEM((ny * nx, nz), F32),
            pltpu.VMEM((ny * nx // 2, 2 * KB), F32),
        ],
        limit=20,
    )
    send = send.reshape(planes * width, 1, 2 * KB)
    got = lax.all_to_all(send, ("bx", "by"), split_axis=0, concat_axis=0, tiled=True)
    (coef,) = call(
        functools.partial(collect_kernel, planes),
        [((KB, GRP_DEV), F32)],
        [got.reshape(planes * width, 2 * KB)],
        scratch=[pltpu.VMEM((128, 2 * KB), F32)],
        leave=1,
    )
    return electric, adjoint, coef


def solution(mesh):
    field = P(None, "by", "bx", "gz")
    scalar = P("by", "bx", "gz")
    flat = ("bx", "by", "gz")
    return jax.shard_map(
        local,
        mesh=mesh,
        in_specs=(field, field, field, field, scalar, scalar, P(flat), P(flat, None, None), P(flat, None), P(flat)),
        out_specs=(field, field, P(None, flat)),
        check_vma=False,
    )
```
